128 devices in a mesh: slot: 4 (over x_hi, core), ctx: 32 (over z, x_lo, y).
Axes of the slice: x: 4 (x_hi: 2, x_lo: 2; x = x_hi * 2 + x_lo), y: 4, z: 4, core: 2. Of those that a mesh axis runs over, the one named last changes fastest.
Arguments:
- latents: bfloat16 [4, 2048, 3072], P('slot', 'ctx'), may hold values from -6 to 6
- fresh: bfloat16 [2048, 3072], P('ctx'), may hold values from -6 to 6
- span_ids: int32 [4], replicated, may hold values from 0 to 3, each once
- noise_step: int32 [4], replicated, may hold values from 0 to 1
- ada_table: float32 [9, 3, 3072], replicated, may hold values from -3 to 3
- w_qkv: bfloat16 [3072, 5120], P(None, 'slot'), may hold values from -1 to 1
- w_out: bfloat16 [3072, 3072], P(None, 'slot'), may hold values from -0.109375 to 0.109375
Outputs:
- velocity: bfloat16 [2, 4, 2048, 3072], P(None, 'slot', 'ctx')
- finished: bfloat16 [2048, 3072], P('ctx', 'slot')
The draws below stay inside these ranges and needn't reach their ends.
Inputs may be any that keep to these rules, and one draw needn't show every extreme that they name: `span_ids`: each slot holds another span number.
All inputs are finite; a program needn't handle non-finite values.
Results may differ from the reference program's by a relative error of at most 0.02.
Values may be sent and summed in bfloat16 or wider, within the bound.
No kernel may reach another device: no remote copies, remote signals or barrier semaphores. Data moves between devices by JAX's collectives and lax.ppermute only.
A program may use at most 128 MiB of HBM per device.

```python
import jax
import jax.numpy as jnp
from jax import lax

D = 3072
HEADS = 24
KV_GROUPS = 8
HD = 128
PER = 2
SLOTS = 4
TOKENS = 2048
LEVELS = 9


def draw_latents(key, part):
    key = jax.random.fold_in(key, 3)
    values = jax.random.normal(key, (SLOTS, TOKENS, D), jnp.float32)
    return jnp.clip(values, -6.0, 6.0).astype(jnp.bfloat16)


def draw_w_qkv(key, part):
    key = jax.random.fold_in(key, 5)
    columns = (HEADS + 2 * KV_GROUPS) * HD
    values = jnp.clip(jax.random.normal(key, (D, columns), jnp.float32), -6.0, 6.0) * D ** (-0.5)
    return values.astype(jnp.bfloat16)


def place_ends(entries, rng, smallest, largest):
    longest = entries.shape.index(max(entries.shape))
    spots = []
    for shift in (0, 1):
        where = [jax.random.randint(jax.random.fold_in(rng, axis), (), 0, length) for axis, length in enumerate(entries.shape)]
        where[longest] = (where[longest] + shift) % entries.shape[longest]
        spots.append(tuple(where))
    return entries.at[spots[0]].set(smallest).at[spots[1]].set(largest)


def steps_of(rng, extent, pieces, low, high):
    def one(dim, parts):
        draws = jax.random.uniform(jax.random.fold_in(jax.random.fold_in(rng, 6), dim), (parts,), jnp.float32, low / len(pieces), high / len(pieces))
        return jnp.repeat(jnp.exp(draws), extent[dim] // parts).reshape((-1,) + (1,) * (len(extent) - dim - 1))

    gain = one(*pieces[0])
    for cut in pieces[1:]:
        gain = gain * one(*cut)
    return gain


def noise(stream_key, shape, width, limit, cuts=(), held_as=jnp.bfloat16):
    drawn = jax.random.normal(stream_key, shape, jnp.float32) * width
    if len(cuts) > 0:
        drawn = steps_of(stream_key, shape, cuts, -0.22, 0.18) * drawn
    return jnp.clip(drawn, min=-limit, max=limit).astype(held_as)


def setup_inputs(seed: int = 0) -> dict:
    keys = jax.random.split(jax.random.key(seed), 8)
    latents = draw_latents(jax.random.fold_in(keys[7], 71), 0)
    fresh = noise(keys[1], (TOKENS, D), 1.0, 6.0, ((0, 32),))
    span_ids = jax.random.permutation(keys[2], SLOTS).astype(jnp.int32)
    noise_step = place_ends(jax.random.randint(keys[3], (SLOTS,), 0, PER), jax.random.fold_in(keys[3], 1), 0, PER - 1).astype(jnp.int32)
    ada_table = noise(keys[4], (LEVELS, 3, D), 0.5, 3.0, (), jnp.float32)
    w_qkv = draw_w_qkv(jax.random.fold_in(keys[7], 71), 0)
    w_out = noise(keys[6], (HEADS * HD, D), (HEADS * HD) ** -0.5, 0.109375, ((1, 4),))
    return dict(latents=latents, fresh=fresh, span_ids=span_ids, noise_step=noise_step, ada_table=ada_table, w_qkv=w_qkv, w_out=w_out)


EPS = 1e-06
NEG = -1e+30

def level_from(ids, noise_step):
    rank = lax.optimization_barrier(jnp.sum((ids[None, :] < ids[:, None]).astype(jnp.int32), axis=1))
    return (rank * PER + noise_step + 1).astype(jnp.int32)

def block_step(latent, ids, levels, ada_table, w_qkv, w_out):
    modulation = ada_table[levels]
    values = latent.astype(jnp.float32)
    center = lax.optimization_barrier(jnp.mean(values, axis=-1, keepdims=True))
    spread = lax.optimization_barrier(jnp.mean((values - center) ** 2, axis=-1, keepdims=True))
    normed = (values - center) * lax.rsqrt(spread + EPS)
    hidden = (normed * (1.0 + modulation[:, 1][:, None, :]) + modulation[:, 0][:, None, :]).astype(jnp.bfloat16)
    qkv = jnp.dot(hidden.reshape(SLOTS * TOKENS, D), w_qkv, preferred_element_type=jnp.float32)
    qkv = qkv.astype(jnp.bfloat16)
    query_all = qkv[:, :HEADS * HD].reshape(SLOTS, TOKENS, HEADS, HD)
    key_groups = qkv[:, HEADS * HD:(HEADS + KV_GROUPS) * HD].reshape(SLOTS * TOKENS, KV_GROUPS, HD).transpose(1, 0, 2)
    value_groups = qkv[:, (HEADS + KV_GROUPS) * HD:].reshape(SLOTS * TOKENS, KV_GROUPS, HD).transpose(1, 0, 2)
    share = HEADS // KV_GROUPS
    key_all = jnp.repeat(key_groups, share, axis=0)
    value_all = jnp.repeat(value_groups, share, axis=0)
    key_ids = jnp.repeat(ids, TOKENS)
    scale = 1.0 / HD ** 0.5

    def per_slot(args):
        query_slot, own_id = args
        allowed = key_ids <= own_id

        def per_head(hargs):
            query_head, key_head, value_head = hargs
            scores = jnp.dot(query_head, key_head.T, preferred_element_type=jnp.float32) * scale
            scores = jnp.where(allowed[None, :], scores, NEG)
            top = lax.optimization_barrier(jnp.max(scores, axis=-1, keepdims=True))
            weights = jnp.where(allowed[None, :], jnp.exp(scores - top), 0.0)
            total = lax.optimization_barrier(jnp.sum(weights, axis=-1, keepdims=True))
            out_head = jnp.dot(weights.astype(jnp.bfloat16), value_head, preferred_element_type=jnp.float32)
            return (out_head / total).astype(jnp.bfloat16)
        return lax.map(per_head, (query_slot.transpose(1, 0, 2), key_all, value_all))
    attn = lax.map(per_slot, (query_all, ids))
    attn = attn.transpose(0, 2, 1, 3).reshape(SLOTS * TOKENS, HEADS * HD)
    proj = jnp.dot(attn, w_out, preferred_element_type=jnp.float32).reshape(SLOTS, TOKENS, D)
    return (proj * modulation[:, 2][:, None, :]).astype(jnp.bfloat16)

def reference(latents, fresh, span_ids, noise_step, ada_table, w_qkv, w_out):
    level_one = level_from(span_ids, noise_step)
    vel_one = block_step(latents, span_ids, level_one, ada_table, w_qkv, w_out)
    step_size = 1.0 / (SLOTS * PER)
    moved = (latents.astype(jnp.float32) - vel_one.astype(jnp.float32) * step_size).astype(jnp.bfloat16)
    first = span_ids == jnp.min(span_ids)
    finished = lax.optimization_barrier(jnp.sum(jnp.where(first[:, None, None], moved.astype(jnp.float32), 0.0), axis=0)).astype(jnp.bfloat16)
    moved = jnp.where(first[:, None, None], fresh[None, :, :], moved)
    ids_two = jnp.where(first, SLOTS, span_ids).astype(jnp.int32)
    level_two = jnp.where(first, SLOTS * PER, level_one - 1).astype(jnp.int32)
    vel_two = block_step(moved, ids_two, level_two, ada_table, w_qkv, w_out)
    return (jnp.stack([vel_one, vel_two]), finished)
```

```python
import math

import jax
import jax.numpy as jnp
from jax import lax
from jax.experimental import pallas as pl
from jax.experimental.pallas import tpu as pltpu
from jax.sharding import PartitionSpec as P

HD = 128
EPS = 1e-06
BF = jnp.bfloat16
F32 = jnp.float32
AXES = ("slot", "ctx")
VM = pl.BlockSpec(memory_space=pltpu.VMEM)
SM = pl.BlockSpec(memory_space=pltpu.SMEM)
SLOTS = 4
PER = 2
TOK = 64
HALF = 32
ROWS = SLOTS * HALF
WIDTH = 3072
COLS = WIDTH // SLOTS
LOG2E = 1.4426950408889634


def where_is(flat):
    s, c = flat // 32, flat % 32
    return dict(h=s // 2, i=s % 2, z=c // 8, xl=(c // 4) % 2, y=c % 4)


def flat_of(d):
    return (d["h"] * 2 + d["i"]) * 32 + d["z"] * 8 + d["xl"] * 4 + d["y"]


def move(x, h=0, i=0, z=0, y=0):
    pairs = []
    for f in range(128):
        d = where_is(f)
        d["h"] = (d["h"] + h) % 2
        d["i"] = (d["i"] + i) % 2
        d["z"] = (d["z"] + z) % 4
        d["y"] = (d["y"] + y) % 4
        pairs.append((f, flat_of(d)))
    return lax.ppermute(x, AXES, pairs)


def group_lists():
    out = []
    for i in range(2):
        for z in range(4):
            for yh in range(2):
                out.append(
                    [
                        flat_of(dict(h=h, i=i, z=z, xl=xl, y=2 * yh + yl))
                        for h in range(2)
                        for xl in range(2)
                        for yl in range(2)
                    ]
                )
    return out


def exchange(x):
    return lax.all_to_all(x, AXES, 0, 0, tiled=True, axis_index_groups=group_lists())


def params(mib, **kw):
    return pltpu.CompilerParams(vmem_limit_bytes=mib * 1024 * 1024, **kw)


def first_slot(ids):
    best, at = ids[0], jnp.int32(0)
    for j in range(1, SLOTS):
        less = ids[j] < best
        best = jnp.where(less, ids[j], best)
        at = jnp.where(less, j, at)
    return at


def level_of(ids, noise, t, step):
    mine = ids[t]
    rank = jnp.int32(0)
    for j in range(SLOTS):
        rank = rank + (ids[j] < mine).astype(jnp.int32)
    level = PER * rank + noise[t] + 1
    if step == 0:
        return level
    return jnp.where(rank == 0, SLOTS * PER, level - 1)


def row_of(half, slot):
    return pl.ds(pl.multiple_of((half * SLOTS + slot) * HALF, HALF), HALF)


def col_of(slot, width=COLS):
    return pl.ds(pl.multiple_of(slot * width, 128), width)


def modulated(values, ada, level):
    center = jnp.mean(values, axis=-1, keepdims=True)
    off = values - center
    spread = jnp.mean(off * off, axis=-1, keepdims=True)
    normed = off * lax.rsqrt(spread + EPS)
    return (normed * (1.0 + ada[level, 1:2, :]) + ada[level, 0:1, :]).astype(BF)


def project(hidden, w, mine, theirs):
    out = jnp.dot(hidden[...], w[...], preferred_element_type=F32).astype(BF)
    for k in range(2):
        mine[k] = out[:ROWS, k * HD : (k + 1) * HD]
        theirs[k] = out[ROWS:, k * HD : (k + 1) * HD]


def first_body(pos, ids, noise, x0, x1, x2, x3, ada, w, mine, theirs, hidden):
    s = pos[0]
    i = s % 2

    @pl.when(pl.program_id(0) == 0)
    def _():
        for r, x in enumerate((x0, x1, x2, x3)):
            t = s ^ r
            level = level_of(ids, noise, t, 0)
            for a in range(2):
                values = x[a * HALF : (a + 1) * HALF, :].astype(F32)
                hidden[row_of(i ^ a, t), :] = modulated(values, ada, level)

    project(hidden, w, mine, theirs)


def second_body(
    pos, ids, noise, x0, x1, x2, x3, v0, v1, v2, v3, fresh, ada, w,
    mine, theirs, vel, fin, hidden, vall, moved,
):
    s = pos[0]
    i = s % 2

    @pl.when(pl.program_id(0) == 0)
    def _():
        for k, v in enumerate((v0, v1, v2, v3)):
            if k % 2 == 0:
                vall[:, col_of(s ^ k)] = v[...]
            else:
                vall[:ROWS, col_of(s ^ k)] = v[ROWS:, :]
                vall[ROWS:, col_of(s ^ k)] = v[:ROWS, :]
        first = first_slot(ids)
        for a in range(2):
            vel[a * HALF : (a + 1) * HALF, :] = vall[row_of(i ^ a, s), :]
        for r, x in enumerate((x0, x1, x2, x3)):
            t = s ^ r
            level = level_of(ids, noise, t, 1)
            for a in range(2):
                rows = slice(a * HALF, (a + 1) * HALF)
                where = row_of(i ^ a, t)
                moved[...] = (
                    x[rows, :].astype(F32) - vall[where, :].astype(F32) * (1.0 / (SLOTS * PER))
                ).astype(BF)

                @pl.when(t == first)
                def _():
                    fin[rows, :] = moved[:, col_of(s)]
                    moved[...] = fresh[rows, :]

                hidden[where, :] = modulated(moved[...].astype(F32), ada, level)

    project(hidden, w, mine, theirs)


def whole(shape):
    return pl.BlockSpec(shape, lambda n: (0,) * len(shape))


def projected_shapes(heads):
    return [jax.ShapeDtypeStruct((heads, ROWS, HD), BF)] * 2


def first_projection(pos, ids, noise, xs, ada, w):
    heads = w.shape[1] // HD
    return pl.pallas_call(
        first_body,
        grid=(heads // 2,),
        in_specs=[SM, SM, SM]
        + [whole((TOK, WIDTH))] * 4
        + [whole(ada.shape), pl.BlockSpec((WIDTH, 2 * HD), lambda n: (0, n))],
        out_specs=[pl.BlockSpec((2, ROWS, HD), lambda n: (n, 0, 0))] * 2,
        out_shape=projected_shapes(heads),
        scratch_shapes=[pltpu.VMEM((2 * ROWS, WIDTH), BF)],
        compiler_params=params(32),
        name="modulate_project",
    )(pos, ids, noise, *xs, ada, w)


def second_projection(pos, ids, noise, xs, vs, fresh, ada, w):
    heads = w.shape[1] // HD
    return pl.pallas_call(
        second_body,
        grid=(heads // 2,),
        in_specs=[SM, SM, SM]
        + [whole((TOK, WIDTH))] * 4
        + [whole((2 * ROWS, COLS))] * 4
        + [whole((TOK, WIDTH)), whole(ada.shape), pl.BlockSpec((WIDTH, 2 * HD), lambda n: (0, n))],
        out_specs=[pl.BlockSpec((2, ROWS, HD), lambda n: (n, 0, 0))] * 2
        + [whole((TOK, WIDTH)), whole((TOK, COLS))],
        out_shape=projected_shapes(heads)
        + [jax.ShapeDtypeStruct((TOK, WIDTH), BF), jax.ShapeDtypeStruct((TOK, COLS), BF)],
        scratch_shapes=[
            pltpu.VMEM((2 * ROWS, WIDTH), BF),
            pltpu.VMEM((2 * ROWS, WIDTH), BF),
            pltpu.VMEM((HALF, WIDTH), BF),
        ],
        compiler_params=params(40),
        name="advance_modulate_project",
    )(pos, ids, noise, *xs, *vs, fresh, ada, w)


def pack_body(pos, mine, other, kv, q, chip):
    i, h = pos[0] % 2, pos[0] // 2
    chip[pl.ds(10 * i, 10)] = mine[...]
    chip[pl.ds(10 * (1 - i), 10)] = other[...]
    for g in range(8):
        kv[g, 0] = chip[4 + g]
        kv[g, 1] = chip[12 + g]

    @pl.when(h == 0)
    def _():
        q[0:20] = chip[...]
        q[20:24] = jnp.zeros((4, ROWS, HD), BF)

    @pl.when(h != 0)
    def _():
        q[0:20] = jnp.zeros((20, ROWS, HD), BF)
        q[20:24] = chip[0:4]


def pack(pos, mine, other):
    return pl.pallas_call(
        pack_body,
        in_specs=[SM, VM, VM],
        out_specs=[VM, VM],
        out_shape=[
            jax.ShapeDtypeStruct((8, 2, ROWS, HD), BF),
            jax.ShapeDtypeStruct((24, ROWS, HD), BF),
        ],
        scratch_shapes=[pltpu.VMEM((20, ROWS, HD), BF)],
        compiler_params=params(16),
        name="pack_heads",
    )(pos, mine, other)


NB = 64
KEYS = NB * HALF
QROWS = 4 * 3 * HALF


def attend_body(step, parts, ids, q, *refs):
    blocks = refs[:parts]
    out, qs, ks, vs, top, acc = refs[parts:]
    at = 0
    for ref in blocks:
        for b in range(ref.shape[0]):
            for j in range(SLOTS):
                rows = slice(j * HALF, (j + 1) * HALF)
                ks[j, at * HALF : (at + 1) * HALF, :] = ref[b, 0, rows, :]
                vs[j, at * HALF : (at + 1) * HALF, :HD] = ref[b, 1, rows, :]
            at += 1
    vs[:, :, HD:] = jnp.ones((SLOTS, KEYS, HD), BF)
    for c in range(4):
        for m in range(3):
            both = q[c, m] + q[4 + c, m]
            for j in range(SLOTS):
                qs[j, (c * 3 + m) * HALF : (c * 3 + m + 1) * HALF, :] = both[j * HALF : (j + 1) * HALF]
    factor = LOG2E / math.sqrt(HD)

    def id_of(t):
        if step == 0:
            return ids[t]
        return jnp.where(first_slot(ids) == t, SLOTS, ids[t])

    def per_span(t, _):
        top[...] = jnp.full_like(top, -1e30)
        acc[...] = jnp.zeros_like(acc)
        own = id_of(t)

        def per_key(j, _):
            @pl.when(id_of(j) <= own)
            def _():
                for n in range(0, KEYS, 1024):
                    scores = lax.dot_general(
                        qs[t], ks[j, n : n + 1024, :], (((1,), (1,)), ((), ())), preferred_element_type=F32
                    )
                    old = top[...]
                    new = jnp.maximum(old, jnp.max(scores, axis=-1, keepdims=True))
                    weights = jnp.exp2((scores - new) * factor).astype(BF)
                    acc[...] = acc[...] * jnp.exp2((old - new) * factor) + jnp.dot(
                        weights, vs[j, n : n + 1024, :], preferred_element_type=F32
                    )
                    top[...] = new

            return 0

        lax.fori_loop(0, SLOTS, per_key, 0)
        res = (acc[:, :HD] / acc[:, HD : HD + 1]).astype(BF)
        rows = pl.ds(pl.multiple_of(t * HALF, HALF), HALF)
        for c in range(4):
            for m in range(3):
                piece = res[(c * 3 + m) * HALF : (c * 3 + m + 1) * HALF]
                out[c, m, rows, :] = piece
                out[4 + c, m, rows, :] = piece
        return 0

    lax.fori_loop(0, SLOTS, per_span, 0)


def attend(step, ids, q, blocks):
    def body(*refs):
        attend_body(step, len(blocks), *refs)

    return pl.pallas_call(
        body,
        in_specs=[SM] + [VM] * (1 + len(blocks)),
        out_specs=VM,
        out_shape=jax.ShapeDtypeStruct((8, 3, ROWS, HD), BF),
        scratch_shapes=[
            pltpu.VMEM((SLOTS, QROWS, HD), BF),
            pltpu.VMEM((SLOTS, KEYS, HD), BF),
            pltpu.VMEM((SLOTS, KEYS, 2 * HD), BF),
            pltpu.VMEM((QROWS, 1), F32),
            pltpu.VMEM((QROWS, 2 * HD), F32),
        ],
        compiler_params=params(48),
        name="span_attention",
    )(ids, q, *blocks)


def out_body(step, pos, ids, noise, mine, other, ada, w, out, attn):
    n = pl.program_id(0)
    s = pos[0]
    i = s % 2
    width = w.shape[1]

    @pl.when(n == 0)
    def _():
        for m in range(24):
            attn[:ROWS, m * HD : (m + 1) * HD] = mine[m]
            attn[ROWS:, m * HD : (m + 1) * HD] = other[m]

    product = jnp.dot(attn[...], w[...], preferred_element_type=F32)
    cols = pl.ds(pl.multiple_of(s * COLS + n * width, 128), width)
    for t in range(SLOTS):
        gate = ada[level_of(ids, noise, t, step), 2:3, cols]
        for a in range(2):
            at = (a * SLOTS + t) * HALF
            piece = (product[at : at + HALF] * gate).astype(BF)
            if step == 0:
                out[at : at + HALF, :] = piece
            else:
                rows = pl.ds(pl.multiple_of((i ^ a) * HALF, HALF), HALF)
                out[s ^ t, rows, :] = piece


def out_projection(step, pos, ids, noise, mine, other, ada, w):
    width = 256
    if step == 0:
        out_spec = pl.BlockSpec((2 * ROWS, width), lambda n: (0, n))
        out_shape = jax.ShapeDtypeStruct((2 * ROWS, COLS), BF)
    else:
        out_spec = pl.BlockSpec((SLOTS, TOK, width), lambda n: (0, 0, n))
        out_shape = jax.ShapeDtypeStruct((SLOTS, TOK, COLS), BF)

    def body(*refs):
        out_body(step, *refs)

    return pl.pallas_call(
        body,
        grid=(COLS // width,),
        in_specs=[SM, SM, SM]
        + [whole((24, ROWS, HD))] * 2
        + [whole(ada.shape), pl.BlockSpec((WIDTH, width), lambda n: (0, n))],
        out_specs=out_spec,
        out_shape=out_shape,
        scratch_shapes=[pltpu.VMEM((2 * ROWS, WIDTH), BF)],
        compiler_params=params(32),
        name="out_projection",
    )(pos, ids, noise, mine, other, ada, w)


def finish_body(pos, vel, r0, r1, r2, r3, out):
    s = pos[0]
    out[0] = vel[...]
    for k, r in enumerate((r0, r1, r2, r3)):
        out[1, :, col_of(s ^ k)] = r[...]


def finish(pos, vel, rs):
    return pl.pallas_call(
        finish_body,
        in_specs=[SM] + [VM] * 5,
        out_specs=VM,
        out_shape=jax.ShapeDtypeStruct((2, TOK, WIDTH), BF),
        compiler_params=params(16),
        name="collect_velocity",
    )(pos, vel, *rs)


def gather_slots(x):
    far = move(x, h=1)
    near = move(x, i=1)
    return x, near, far, move(far, i=1)


def gather_keys(x):
    low, high = x[:2], x[2:]
    low_y = move(low, y=2)
    high_z = [move(high, z=k) for k in (1, -1, 2)]
    early = jnp.concatenate([x, low_y, *high_z])
    lows = jnp.concatenate([low, low_y])
    highs = jnp.concatenate([high, *high_z])
    late = [move(lows, z=k) for k in (1, -1, 2)] + [move(highs, y=2)]
    late = jnp.concatenate(late)
    return [early, move(early, i=1), late, move(late, i=1)]


def shards(latents, fresh, span_ids, noise_step, ada_table, w_qkv, w_out):
    pos = lax.axis_index("slot").astype(jnp.int32).reshape(1)
    scalars = (pos, span_ids, noise_step)
    xs = gather_slots(latents[0])

    def one_step(step, mine, theirs):
        kv, q = pack(pos, mine, move(theirs, i=1))
        keys = gather_keys(exchange(kv)[4:])
        q = exchange(q.reshape(8, 3, ROWS, HD))
        attn = exchange(attend(step, span_ids, q, keys)).reshape(24, ROWS, HD)
        return out_projection(step, *scalars, attn, move(attn, i=1), ada_table, w_out)

    vel = one_step(0, *first_projection(*scalars, xs, ada_table, w_qkv))
    mine, theirs, vel, fin = second_projection(
        *scalars, xs, gather_slots(vel), fresh, ada_table, w_qkv
    )
    out = one_step(1, mine, theirs)
    rs = [out[0], move(out[1], i=1), move(out[2], h=1), move(out[3], h=1, i=1)]
    return finish(pos, vel, rs)[:, None], fin


def solution(mesh):
    in_specs = (
        P("slot", "ctx", None),
        P("ctx", None),
        P(),
        P(),
        P(),
        P(None, "slot"),
        P(None, "slot"),
    )
    out_specs = (P(None, "slot", "ctx", None), P("ctx", "slot"))
    return jax.shard_map(shards, mesh=mesh, in_specs=in_specs, out_specs=out_specs, check_vma=False)
```

```python
import math

import jax
import jax.numpy as jnp
from jax import lax
from jax.experimental import pallas as pl
from jax.experimental.pallas import tpu as pltpu
from jax.sharding import PartitionSpec as P

HD = 128
EPS = 1e-06
BF = jnp.bfloat16
F32 = jnp.float32
AXES = ("slot", "ctx")
VM = pl.BlockSpec(memory_space=pltpu.VMEM)
SM = pl.BlockSpec(memory_space=pltpu.SMEM)
SLOTS = 4
PER = 2
TOK = 64
HALF = 32
ROWS = SLOTS * HALF
WIDTH = 3072
COLS = WIDTH // SLOTS
LOG2E = 1.4426950408889634


def where_is(flat):
    s, c = flat // 32, flat % 32
    return dict(h=s // 2, i=s % 2, z=c // 8, xl=(c // 4) % 2, y=c % 4)


def flat_of(d):
    return (d["h"] * 2 + d["i"]) * 32 + d["z"] * 8 + d["xl"] * 4 + d["y"]


def move(x, h=0, i=0, z=0, y=0):
    pairs = []
    for f in range(128):
        d = where_is(f)
        d["h"] = (d["h"] + h) % 2
        d["i"] = (d["i"] + i) % 2
        d["z"] = (d["z"] + z) % 4
        d["y"] = (d["y"] + y) % 4
        pairs.append((f, flat_of(d)))
    return lax.ppermute(x, AXES, pairs)


def group_lists():
    out = []
    for i in range(2):
        for z in range(4):
            for yh in range(2):
                out.append(
                    [
                        flat_of(dict(h=h, i=i, z=z, xl=xl, y=2 * yh + yl))
                        for h in range(2)
                        for xl in range(2)
                        for yl in range(2)
                    ]
                )
    return out


def exchange(x):
    return lax.all_to_all(x, AXES, 0, 0, tiled=True, axis_index_groups=group_lists())


def params(mib, **kw):
    return pltpu.CompilerParams(vmem_limit_bytes=mib * 1024 * 1024, **kw)


def first_slot(sc):
    best, at = sc[0], jnp.int32(0)
    for j in range(1, SLOTS):
        less = sc[j] < best
        best = jnp.where(less, sc[j], best)
        at = jnp.where(less, j, at)
    return at


def id_of(sc, t, step):
    if step == 0:
        return sc[t]
    return jnp.where(first_slot(sc) == t, SLOTS, sc[t])


def level_of(sc, t, step):
    mine = sc[t]
    rank = jnp.int32(0)
    for j in range(SLOTS):
        rank = rank + (sc[j] < mine).astype(jnp.int32)
    level = PER * rank + sc[SLOTS + t] + 1
    if step == 0:
        return level
    return jnp.where(rank == 0, SLOTS * PER, level - 1)


def row_of(half, slot):
    return pl.ds(pl.multiple_of((half * SLOTS + slot) * HALF, HALF), HALF)


def col_of(slot, width=COLS):
    return pl.ds(pl.multiple_of(slot * width, 128), width)


def modulated(values, ada, level):
    center = jnp.mean(values, axis=-1, keepdims=True)
    off = values - center
    spread = jnp.mean(off * off, axis=-1, keepdims=True)
    normed = off * lax.rsqrt(spread + EPS)
    return (normed * (1.0 + ada[level, 1:2, :]) + ada[level, 0:1, :]).astype(BF)


def project(hidden, w, mine, theirs):
    out = jnp.dot(hidden[...], w[...], preferred_element_type=F32).astype(BF)
    cut = out.shape[0] // 2
    for k in range(2):
        mine[k] = out[:cut, k * HD : (k + 1) * HD]
        theirs[k] = out[cut:, k * HD : (k + 1) * HD]


def first_body(sc, x0, x1, ada, w, mine, theirs, hidden, *, far):
    s = sc[8]
    i = s % 2

    @pl.when(pl.program_id(0) == 0)
    def _():
        for r, x in enumerate((x0, x1)):
            t = s ^ (r + far)
            level = level_of(sc, t, 0)
            for a in range(2):
                values = x[a * HALF : (a + 1) * HALF, :].astype(F32)
                at = pl.multiple_of(((i ^ a) * 2 + t % 2) * HALF, HALF)
                hidden[pl.ds(at, HALF), :] = modulated(values, ada, level)

    project(hidden, w, mine, theirs)


def second_body(
    sc, x0, x1, x2, x3, v0, v1, v2, v3, fresh, ada, w,
    mine, theirs, vel, fin, hidden, vall, moved,
):
    s = sc[8]
    i = s % 2

    @pl.when(pl.program_id(0) == 0)
    def _():
        for k, v in enumerate((v0, v1, v2, v3)):
            if k % 2 == 0:
                vall[:, col_of(s ^ k)] = v[...]
            else:
                vall[:ROWS, col_of(s ^ k)] = v[ROWS:, :]
                vall[ROWS:, col_of(s ^ k)] = v[:ROWS, :]
        first = first_slot(sc)
        for a in range(2):
            vel[a * HALF : (a + 1) * HALF, :] = vall[row_of(i ^ a, s), :]
        for r, x in enumerate((x0, x1, x2, x3)):
            t = s ^ r
            level = level_of(sc, t, 1)
            for a in range(2):
                rows = slice(a * HALF, (a + 1) * HALF)
                where = row_of(i ^ a, t)
                moved[...] = (
                    x[rows, :].astype(F32) - vall[where, :].astype(F32) * (1.0 / (SLOTS * PER))
                ).astype(BF)

                @pl.when(t == first)
                def _():
                    fin[rows, :] = moved[:, col_of(s)]
                    moved[...] = fresh[rows, :]

                hidden[where, :] = modulated(moved[...].astype(F32), ada, level)

    project(hidden, w, mine, theirs)


def whole(shape):
    return pl.BlockSpec(shape, lambda n: (0,) * len(shape))


def projected_shapes(heads, rows):
    return [jax.ShapeDtypeStruct((heads, rows, HD), BF)] * 2


def first_projection(sc, xs, far, ada, w):
    heads = w.shape[1] // HD

    def body(*refs):
        first_body(*refs, far=far)

    return pl.pallas_call(
        body,
        grid=(heads // 2,),
        in_specs=[SM]
        + [whole((TOK, WIDTH))] * 2
        + [whole(ada.shape), pl.BlockSpec((WIDTH, 2 * HD), lambda n: (0, n))],
        out_specs=[pl.BlockSpec((2, ROWS // 2, HD), lambda n: (n, 0, 0))] * 2,
        out_shape=projected_shapes(heads, ROWS // 2),
        scratch_shapes=[pltpu.VMEM((ROWS, WIDTH), BF)],
        compiler_params=params(24),
        cost_estimate=pl.CostEstimate(flops=4 * 10**9, bytes_accessed=10**7, transcendentals=0),
        name="modulate_project",
    )(sc, *xs, ada, w)


def second_projection(sc, xs, vs, fresh, ada, w):
    heads = w.shape[1] // HD
    return pl.pallas_call(
        second_body,
        grid=(heads // 2,),
        in_specs=[SM]
        + [whole((TOK, WIDTH))] * 4
        + [whole((2 * ROWS, COLS))] * 4
        + [whole((TOK, WIDTH)), whole(ada.shape), pl.BlockSpec((WIDTH, 2 * HD), lambda n: (0, n))],
        out_specs=[pl.BlockSpec((2, ROWS, HD), lambda n: (n, 0, 0))] * 2
        + [whole((TOK, WIDTH)), whole((TOK, COLS))],
        out_shape=projected_shapes(heads, ROWS)
        + [jax.ShapeDtypeStruct((TOK, WIDTH), BF), jax.ShapeDtypeStruct((TOK, COLS), BF)],
        scratch_shapes=[
            pltpu.VMEM((2 * ROWS, WIDTH), BF),
            pltpu.VMEM((2 * ROWS, WIDTH), BF),
            pltpu.VMEM((HALF, WIDTH), BF),
        ],
        compiler_params=params(40),
        name="advance_modulate_project",
    )(sc, *xs, *vs, fresh, ada, w)


def pack_body(sc, *refs):
    parts, (out, chip) = refs[:-2], refs[-2:]
    i, h = sc[8] % 2, sc[8] // 2
    for k in range(2):
        to = pl.ds(10 * jnp.where(k == 0, i, 1 - i), 10)
        if len(parts) == 2:
            chip[to] = parts[k][...]
        else:
            cut = ROWS // 2
            chip[to, pl.ds(pl.multiple_of(h * cut, cut), cut)] = parts[2 * k][...]
            chip[to, pl.ds(pl.multiple_of((1 - h) * cut, cut), cut)] = parts[2 * k + 1][...]
    for g in range(8):
        out[g, 3] = chip[4 + g]
        out[g, 4] = chip[12 + g]

    def queries(low, high, at):
        for n in range(24):
            if low <= n < high:
                out[n // 3, n % 3] = chip[n - at]
            else:
                out[n // 3, n % 3] = jnp.zeros((ROWS, HD), BF)

    @pl.when(h == 0)
    def _():
        queries(0, 20, 0)

    @pl.when(h != 0)
    def _():
        queries(20, 24, 20)


def pack(sc, *parts):
    return pl.pallas_call(
        pack_body,
        in_specs=[SM] + [VM] * len(parts),
        out_specs=VM,
        out_shape=jax.ShapeDtypeStruct((8, 5, ROWS, HD), BF),
        scratch_shapes=[pltpu.VMEM((20, ROWS, HD), BF)],
        compiler_params=params(16),
        name="pack_heads",
    )(sc, *parts)


QROWS = 4 * 3 * HALF
BLOCK = 128


def attend_body(step, parts, chunk, last, sc, q, *refs):
    blocks, refs = refs[:parts], refs[parts:]
    if last:
        top_in, acc_in, out, qs, ks, vs, tops, accs = refs
    else:
        tops, accs, qs, ks, vs = refs
    keys = ks.shape[1]
    at = 0
    for ref in blocks:
        for b in range(ref.shape[0]):
            for j in range(SLOTS):
                rows = slice(j * HALF, (j + 1) * HALF)
                ks[j, at * HALF : (at + 1) * HALF, :] = ref[b, 0, rows, :]
                vs[j, at * HALF : (at + 1) * HALF, :HD] = ref[b, 1, rows, :]
            at += 1
    vs[:, :, HD:] = jnp.ones((SLOTS, keys, HD), BF)
    factor = LOG2E / math.sqrt(HD)
    for c in range(4):
        for m in range(3):
            both = ((q[c, m].astype(F32) + q[4 + c, m].astype(F32)) * factor).astype(BF)
            for j in range(SLOTS):
                qs[j, (c * 3 + m) * HALF : (c * 3 + m + 1) * HALF, :] = both[j * HALF : (j + 1) * HALF]

    def per_span(t, _):
        if last:
            top, acc = tops, accs
            top[...] = top_in[t]
            acc[...] = acc_in[t]
        else:
            top, acc = tops.at[t], accs.at[t]
            top[...] = jnp.full(top.shape, -1e30, F32)
            acc[...] = jnp.zeros(acc.shape, F32)
        own = id_of(sc, t, step)

        def per_key(j, _):
            @pl.when(id_of(sc, j, step) <= own)
            def _():
                def scores_of(r, n):
                    return lax.dot_general(
                        qs[t, r : r + BLOCK], ks[j, n : n + chunk, :], (((1,), (1,)), ((), ())),
                        preferred_element_type=F32,
                    )

                todo = [(r, n) for r in range(0, QROWS, BLOCK) for n in range(0, keys, chunk)]
                ahead = scores_of(*todo[0])
                for x, (r, n) in enumerate(todo):
                    scores = ahead
                    rows = slice(r, r + BLOCK)
                    if n == 0:
                        old, total = top[rows], acc[rows]
                    if x + 1 < len(todo):
                        ahead = scores_of(*todo[x + 1])
                    new = jnp.maximum(old, jnp.max(scores, axis=-1, keepdims=True))
                    weights = jnp.exp2(scores - new[:, :1]).astype(BF)
                    shrink = jnp.exp2(old - new)
                    total = total * jnp.concatenate([shrink, shrink], axis=1) + jnp.dot(
                        weights, vs[j, n : n + chunk, :], preferred_element_type=F32
                    )
                    old = new
                    if n + chunk == keys:
                        top[rows] = new
                        acc[rows] = total

            return 0

        lax.fori_loop(0, SLOTS, per_key, 0)
        if last:
            res = (acc[:, :HD] / acc[:, HD:]).astype(BF)
            rows = pl.ds(pl.multiple_of(t * HALF, HALF), HALF)
            for c in range(4):
                for m in range(3):
                    piece = res[(c * 3 + m) * HALF : (c * 3 + m + 1) * HALF]
                    out[c, m, rows, :] = piece
                    out[4 + c, m, rows, :] = piece
        return 0

    lax.fori_loop(0, SLOTS, per_span, 0)


def attend(step, sc, q, blocks, chunk, state=None):
    last = state is not None
    keys = sum(b.shape[0] for b in blocks) * HALF

    def body(*refs):
        attend_body(step, len(blocks), chunk, last, *refs)

    state_shapes = [(QROWS, HD), (QROWS, 2 * HD)]
    scratch = [
        pltpu.VMEM((SLOTS, QROWS, HD), BF),
        pltpu.VMEM((SLOTS, keys, HD), BF),
        pltpu.VMEM((SLOTS, keys, 2 * HD), BF),
    ]
    if last:
        out_shape = jax.ShapeDtypeStruct((8, 3, ROWS, HD), BF)
        scratch += [pltpu.VMEM(x, F32) for x in state_shapes]
    else:
        out_shape = [jax.ShapeDtypeStruct((SLOTS, *x), F32) for x in state_shapes]
    pairs = 10 * QROWS * keys
    return pl.pallas_call(
        body,
        in_specs=[SM] + [VM] * (1 + len(blocks) + (2 if last else 0)),
        out_specs=VM if last else [VM, VM],
        out_shape=out_shape,
        scratch_shapes=scratch,
        compiler_params=params(32),
        cost_estimate=pl.CostEstimate(
            flops=pairs * HD * 8, bytes_accessed=8 * 10**6, transcendentals=pairs
        ),
        name="span_attention_end" if last else "span_attention_begin",
    )(sc, q, *blocks, *(state or ()))


def out_body(step, sc, mine, other, ada, w, out, attn):
    n = pl.program_id(0)
    s = sc[8]
    i = s % 2
    width = w.shape[1]

    @pl.when(n == 0)
    def _():
        for m in range(24):
            attn[:ROWS, m * HD : (m + 1) * HD] = mine[m]
            attn[ROWS:, m * HD : (m + 1) * HD] = other[m]

    product = jnp.dot(attn[...], w[...], preferred_element_type=F32)
    cols = pl.ds(pl.multiple_of(s * COLS + n * width, 128), width)
    for t in range(SLOTS):
        gate = ada[level_of(sc, t, step), 2:3, cols]
        for a in range(2):
            at = (a * SLOTS + t) * HALF
            piece = (product[at : at + HALF] * gate).astype(BF)
            if step == 0:
                out[at : at + HALF, :] = piece
            else:
                rows = pl.ds(pl.multiple_of((i ^ a) * HALF, HALF), HALF)
                out[s ^ t, rows, :] = piece


def out_projection(step, sc, mine, other, ada, w):
    width = 256
    if step == 0:
        out_spec = pl.BlockSpec((2 * ROWS, width), lambda n: (0, n))
        out_shape = jax.ShapeDtypeStruct((2 * ROWS, COLS), BF)
    else:
        out_spec = pl.BlockSpec((SLOTS, TOK, width), lambda n: (0, 0, n))
        out_shape = jax.ShapeDtypeStruct((SLOTS, TOK, COLS), BF)

    def body(*refs):
        out_body(step, *refs)

    return pl.pallas_call(
        body,
        grid=(COLS // width,),
        in_specs=[SM]
        + [whole((24, ROWS, HD))] * 2
        + [whole(ada.shape), pl.BlockSpec((WIDTH, width), lambda n: (0, n))],
        out_specs=out_spec,
        out_shape=out_shape,
        scratch_shapes=[pltpu.VMEM((2 * ROWS, WIDTH), BF)],
        compiler_params=params(32),
        name="out_projection",
    )(sc, mine, other, ada, w)


def finish_body(sc, vel, r0, r1, r2, r3, out):
    s = sc[8]
    out[0] = vel[...]
    for k, r in enumerate((r0, r1, r2, r3)):
        out[1, :, col_of(s ^ k)] = r[...]


def finish(sc, vel, rs):
    return pl.pallas_call(
        finish_body,
        in_specs=[SM] + [VM] * 5,
        out_specs=VM,
        out_shape=jax.ShapeDtypeStruct((2, TOK, WIDTH), BF),
        compiler_params=params(16),
        name="collect_velocity",
    )(sc, vel, *rs)


def gather_slots(x):
    far = move(x, h=1)
    near = move(x, i=1)
    return x, near, far, move(far, i=1)


def gather_keys(low, high):
    low_y = move(low, y=2)
    high_z = [move(high, z=k) for k in (1, -1, 2)]
    early = jnp.concatenate([low, high, low_y, *high_z])
    lows = jnp.concatenate([low, low_y])
    highs = jnp.concatenate([high, *high_z])
    late = [move(lows, z=k) for k in (1, -1, 2)] + [move(highs, y=2)]
    late = jnp.concatenate(late)
    return [early, move(early, i=1)], [late, move(late, i=1)]


def shards(latents, fresh, span_ids, noise_step, ada_table, w_qkv, w_out):
    pos = lax.axis_index("slot").astype(jnp.int32).reshape(1)
    sc = jnp.concatenate([span_ids, noise_step, pos])
    own = latents[0]

    def one_step(step, *parts):
        got = exchange(pack(sc, *parts))
        early, late = gather_keys(got[4:6, 3:], got[6:, 3:])
        state = attend(step, sc, got, early, 768)
        attn = attend(step, sc, got, late, 1280, state)
        attn = exchange(attn).reshape(24, ROWS, HD)
        return out_projection(step, sc, attn, move(attn, i=1), ada_table, w_out)

    xs = gather_slots(own)
    mine_a, theirs_a = first_projection(sc, xs[:2], 0, ada_table, w_qkv)
    other_a = move(theirs_a, i=1)
    mine_b, theirs_b = first_projection(sc, xs[2:], 2, ada_table, w_qkv)
    vel = one_step(0, mine_a, mine_b, other_a, move(theirs_b, i=1))
    mine, theirs, vel, fin = second_projection(sc, xs, gather_slots(vel), fresh, ada_table, w_qkv)
    out = one_step(1, mine, move(theirs, i=1))
    rs = [out[0], move(out[1], i=1), move(out[2], h=1), move(out[3], h=1, i=1)]
    return finish(sc, vel, rs)[:, None], fin


def solution(mesh):
    in_specs = (
        P("slot", "ctx", None),
        P("ctx", None),
        P(),
        P(),
        P(),
        P(None, "slot"),
        P(None, "slot"),
    )
    out_specs = (P(None, "slot", "ctx", None), P("ctx", "slot"))
    return jax.shard_map(shards, mesh=mesh, in_specs=in_specs, out_specs=out_specs, check_vma=False)
```

```python
import math

import jax
import jax.numpy as jnp
from jax import lax
from jax.experimental import pallas as pl
from jax.experimental.pallas import tpu as pltpu
from jax.sharding import PartitionSpec as P

HD = 128
EPS = 1e-06
BF = jnp.bfloat16
F32 = jnp.float32
AXES = ("slot", "ctx")
VM = pl.BlockSpec(memory_space=pltpu.VMEM)
SM = pl.BlockSpec(memory_space=pltpu.SMEM)
SLOTS = 4
PER = 2
TOK = 64
HALF = 32
ROWS = SLOTS * HALF
WIDTH = 3072
COLS = WIDTH // SLOTS
LOG2E = 1.4426950408889634


def where_is(flat):
    s, c = flat // 32, flat % 32
    return dict(h=s // 2, i=s % 2, z=c // 8, xl=(c // 4) % 2, y=c % 4)


def flat_of(d):
    return (d["h"] * 2 + d["i"]) * 32 + d["z"] * 8 + d["xl"] * 4 + d["y"]


def move(x, h=0, i=0, z=0, y=0):
    pairs = []
    for f in range(128):
        d = where_is(f)
        d["h"] = (d["h"] + h) % 2
        d["i"] = (d["i"] + i) % 2
        d["z"] = (d["z"] + z) % 4
        d["y"] = (d["y"] + y) % 4
        pairs.append((f, flat_of(d)))
    return lax.ppermute(x, AXES, pairs)


def group_lists():
    out = []
    for i in range(2):
        for z in range(4):
            for yh in range(2):
                out.append(
                    [
                        flat_of(dict(h=h, i=i, z=z, xl=xl, y=2 * yh + yl))
                        for h in range(2)
                        for xl in range(2)
                        for yl in range(2)
                    ]
                )
    return out


def exchange(x):
    return lax.all_to_all(x, AXES, 0, 0, tiled=True, axis_index_groups=group_lists())


def params(mib, **kw):
    return pltpu.CompilerParams(vmem_limit_bytes=mib * 1024 * 1024, **kw)


def first_slot(sc):
    best, at = sc[0], jnp.int32(0)
    for j in range(1, SLOTS):
        less = sc[j] < best
        best = jnp.where(less, sc[j], best)
        at = jnp.where(less, j, at)
    return at


def id_of(sc, t, step):
    if step == 0:
        return sc[t]
    return jnp.where(first_slot(sc) == t, SLOTS, sc[t])


def level_of(sc, t, step):
    mine = sc[t]
    rank = jnp.int32(0)
    for j in range(SLOTS):
        rank = rank + (sc[j] < mine).astype(jnp.int32)
    level = PER * rank + sc[SLOTS + t] + 1
    if step == 0:
        return level
    return jnp.where(rank == 0, SLOTS * PER, level - 1)


def row_of(half, slot):
    return pl.ds(pl.multiple_of((half * SLOTS + slot) * HALF, HALF), HALF)


def col_of(slot, width=COLS):
    return pl.ds(pl.multiple_of(slot * width, 128), width)


def modulated(values, ada, level):
    center = jnp.mean(values, axis=-1, keepdims=True)
    off = values - center
    spread = jnp.mean(off * off, axis=-1, keepdims=True)
    normed = off * lax.rsqrt(spread + EPS)
    return (normed * (1.0 + ada[level, 1:2, :]) + ada[level, 0:1, :]).astype(BF)


def project(hidden, w, mine, theirs):
    out = jnp.dot(hidden[...], w[...], preferred_element_type=F32).astype(BF)
    cut = out.shape[0] // 2
    for k in range(2):
        mine[k] = out[:cut, k * HD : (k + 1) * HD]
        theirs[k] = out[cut:, k * HD : (k + 1) * HD]


def first_body(sc, x0, x1, ada, w, mine, theirs, hidden, *, far):
    s = sc[8]
    i = s % 2

    @pl.when(pl.program_id(0) == 0)
    def _():
        for r, x in enumerate((x0, x1)):
            t = s ^ (r + far)
            level = level_of(sc, t, 0)
            for a in range(2):
                values = x[a * HALF : (a + 1) * HALF, :].astype(F32)
                at = pl.multiple_of(((i ^ a) * 2 + t % 2) * HALF, HALF)
                hidden[pl.ds(at, HALF), :] = modulated(values, ada, level)

    project(hidden, w, mine, theirs)


def second_body(
    sc, x0, x1, x2, x3, v0, v1, v2, v3, fresh, ada, w,
    mine, theirs, vel, fin, hidden, vall, moved,
):
    s = sc[8]
    i = s % 2

    @pl.when(pl.program_id(0) == 0)
    def _():
        for k, v in enumerate((v0, v1, v2, v3)):
            if k % 2 == 0:
                vall[:, col_of(s ^ k)] = v[...]
            else:
                vall[:ROWS, col_of(s ^ k)] = v[ROWS:, :]
                vall[ROWS:, col_of(s ^ k)] = v[:ROWS, :]
        first = first_slot(sc)
        for a in range(2):
            vel[a * HALF : (a + 1) * HALF, :] = vall[row_of(i ^ a, s), :]
        for r, x in enumerate((x0, x1, x2, x3)):
            t = s ^ r
            level = level_of(sc, t, 1)
            for a in range(2):
                rows = slice(a * HALF, (a + 1) * HALF)
                where = row_of(i ^ a, t)
                moved[...] = (
                    x[rows, :].astype(F32) - vall[where, :].astype(F32) * (1.0 / (SLOTS * PER))
                ).astype(BF)

                @pl.when(t == first)
                def _():
                    fin[rows, :] = moved[:, col_of(s)]
                    moved[...] = fresh[rows, :]

                hidden[where, :] = modulated(moved[...].astype(F32), ada, level)

    project(hidden, w, mine, theirs)


def whole(shape):
    return pl.BlockSpec(shape, lambda n: (0,) * len(shape))


def projected_shapes(heads, rows):
    return [jax.ShapeDtypeStruct((heads, rows, HD), BF)] * 2


def first_projection(sc, xs, far, ada, w):
    heads = w.shape[1] // HD

    def body(*refs):
        first_body(*refs, far=far)

    return pl.pallas_call(
        body,
        grid=(heads // 2,),
        in_specs=[SM]
        + [whole((TOK, WIDTH))] * 2
        + [whole(ada.shape), pl.BlockSpec((WIDTH, 2 * HD), lambda n: (0, n))],
        out_specs=[pl.BlockSpec((2, ROWS // 2, HD), lambda n: (n, 0, 0))] * 2,
        out_shape=projected_shapes(heads, ROWS // 2),
        scratch_shapes=[pltpu.VMEM((ROWS, WIDTH), BF)],
        compiler_params=params(24),
        cost_estimate=pl.CostEstimate(flops=4 * 10**9, bytes_accessed=10**7, transcendentals=0),
        name="modulate_project",
    )(sc, *xs, ada, w)


def second_projection(sc, xs, vs, fresh, ada, w):
    heads = w.shape[1] // HD
    return pl.pallas_call(
        second_body,
        grid=(heads // 2,),
        in_specs=[SM]
        + [whole((TOK, WIDTH))] * 4
        + [whole((2 * ROWS, COLS))] * 4
        + [whole((TOK, WIDTH)), whole(ada.shape), pl.BlockSpec((WIDTH, 2 * HD), lambda n: (0, n))],
        out_specs=[pl.BlockSpec((2, ROWS, HD), lambda n: (n, 0, 0))] * 2
        + [whole((TOK, WIDTH)), whole((TOK, COLS))],
        out_shape=projected_shapes(heads, ROWS)
        + [jax.ShapeDtypeStruct((TOK, WIDTH), BF), jax.ShapeDtypeStruct((TOK, COLS), BF)],
        scratch_shapes=[
            pltpu.VMEM((2 * ROWS, WIDTH), BF),
            pltpu.VMEM((2 * ROWS, WIDTH), BF),
            pltpu.VMEM((HALF, WIDTH), BF),
        ],
        compiler_params=params(40),
        name="advance_modulate_project",
    )(sc, *xs, *vs, fresh, ada, w)


def pack_body(sc, *refs):
    parts, (out, chip) = refs[:-2], refs[-2:]
    i, h = sc[8] % 2, sc[8] // 2
    for k in range(2):
        to = pl.ds(10 * jnp.where(k == 0, i, 1 - i), 10)
        if len(parts) == 2:
            chip[to] = parts[k][...]
        else:
            cut = ROWS // 2
            chip[to, pl.ds(pl.multiple_of(h * cut, cut), cut)] = parts[2 * k][...]
            chip[to, pl.ds(pl.multiple_of((1 - h) * cut, cut), cut)] = parts[2 * k + 1][...]
    for g in range(8):
        out[g, 3] = chip[4 + g]
        out[g, 4] = chip[12 + g]

    def queries(low, high, at):
        for n in range(24):
            if low <= n < high:
                out[n // 3, n % 3] = chip[n - at]
            else:
                out[n // 3, n % 3] = jnp.zeros((ROWS, HD), BF)

    @pl.when(h == 0)
    def _():
        queries(0, 20, 0)

    @pl.when(h != 0)
    def _():
        queries(20, 24, 20)


def pack(sc, *parts):
    return pl.pallas_call(
        pack_body,
        in_specs=[SM] + [VM] * len(parts),
        out_specs=VM,
        out_shape=jax.ShapeDtypeStruct((8, 5, ROWS, HD), BF),
        scratch_shapes=[pltpu.VMEM((20, ROWS, HD), BF)],
        compiler_params=params(16),
        name="pack_heads",
    )(sc, *parts)


QROWS = 4 * 3 * HALF
BLOCK = 128


def attend_body(step, parts, chunk, last, sc, q, *refs):
    blocks, refs = refs[:parts], refs[parts:]
    if last:
        top_in, acc_in, out, qs, ks, vs, tops, accs = refs
    else:
        tops, accs, qs, ks, vs = refs
    keys = ks.shape[1]
    at = 0
    for ref in blocks:
        for b in range(ref.shape[0]):
            for j in range(SLOTS):
                rows = slice(j * HALF, (j + 1) * HALF)
                ks[j, at * HALF : (at + 1) * HALF, :] = ref[b, 0, rows, :]
                vs[j, at * HALF : (at + 1) * HALF, :HD] = ref[b, 1, rows, :]
            at += 1
    vs[:, :, HD:] = jnp.ones((SLOTS, keys, HD), BF)
    factor = LOG2E / math.sqrt(HD)
    for c in range(4):
        for m in range(3):
            both = ((q[c, m].astype(F32) + q[4 + c, m].astype(F32)) * factor).astype(BF)
            for j in range(SLOTS):
                qs[j, (c * 3 + m) * HALF : (c * 3 + m + 1) * HALF, :] = both[j * HALF : (j + 1) * HALF]

    def per_span(t, _):
        if last:
            top, acc = tops, accs
            top[...] = top_in[t]
            acc[...] = acc_in[t]
        else:
            top, acc = tops.at[t], accs.at[t]
            top[...] = jnp.full(top.shape, -1e30, F32)
            acc[...] = jnp.zeros(acc.shape, F32)
        own = id_of(sc, t, step)

        def per_key(j, _):
            @pl.when(id_of(sc, j, step) <= own)
            def _():
                def scores_of(r, n):
                    return lax.dot_general(
                        qs[t, r : r + BLOCK], ks[j, n : n + chunk, :], (((1,), (1,)), ((), ())),
                        preferred_element_type=F32,
                    )

                todo = [(r, n) for r in range(0, QROWS, BLOCK) for n in range(0, keys, chunk)]
                ahead = scores_of(*todo[0])
                for x, (r, n) in enumerate(todo):
                    scores = ahead
                    rows = slice(r, r + BLOCK)
                    if n == 0:
                        old, total = top[rows], acc[rows]
                    if x + 1 < len(todo):
                        ahead = scores_of(*todo[x + 1])
                    new = jnp.maximum(old, jnp.max(scores, axis=-1, keepdims=True))
                    weights = jnp.exp2(scores - new[:, :1]).astype(BF)
                    shrink = jnp.exp2(old - new)
                    total = total * jnp.concatenate([shrink, shrink], axis=1) + jnp.dot(
                        weights, vs[j, n : n + chunk, :], preferred_element_type=F32
                    )
                    old = new
                    if n + chunk == keys:
                        top[rows] = new
                        acc[rows] = total

            return 0

        lax.fori_loop(0, SLOTS, per_key, 0)
        if last:
            res = (acc[:, :HD] / acc[:, HD:]).astype(BF)
            rows = pl.ds(pl.multiple_of(t * HALF, HALF), HALF)
            for c in range(4):
                for m in range(3):
                    piece = res[(c * 3 + m) * HALF : (c * 3 + m + 1) * HALF]
                    out[c, m, rows, :] = piece
                    out[4 + c, m, rows, :] = piece
        return 0

    lax.fori_loop(0, SLOTS, per_span, 0)


def attend(step, sc, q, blocks, chunk, state=None):
    last = state is not None
    keys = sum(b.shape[0] for b in blocks) * HALF

    def body(*refs):
        attend_body(step, len(blocks), chunk, last, *refs)

    state_shapes = [(QROWS, HD), (QROWS, 2 * HD)]
    scratch = [
        pltpu.VMEM((SLOTS, QROWS, HD), BF),
        pltpu.VMEM((SLOTS, keys, HD), BF),
        pltpu.VMEM((SLOTS, keys, 2 * HD), BF),
    ]
    if last:
        out_shape = jax.ShapeDtypeStruct((8, 3, ROWS, HD), BF)
        scratch += [pltpu.VMEM(x, F32) for x in state_shapes]
    else:
        out_shape = [jax.ShapeDtypeStruct((SLOTS, *x), F32) for x in state_shapes]
    pairs = 10 * QROWS * keys
    return pl.pallas_call(
        body,
        in_specs=[SM] + [VM] * (1 + len(blocks) + (2 if last else 0)),
        out_specs=VM if last else [VM, VM],
        out_shape=out_shape,
        scratch_shapes=scratch,
        compiler_params=params(32),
        cost_estimate=pl.CostEstimate(
            flops=pairs * HD * 8, bytes_accessed=8 * 10**6, transcendentals=pairs
        ),
        name="span_attention_end" if last else "span_attention_begin",
    )(sc, q, *blocks, *(state or ()))


def out_body(step, sc, mine, other, ada, w, out, attn):
    n = pl.program_id(0)
    s = sc[8]
    i = s % 2
    width = w.shape[1]

    @pl.when(n == 0)
    def _():
        for m in range(24):
            attn[:ROWS, m * HD : (m + 1) * HD] = mine[m]
            attn[ROWS:, m * HD : (m + 1) * HD] = other[m]

    product = jnp.dot(attn[...], w[...], preferred_element_type=F32)
    cols = pl.ds(pl.multiple_of(s * COLS + n * width, 128), width)
    for t in range(SLOTS):
        gate = ada[level_of(sc, t, step), 2:3, cols]
        for a in range(2):
            at = (a * SLOTS + t) * HALF
            piece = (product[at : at + HALF] * gate).astype(BF)
            if step == 0:
                out[at : at + HALF, :] = piece
            else:
                rows = pl.ds(pl.multiple_of((i ^ a) * HALF, HALF), HALF)
                out[s ^ t, rows, :] = piece


def out_projection(step, sc, mine, other, ada, w):
    width = 256
    if step == 0:
        out_spec = pl.BlockSpec((2 * ROWS, width), lambda n: (0, n))
        out_shape = jax.ShapeDtypeStruct((2 * ROWS, COLS), BF)
    else:
        out_spec = pl.BlockSpec((SLOTS, TOK, width), lambda n: (0, 0, n))
        out_shape = jax.ShapeDtypeStruct((SLOTS, TOK, COLS), BF)

    def body(*refs):
        out_body(step, *refs)

    return pl.pallas_call(
        body,
        grid=(COLS // width,),
        in_specs=[SM]
        + [whole((24, ROWS, HD))] * 2
        + [whole(ada.shape), pl.BlockSpec((WIDTH, width), lambda n: (0, n))],
        out_specs=out_spec,
        out_shape=out_shape,
        scratch_shapes=[pltpu.VMEM((2 * ROWS, WIDTH), BF)],
        compiler_params=params(32),
        name="out_projection",
    )(sc, mine, other, ada, w)


def finish_body(sc, vel, r0, r1, r2, r3, out):
    s = sc[8]
    out[0] = vel[...]
    for k, r in enumerate((r0, r1, r2, r3)):
        out[1, :, col_of(s ^ k)] = r[...]


def finish(sc, vel, rs):
    return pl.pallas_call(
        finish_body,
        in_specs=[SM] + [VM] * 5,
        out_specs=VM,
        out_shape=jax.ShapeDtypeStruct((2, TOK, WIDTH), BF),
        compiler_params=params(16),
        name="collect_velocity",
    )(sc, vel, *rs)


def gather_slots(x):
    far = move(x, h=1)
    near = move(x, i=1)
    return x, near, far, move(far, i=1)


def begin_keys(low, high):
    low_y = move(low, y=2)
    high_z = [move(high, z=k) for k in (1, -1, 2)]
    early = jnp.concatenate([low, high, low_y, *high_z])
    lows = jnp.concatenate([low, low_y])
    highs = jnp.concatenate([high, *high_z])
    late = [move(lows, z=k) for k in (1, -1, 2)] + [move(highs, y=2)]
    return [early, move(early, i=1)], late


def shards(latents, fresh, span_ids, noise_step, ada_table, w_qkv, w_out):
    pos = lax.axis_index("slot").astype(jnp.int32).reshape(1)
    sc = jnp.concatenate([span_ids, noise_step, pos])
    own = latents[0]

    def one_step(step, *parts):
        got = exchange(pack(sc, *parts))
        early, late = begin_keys(got[4:6, 3:], got[6:, 3:])
        state = attend(step, sc, got, early, 768)
        late, state = lax.optimization_barrier((late, state))
        late = jnp.concatenate(late)
        attn = attend(step, sc, got, [late, move(late, i=1)], 1280, state)
        attn = exchange(attn).reshape(24, ROWS, HD)
        return out_projection(step, sc, attn, move(attn, i=1), ada_table, w_out)

    far = move(own, h=1)
    near = move(own, i=1)
    near_parts = first_projection(sc, (own, near), 0, ada_table, w_qkv)
    far, near_parts = lax.optimization_barrier((far, near_parts))
    far_near = move(far, i=1)
    far_parts = first_projection(sc, (far, far_near), 2, ada_table, w_qkv)
    vel = one_step(
        0, near_parts[0], far_parts[0], move(near_parts[1], i=1), move(far_parts[1], i=1)
    )
    xs = (own, near, far, far_near)
    mine, theirs, vel, fin = second_projection(sc, xs, gather_slots(vel), fresh, ada_table, w_qkv)
    out = one_step(1, mine, move(theirs, i=1))
    rs = [out[0], move(out[1], i=1), move(out[2], h=1), move(out[3], h=1, i=1)]
    return finish(sc, vel, rs)[:, None], fin


def solution(mesh):
    in_specs = (
        P("slot", "ctx", None),
        P("ctx", None),
        P(),
        P(),
        P(),
        P(None, "slot"),
        P(None, "slot"),
    )
    out_specs = (P(None, "slot", "ctx", None), P("ctx", "slot"))
    return jax.shard_map(shards, mesh=mesh, in_specs=in_specs, out_specs=out_specs, check_vma=False)
```

```python
import math

import jax
import jax.numpy as jnp
from jax import lax
from jax.experimental import pallas as pl
from jax.experimental.pallas import tpu as pltpu
from jax.sharding import PartitionSpec as P

HD = 128
EPS = 1e-06
BF = jnp.bfloat16
F32 = jnp.float32
AXES = ("slot", "ctx")
VM = pl.BlockSpec(memory_space=pltpu.VMEM)
SM = pl.BlockSpec(memory_space=pltpu.SMEM)
SLOTS = 4
PER = 2
TOK = 64
HALF = 32
ROWS = SLOTS * HALF
WIDTH = 3072
COLS = WIDTH // SLOTS
LOG2E = 1.4426950408889634


def where_is(flat):
    s, c = flat // 32, flat % 32
    return dict(h=s // 2, i=s % 2, z=c // 8, xl=(c // 4) % 2, y=c % 4)


def flat_of(d):
    return (d["h"] * 2 + d["i"]) * 32 + d["z"] * 8 + d["xl"] * 4 + d["y"]


def move(x, h=0, i=0, z=0, y=0):
    pairs = []
    for f in range(128):
        d = where_is(f)
        d["h"] = (d["h"] + h) % 2
        d["i"] = (d["i"] + i) % 2
        d["z"] = (d["z"] + z) % 4
        d["y"] = (d["y"] + y) % 4
        pairs.append((f, flat_of(d)))
    return lax.ppermute(x, AXES, pairs)


def group_lists():
    out = []
    for i in range(2):
        for z in range(4):
            for yh in range(2):
                out.append(
                    [
                        flat_of(dict(h=h, i=i, z=z, xl=xl, y=2 * yh + yl))
                        for h in range(2)
                        for xl in range(2)
                        for yl in range(2)
                    ]
                )
    return out


def exchange(x):
    return lax.all_to_all(x, AXES, 0, 0, tiled=True, axis_index_groups=group_lists())


def params(mib, **kw):
    return pltpu.CompilerParams(vmem_limit_bytes=mib * 1024 * 1024, **kw)


def first_slot(sc):
    best, at = sc[0], jnp.int32(0)
    for j in range(1, SLOTS):
        less = sc[j] < best
        best = jnp.where(less, sc[j], best)
        at = jnp.where(less, j, at)
    return at


def rank_of(sc, t, step):
    mine = sc[t]
    rank = jnp.int32(0)
    for j in range(SLOTS):
        rank = rank + (sc[j] < mine).astype(jnp.int32)
    if step == 0:
        return rank
    return jnp.where(rank == 0, SLOTS - 1, rank - 1)


def level_of(sc, t, step):
    rank = rank_of(sc, t, 0)
    level = PER * rank + sc[SLOTS + t] + 1
    if step == 0:
        return level
    return jnp.where(rank == 0, SLOTS * PER, level - 1)


def row_of(half, slot):
    return pl.ds(pl.multiple_of((half * SLOTS + slot) * HALF, HALF), HALF)


def col_of(slot, width=COLS):
    return pl.ds(pl.multiple_of(slot * width, 128), width)


def modulated(values, ada, level):
    center = jnp.mean(values, axis=-1, keepdims=True)
    off = values - center
    spread = jnp.mean(off * off, axis=-1, keepdims=True)
    normed = off * lax.rsqrt(spread + EPS)
    return (normed * (1.0 + ada[level, 1:2, :]) + ada[level, 0:1, :]).astype(BF)


def project(hidden, w, mine, theirs):
    out = jnp.dot(hidden[...], w[...], preferred_element_type=F32).astype(BF)
    cut = out.shape[0] // 2
    for k in range(2):
        mine[k] = out[:cut, k * HD : (k + 1) * HD]
        theirs[k] = out[cut:, k * HD : (k + 1) * HD]


def first_body(sc, x0, x1, ada, w, mine, theirs, hidden, *, far):
    s = sc[8]
    i = s % 2

    @pl.when(pl.program_id(0) == 0)
    def _():
        for r, x in enumerate((x0, x1)):
            t = s ^ (r + far)
            level = level_of(sc, t, 0)
            for a in range(2):
                values = x[a * HALF : (a + 1) * HALF, :].astype(F32)
                at = pl.multiple_of(((i ^ a) * 2 + t % 2) * HALF, HALF)
                hidden[pl.ds(at, HALF), :] = modulated(values, ada, level)

    project(hidden, w, mine, theirs)


def second_body(
    sc, x0, x1, x2, x3, v0, v1, v2, v3, fresh, ada, w,
    mine, theirs, vel, fin, hidden, vall, moved,
):
    s = sc[8]
    i = s % 2

    @pl.when(pl.program_id(0) == 0)
    def _():
        for k, v in enumerate((v0, v1, v2, v3)):
            if k % 2 == 0:
                vall[:, col_of(s ^ k)] = v[...]
            else:
                vall[:ROWS, col_of(s ^ k)] = v[ROWS:, :]
                vall[ROWS:, col_of(s ^ k)] = v[:ROWS, :]
        first = first_slot(sc)
        for a in range(2):
            vel[a * HALF : (a + 1) * HALF, :] = vall[row_of(i ^ a, s), :]
        for r, x in enumerate((x0, x1, x2, x3)):
            t = s ^ r
            level = level_of(sc, t, 1)
            for a in range(2):
                rows = slice(a * HALF, (a + 1) * HALF)
                where = row_of(i ^ a, t)
                moved[...] = (
                    x[rows, :].astype(F32) - vall[where, :].astype(F32) * (1.0 / (SLOTS * PER))
                ).astype(BF)

                @pl.when(t == first)
                def _():
                    fin[rows, :] = moved[:, col_of(s)]
                    moved[...] = fresh[rows, :]

                hidden[where, :] = modulated(moved[...].astype(F32), ada, level)

    project(hidden, w, mine, theirs)


def whole(shape):
    return pl.BlockSpec(shape, lambda n: (0,) * len(shape))


def projected_shapes(heads, rows):
    return [jax.ShapeDtypeStruct((heads, rows, HD), BF)] * 2


def first_projection(sc, xs, far, ada, w):
    heads = w.shape[1] // HD

    def body(*refs):
        first_body(*refs, far=far)

    return pl.pallas_call(
        body,
        grid=(heads // 2,),
        in_specs=[SM]
        + [whole((TOK, WIDTH))] * 2
        + [whole(ada.shape), pl.BlockSpec((WIDTH, 2 * HD), lambda n: (0, n))],
        out_specs=[pl.BlockSpec((2, ROWS // 2, HD), lambda n: (n, 0, 0))] * 2,
        out_shape=projected_shapes(heads, ROWS // 2),
        scratch_shapes=[pltpu.VMEM((ROWS, WIDTH), BF)],
        compiler_params=params(24),
        cost_estimate=pl.CostEstimate(flops=4 * 10**9, bytes_accessed=10**7, transcendentals=0),
        name="modulate_project",
    )(sc, *xs, ada, w)


def second_projection(sc, xs, vs, fresh, ada, w):
    heads = w.shape[1] // HD
    return pl.pallas_call(
        second_body,
        grid=(heads // 2,),
        in_specs=[SM]
        + [whole((TOK, WIDTH))] * 4
        + [whole((2 * ROWS, COLS))] * 4
        + [whole((TOK, WIDTH)), whole(ada.shape), pl.BlockSpec((WIDTH, 2 * HD), lambda n: (0, n))],
        out_specs=[pl.BlockSpec((2, ROWS, HD), lambda n: (n, 0, 0))] * 2
        + [whole((TOK, WIDTH)), whole((TOK, COLS))],
        out_shape=projected_shapes(heads, ROWS)
        + [jax.ShapeDtypeStruct((TOK, WIDTH), BF), jax.ShapeDtypeStruct((TOK, COLS), BF)],
        scratch_shapes=[
            pltpu.VMEM((2 * ROWS, WIDTH), BF),
            pltpu.VMEM((2 * ROWS, WIDTH), BF),
            pltpu.VMEM((HALF, WIDTH), BF),
        ],
        compiler_params=params(40),
        name="advance_modulate_project",
    )(sc, *xs, *vs, fresh, ada, w)


def pack_body(sc, *refs):
    parts, (out, chip) = refs[:-2], refs[-2:]
    i, h = sc[8] % 2, sc[8] // 2
    for k in range(2):
        to = pl.ds(10 * jnp.where(k == 0, i, 1 - i), 10)
        if len(parts) == 2:
            chip[to] = parts[k][...]
        else:
            cut = ROWS // 2
            chip[to, pl.ds(pl.multiple_of(h * cut, cut), cut)] = parts[2 * k][...]
            chip[to, pl.ds(pl.multiple_of((1 - h) * cut, cut), cut)] = parts[2 * k + 1][...]
    for g in range(8):
        out[g, 3] = chip[4 + g]
        out[g, 4] = chip[12 + g]

    def queries(low, high, at):
        for n in range(24):
            if low <= n < high:
                out[n // 3, n % 3] = chip[n - at]
            else:
                out[n // 3, n % 3] = jnp.zeros((ROWS, HD), BF)

    @pl.when(h == 0)
    def _():
        queries(0, 20, 0)

    @pl.when(h != 0)
    def _():
        queries(20, 24, 20)


def pack(sc, *parts):
    return pl.pallas_call(
        pack_body,
        in_specs=[SM] + [VM] * len(parts),
        out_specs=VM,
        out_shape=jax.ShapeDtypeStruct((8, 5, ROWS, HD), BF),
        scratch_shapes=[pltpu.VMEM((20, ROWS, HD), BF)],
        compiler_params=params(16),
        name="pack_heads",
    )(sc, *parts)


QROWS = 4 * 3 * HALF


def attend_body(step, parts, chunk, block, last, sc, q, *refs):
    blocks, refs = refs[:parts], refs[parts:]
    if last:
        top_in, acc_in, out, qs, ks, vs = refs
    else:
        top_out, acc_out, qs, ks, vs = refs
    keys = ks.shape[0] // SLOTS
    ranks = [rank_of(sc, t, step) for t in range(SLOTS)]
    at = 0
    for ref in blocks:
        for b in range(ref.shape[0]):
            for j in range(SLOTS):
                rows = slice(j * HALF, (j + 1) * HALF)
                to = pl.ds(pl.multiple_of(ranks[j] * keys + at * HALF, HALF), HALF)
                ks[to, :] = ref[b, 0, rows, :]
                vs[to, :HD] = ref[b, 1, rows, :]
            at += 1
    vs[:, HD:] = jnp.ones((SLOTS * keys, HD), BF)
    factor = LOG2E / math.sqrt(HD)
    for c in range(4):
        for m in range(3):
            both = ((q[c, m].astype(F32) + q[4 + c, m].astype(F32)) * factor).astype(BF)
            for j in range(SLOTS):
                to = pl.ds(pl.multiple_of(ranks[j] * QROWS + (c * 3 + m) * HALF, HALF), HALF)
                qs[to, :] = both[j * HALF : (j + 1) * HALF]

    def scores_of(rank, r, n, size):
        return lax.dot_general(
            qs[rank * QROWS + r : rank * QROWS + r + block], ks[n : n + size, :],
            (((1,), (1,)), ((), ())), preferred_element_type=F32,
        )

    todo = []
    for rank in reversed(range(SLOTS)):
        for r in range(0, QROWS, block):
            span = (rank + 1) * keys
            todo += [(rank, r, n, min(chunk, span - n)) for n in range(0, span, chunk)]
    ahead = scores_of(*todo[0])
    for x, (rank, r, n, size) in enumerate(todo):
        scores = ahead
        rows = slice(r, r + block)
        if n == 0 and last:
            old, total = top_in[rank, rows], acc_in[rank, rows]
        if x + 1 < len(todo):
            ahead = scores_of(*todo[x + 1])
        new = jnp.max(scores, axis=-1, keepdims=True)
        fresh = n == 0 and not last
        new = jnp.broadcast_to(new, (block, HD)) if fresh else jnp.maximum(old, new)
        weights = jnp.exp2(scores - new[:, :1]).astype(BF)
        part = jnp.dot(weights, vs[n : n + size, :], preferred_element_type=F32)
        if fresh:
            total = part
        else:
            shrink = jnp.exp2(old - new)
            total = total * jnp.concatenate([shrink, shrink], axis=1) + part
        old = new
        if n + size < (rank + 1) * keys:
            continue
        if not last:
            top_out[rank, rows] = new
            acc_out[rank, rows] = total
            continue
        res = (total[:, :HD] / total[:, HD:]).astype(BF)
        slot = jnp.int32(0)
        for j in range(1, SLOTS):
            slot = jnp.where(ranks[j] == rank, j, slot)
        to = pl.ds(pl.multiple_of(slot * HALF, HALF), HALF)
        for k in range(block // HALF):
            c, m = divmod(r // HALF + k, 3)
            out[c, m, to, :] = res[k * HALF : (k + 1) * HALF]
            out[4 + c, m, to, :] = res[k * HALF : (k + 1) * HALF]


def attend(step, sc, q, blocks, chunk, block, state=None):
    last = state is not None
    keys = sum(b.shape[0] for b in blocks) * HALF

    def body(*refs):
        attend_body(step, len(blocks), chunk, block, last, *refs)

    scratch = [
        pltpu.VMEM((SLOTS * QROWS, HD), BF),
        pltpu.VMEM((SLOTS * keys, HD), BF),
        pltpu.VMEM((SLOTS * keys, 2 * HD), BF),
    ]
    if last:
        out_shape = jax.ShapeDtypeStruct((8, 3, ROWS, HD), BF)
    else:
        out_shape = [
            jax.ShapeDtypeStruct((SLOTS, QROWS, HD), F32),
            jax.ShapeDtypeStruct((SLOTS, QROWS, 2 * HD), F32),
        ]
    pairs = 10 * QROWS * keys
    return pl.pallas_call(
        body,
        in_specs=[SM] + [VM] * (1 + len(blocks) + (2 if last else 0)),
        out_specs=VM if last else [VM, VM],
        out_shape=out_shape,
        scratch_shapes=scratch,
        compiler_params=params(32),
        cost_estimate=pl.CostEstimate(
            flops=pairs * HD * 8, bytes_accessed=8 * 10**6, transcendentals=pairs
        ),
        name="span_attention_end" if last else "span_attention_begin",
    )(sc, q, *blocks, *(state or ()))


def out_body(step, sc, mine, other, ada, w, out, attn):
    n = pl.program_id(0)
    s = sc[8]
    i = s % 2
    width = w.shape[1]

    @pl.when(n == 0)
    def _():
        for m in range(24):
            attn[:ROWS, m * HD : (m + 1) * HD] = mine[m]
            attn[ROWS:, m * HD : (m + 1) * HD] = other[m]

    product = jnp.dot(attn[...], w[...], preferred_element_type=F32)
    cols = pl.ds(pl.multiple_of(s * COLS + n * width, 128), width)
    for t in range(SLOTS):
        gate = ada[level_of(sc, t, step), 2:3, cols]
        for a in range(2):
            at = (a * SLOTS + t) * HALF
            piece = (product[at : at + HALF] * gate).astype(BF)
            if step == 0:
                out[at : at + HALF, :] = piece
            else:
                rows = pl.ds(pl.multiple_of((i ^ a) * HALF, HALF), HALF)
                out[s ^ t, rows, :] = piece


def out_projection(step, sc, mine, other, ada, w):
    width = 256
    if step == 0:
        out_spec = pl.BlockSpec((2 * ROWS, width), lambda n: (0, n))
        out_shape = jax.ShapeDtypeStruct((2 * ROWS, COLS), BF)
    else:
        out_spec = pl.BlockSpec((SLOTS, TOK, width), lambda n: (0, 0, n))
        out_shape = jax.ShapeDtypeStruct((SLOTS, TOK, COLS), BF)

    def body(*refs):
        out_body(step, *refs)

    return pl.pallas_call(
        body,
        grid=(COLS // width,),
        in_specs=[SM]
        + [whole((24, ROWS, HD))] * 2
        + [whole(ada.shape), pl.BlockSpec((WIDTH, width), lambda n: (0, n))],
        out_specs=out_spec,
        out_shape=out_shape,
        scratch_shapes=[pltpu.VMEM((2 * ROWS, WIDTH), BF)],
        compiler_params=params(32),
        name="out_projection",
    )(sc, mine, other, ada, w)


def finish_body(sc, vel, r0, r1, r2, r3, out):
    s = sc[8]
    out[0] = vel[...]
    for k, r in enumerate((r0, r1, r2, r3)):
        out[1, :, col_of(s ^ k)] = r[...]


def finish(sc, vel, rs):
    return pl.pallas_call(
        finish_body,
        in_specs=[SM] + [VM] * 5,
        out_specs=VM,
        out_shape=jax.ShapeDtypeStruct((2, TOK, WIDTH), BF),
        compiler_params=params(16),
        name="collect_velocity",
    )(sc, vel, *rs)


def gather_slots(x):
    far = move(x, h=1)
    near = move(x, i=1)
    return x, near, far, move(far, i=1)


EARLY = ((1, 2), (1, 0), (-1, 0), (2, 0), (0, 2))
LATE = ((-1, 2), (2, 2))


def keys_from(x, places):
    return [move(x, z=z, y=y) for z, y in places]


def both_cores(parts):
    x = jnp.concatenate(parts)
    return [x, move(x, i=1)]


def shards(latents, fresh, span_ids, noise_step, ada_table, w_qkv, w_out):
    pos = lax.axis_index("slot").astype(jnp.int32).reshape(1)
    sc = jnp.concatenate([span_ids, noise_step, pos])
    own = latents[0]

    def one_step(step, *parts):
        got = exchange(pack(sc, *parts))
        own_keys = got[4:, 3:]
        early = keys_from(own_keys, EARLY)
        late = keys_from(own_keys, LATE)
        state = attend(step, sc, got, both_cores([own_keys, *early]), 1536, 384)
        late, state = lax.optimization_barrier((late, state))
        attn = attend(step, sc, got, both_cores(late), 1024, 384, state)
        attn = exchange(attn).reshape(24, ROWS, HD)
        return out_projection(step, sc, attn, move(attn, i=1), ada_table, w_out)

    far = move(own, h=1)
    near = move(own, i=1)
    near_parts = first_projection(sc, (own, near), 0, ada_table, w_qkv)
    far, near_parts = lax.optimization_barrier((far, near_parts))
    far_near = move(far, i=1)
    far_parts = first_projection(sc, (far, far_near), 2, ada_table, w_qkv)
    vel = one_step(
        0, near_parts[0], far_parts[0], move(near_parts[1], i=1), move(far_parts[1], i=1)
    )
    xs = (own, near, far, far_near)
    mine, theirs, vel, fin = second_projection(sc, xs, gather_slots(vel), fresh, ada_table, w_qkv)
    out = one_step(1, mine, move(theirs, i=1))
    rs = [out[0], move(out[1], i=1), move(out[2], h=1), move(out[3], h=1, i=1)]
    return finish(sc, vel, rs)[:, None], fin


def solution(mesh):
    in_specs = (
        P("slot", "ctx", None),
        P("ctx", None),
        P(),
        P(),
        P(),
        P(None, "slot"),
        P(None, "slot"),
    )
    out_specs = (P(None, "slot", "ctx", None), P("ctx", "slot"))
    return jax.shard_map(shards, mesh=mesh, in_specs=in_specs, out_specs=out_specs, check_vma=False)
```

```python
import math

import jax
import jax.numpy as jnp
from jax import lax
from jax.experimental import pallas as pl
from jax.experimental.pallas import tpu as pltpu
from jax.sharding import PartitionSpec as P

HD = 128
EPS = 1e-06
BF = jnp.bfloat16
F32 = jnp.float32
AXES = ("slot", "ctx")
VM = pl.BlockSpec(memory_space=pltpu.VMEM)
SM = pl.BlockSpec(memory_space=pltpu.SMEM)
SLOTS = 4
PER = 2
TOK = 64
HALF = 32
ROWS = SLOTS * HALF
WIDTH = 3072
COLS = WIDTH // SLOTS
LOG2E = 1.4426950408889634


def where_is(flat):
    s, c = flat // 32, flat % 32
    return dict(h=s // 2, i=s % 2, z=c // 8, xl=(c // 4) % 2, y=c % 4)


def flat_of(d):
    return (d["h"] * 2 + d["i"]) * 32 + d["z"] * 8 + d["xl"] * 4 + d["y"]


def move(x, h=0, i=0, z=0, y=0):
    pairs = []
    for f in range(128):
        d = where_is(f)
        d["h"] = (d["h"] + h) % 2
        d["i"] = (d["i"] + i) % 2
        d["z"] = (d["z"] + z) % 4
        d["y"] = (d["y"] + y) % 4
        pairs.append((f, flat_of(d)))
    return lax.ppermute(x, AXES, pairs)


def group_lists():
    out = []
    for i in range(2):
        for z in range(4):
            for yh in range(2):
                out.append(
                    [
                        flat_of(dict(h=h, i=i, z=z, xl=xl, y=2 * yh + yl))
                        for h in range(2)
                        for xl in range(2)
                        for yl in range(2)
                    ]
                )
    return out


def exchange(x):
    return lax.all_to_all(x, AXES, 0, 0, tiled=True, axis_index_groups=group_lists())


def params(mib, **kw):
    return pltpu.CompilerParams(vmem_limit_bytes=mib * 1024 * 1024, **kw)


def first_slot(sc):
    best, at = sc[0], jnp.int32(0)
    for j in range(1, SLOTS):
        less = sc[j] < best
        best = jnp.where(less, sc[j], best)
        at = jnp.where(less, j, at)
    return at


def rank_of(sc, t, step):
    mine = sc[t]
    rank = jnp.int32(0)
    for j in range(SLOTS):
        rank = rank + (sc[j] < mine).astype(jnp.int32)
    if step == 0:
        return rank
    return jnp.where(rank == 0, SLOTS - 1, rank - 1)


def level_of(sc, t, step):
    rank = rank_of(sc, t, 0)
    level = PER * rank + sc[SLOTS + t] + 1
    if step == 0:
        return level
    return jnp.where(rank == 0, SLOTS * PER, level - 1)


def row_of(half, slot):
    return pl.ds(pl.multiple_of((half * SLOTS + slot) * HALF, HALF), HALF)


def col_of(slot, width=COLS):
    return pl.ds(pl.multiple_of(slot * width, 128), width)


def modulated(values, ada, level):
    center = jnp.mean(values, axis=-1, keepdims=True)
    off = values - center
    spread = jnp.mean(off * off, axis=-1, keepdims=True)
    normed = off * lax.rsqrt(spread + EPS)
    return (normed * (1.0 + ada[level, 1:2, :]) + ada[level, 0:1, :]).astype(BF)


def project(hidden, w, mine, theirs):
    out = jnp.dot(hidden[...], w[...], preferred_element_type=F32).astype(BF)
    cut = out.shape[0] // 2
    for k in range(mine.shape[0]):
        mine[k] = out[:cut, k * HD : (k + 1) * HD]
        theirs[k] = out[cut:, k * HD : (k + 1) * HD]


PAIR = 2 * HALF


def first_body(sc, x0, x1, ada, w, mine, theirs, hidden, *, far):
    s = sc[8]
    i = s % 2
    for r, x in enumerate((x0, x1)):
        t = s ^ (r + far)
        level = level_of(sc, t, 0)
        for a in range(2):
            values = x[a * HALF : (a + 1) * HALF, :].astype(F32)
            to = pl.ds(pl.multiple_of(((i ^ a) * 2 + t % 2) * HALF, HALF), HALF)
            hidden[to, :] = modulated(values, ada, level)
    project(hidden, w, mine, theirs)


def second_body(
    sc, x0, x1, x2, x3, v0, v1, v2, v3, fresh, ada, w,
    mine, theirs, vel, fin, hidden, vall,
):
    s = sc[8]
    i = s % 2
    step_size = 1.0 / (SLOTS * PER)
    for k, v in enumerate((v0, v1, v2, v3)):
        if k % 2 == 0:
            vall[:, col_of(s ^ k)] = v[...]
        else:
            vall[:ROWS, col_of(s ^ k)] = v[ROWS:, :]
            vall[ROWS:, col_of(s ^ k)] = v[:ROWS, :]
    first = first_slot(sc)
    for r, x in enumerate((x0, x1, x2, x3)):
        t = s ^ r
        level = level_of(sc, t, 1)
        for a in range(2):
            rows = slice(a * HALF, (a + 1) * HALF)
            where = row_of(i ^ a, t)
            moved = x[rows, :].astype(F32) - vall[where, :].astype(F32) * step_size
            taken = jnp.where(t == first, fresh[rows, :], moved.astype(BF))
            hidden[where, :] = modulated(taken.astype(F32), ada, level)
    for r, x in enumerate((x0, x1, x2, x3)):

        @pl.when(s ^ r == first)
        def _():
            for a in range(2):
                rows = slice(a * HALF, (a + 1) * HALF)
                drift = vall[row_of(i ^ a, s ^ r), col_of(s)].astype(F32)
                fin[rows, :] = (x[rows, col_of(s)].astype(F32) - drift * step_size).astype(BF)

    for a in range(2):
        vel[a * HALF : (a + 1) * HALF, :] = vall[row_of(i ^ a, s), :]
    project(hidden, w, mine, theirs)


def projected_shapes(heads, rows):
    return [jax.ShapeDtypeStruct((heads, rows, HD), BF)] * 2


def first_projection(sc, xs, far, ada, w):
    def body(*refs):
        first_body(*refs, far=far)

    return pl.pallas_call(
        body,
        in_specs=[SM] + [VM] * 4,
        out_specs=[VM] * 2,
        out_shape=projected_shapes(w.shape[1] // HD, PAIR),
        scratch_shapes=[pltpu.VMEM((2 * PAIR, WIDTH), BF)],
        compiler_params=params(24),
        cost_estimate=pl.CostEstimate(flops=4 * 10**9, bytes_accessed=10**7, transcendentals=0),
        name="modulate_project",
    )(sc, *xs, ada, w)


def second_projection(sc, xs, vs, fresh, ada, w):
    return pl.pallas_call(
        second_body,
        in_specs=[SM] + [VM] * 11,
        out_specs=[VM] * 4,
        out_shape=projected_shapes(w.shape[1] // HD, ROWS)
        + [jax.ShapeDtypeStruct((TOK, WIDTH), BF), jax.ShapeDtypeStruct((TOK, COLS), BF)],
        scratch_shapes=[pltpu.VMEM((2 * ROWS, WIDTH), BF)] * 2,
        compiler_params=params(32),
        cost_estimate=pl.CostEstimate(flops=4 * 10**9, bytes_accessed=10**7, transcendentals=0),
        name="advance_modulate_project",
    )(sc, *xs, *vs, fresh, ada, w)


def pack_body(step, sc, *refs):
    parts, (out, chip) = refs[:-2], refs[-2:]
    i, h = sc[8] % 2, sc[8] // 2
    for k in range(2):
        to = pl.ds(10 * jnp.where(k == 0, i, 1 - i), 10)
        if step == 1:
            chip[to] = parts[k][...]
            continue
        for n in range(2):
            at = pl.multiple_of((h ^ n) * PAIR, PAIR)
            chip[to, pl.ds(at, PAIR)] = parts[2 * k + n][...]
    for g in range(8):
        out[g, 3] = chip[4 + g]
        out[g, 4] = chip[12 + g]

    def queries(low, high, at):
        for n in range(24):
            if low <= n < high:
                out[n // 3, n % 3] = chip[n - at]
            else:
                out[n // 3, n % 3] = jnp.zeros((ROWS, HD), BF)

    @pl.when(h == 0)
    def _():
        queries(0, 20, 0)

    @pl.when(h != 0)
    def _():
        queries(20, 24, 20)


def pack(step, sc, *parts):
    def body(*refs):
        pack_body(step, *refs)

    return pl.pallas_call(
        body,
        in_specs=[SM] + [VM] * len(parts),
        out_specs=VM,
        out_shape=jax.ShapeDtypeStruct((8, 5, ROWS, HD), BF),
        scratch_shapes=[pltpu.VMEM((20, ROWS, HD), BF)],
        compiler_params=params(16),
        name="pack_heads",
    )(sc, *parts)


QROWS = 4 * 3 * HALF


def attend_body(step, parts, chunk, block, last, sc, q, *refs):
    blocks, refs = refs[:parts], refs[parts:]
    if last:
        top_in, acc_in, out, qs, ks, vs = refs
    else:
        top_out, acc_out, qs, ks, vs = refs
    keys = ks.shape[0] // SLOTS
    ranks = [rank_of(sc, t, step) for t in range(SLOTS)]
    at = 0
    for ref in blocks:
        for b in range(ref.shape[0]):
            for j in range(SLOTS):
                rows = slice(j * HALF, (j + 1) * HALF)
                to = pl.ds(pl.multiple_of(ranks[j] * keys + at * HALF, HALF), HALF)
                ks[to, :] = ref[b, 0, rows, :]
                vs[to, :HD] = ref[b, 1, rows, :]
            at += 1
    vs[:, HD:] = jnp.ones((SLOTS * keys, HD), BF)
    factor = LOG2E / math.sqrt(HD)
    for c in range(4):
        for m in range(3):
            both = ((q[c, m].astype(F32) + q[4 + c, m].astype(F32)) * factor).astype(BF)
            for j in range(SLOTS):
                to = pl.ds(pl.multiple_of(ranks[j] * QROWS + (c * 3 + m) * HALF, HALF), HALF)
                qs[to, :] = both[j * HALF : (j + 1) * HALF]

    def scores_of(rank, r, n, size):
        return lax.dot_general(
            qs[rank * QROWS + r : rank * QROWS + r + block], ks[n : n + size, :],
            (((1,), (1,)), ((), ())), preferred_element_type=F32,
        )

    todo = []
    for rank in reversed(range(SLOTS)):
        for r in range(0, QROWS, block):
            span = (rank + 1) * keys
            todo += [(rank, r, n, min(chunk, span - n)) for n in range(0, span, chunk)]
    ahead = scores_of(*todo[0])
    for x, (rank, r, n, size) in enumerate(todo):
        scores = ahead
        rows = slice(r, r + block)
        if n == 0 and last:
            old, total = top_in[rank, rows], acc_in[rank, rows]
        if x + 1 < len(todo):
            ahead = scores_of(*todo[x + 1])
        new = jnp.max(scores, axis=-1, keepdims=True)
        fresh = n == 0 and not last
        new = jnp.broadcast_to(new, (block, HD)) if fresh else jnp.maximum(old, new)
        weights = jnp.exp2(scores - new[:, :1]).astype(BF)
        part = jnp.dot(weights, vs[n : n + size, :], preferred_element_type=F32)
        if fresh:
            total = part
        else:
            shrink = jnp.exp2(old - new)
            total = total * jnp.concatenate([shrink, shrink], axis=1) + part
        old = new
        if n + size < (rank + 1) * keys:
            continue
        if not last:
            top_out[rank, rows] = new
            acc_out[rank, rows] = total
            continue
        res = (total[:, :HD] / total[:, HD:]).astype(BF)
        slot = jnp.int32(0)
        for j in range(1, SLOTS):
            slot = jnp.where(ranks[j] == rank, j, slot)
        to = pl.ds(pl.multiple_of(slot * HALF, HALF), HALF)
        for k in range(block // HALF):
            c, m = divmod(r // HALF + k, 3)
            out[c, m, to, :] = res[k * HALF : (k + 1) * HALF]
            out[4 + c, m, to, :] = res[k * HALF : (k + 1) * HALF]


def attend(step, sc, q, blocks, chunk, block, state=None):
    last = state is not None
    keys = sum(b.shape[0] for b in blocks) * HALF

    def body(*refs):
        attend_body(step, len(blocks), chunk, block, last, *refs)

    scratch = [
        pltpu.VMEM((SLOTS * QROWS, HD), BF),
        pltpu.VMEM((SLOTS * keys, HD), BF),
        pltpu.VMEM((SLOTS * keys, 2 * HD), BF),
    ]
    if last:
        out_shape = jax.ShapeDtypeStruct((8, 3, ROWS, HD), BF)
    else:
        out_shape = [
            jax.ShapeDtypeStruct((SLOTS, QROWS, HD), F32),
            jax.ShapeDtypeStruct((SLOTS, QROWS, 2 * HD), F32),
        ]
    pairs = 10 * QROWS * keys
    return pl.pallas_call(
        body,
        in_specs=[SM] + [VM] * (1 + len(blocks) + (2 if last else 0)),
        out_specs=VM if last else [VM, VM],
        out_shape=out_shape,
        scratch_shapes=scratch,
        compiler_params=params(32),
        cost_estimate=pl.CostEstimate(
            flops=pairs * HD * 8, bytes_accessed=8 * 10**6, transcendentals=pairs
        ),
        name="span_attention_end" if last else "span_attention_begin",
    )(sc, q, *blocks, *(state or ()))


def out_body(step, sc, mine, other, ada, w, out, attn):
    s = sc[8]
    i = s % 2
    for m in range(24):
        attn[:ROWS, m * HD : (m + 1) * HD] = mine[m]
        attn[ROWS:, m * HD : (m + 1) * HD] = other[m]
    product = jnp.dot(attn[...], w[...], preferred_element_type=F32)
    for t in range(SLOTS):
        gate = ada[level_of(sc, t, step), 2:3, col_of(s)]
        for a in range(2):
            at = (a * SLOTS + t) * HALF
            piece = (product[at : at + HALF] * gate).astype(BF)
            if step == 0:
                out[at : at + HALF, :] = piece
            else:
                rows = pl.ds(pl.multiple_of((i ^ a) * HALF, HALF), HALF)
                out[s ^ t, rows, :] = piece


def out_projection(step, sc, mine, other, ada, w):
    shape = (2 * ROWS, COLS) if step == 0 else (SLOTS, TOK, COLS)

    def body(*refs):
        out_body(step, *refs)

    return pl.pallas_call(
        body,
        in_specs=[SM] + [VM] * 4,
        out_specs=VM,
        out_shape=jax.ShapeDtypeStruct(shape, BF),
        scratch_shapes=[pltpu.VMEM((2 * ROWS, WIDTH), BF)],
        compiler_params=params(32),
        cost_estimate=pl.CostEstimate(flops=2 * 10**9, bytes_accessed=6 * 10**6, transcendentals=0),
        name="out_projection",
    )(sc, mine, other, ada, w)


def finish_body(sc, vel, r0, r1, r2, r3, out):
    s = sc[8]
    out[0] = vel[...]
    for k, r in enumerate((r0, r1, r2, r3)):
        out[1, :, col_of(s ^ k)] = r[...]


def finish(sc, vel, rs):
    return pl.pallas_call(
        finish_body,
        in_specs=[SM] + [VM] * 5,
        out_specs=VM,
        out_shape=jax.ShapeDtypeStruct((2, TOK, WIDTH), BF),
        compiler_params=params(16),
        name="collect_velocity",
    )(sc, vel, *rs)


def gather_slots(x):
    far = move(x, h=1)
    near = move(x, i=1)
    return x, near, far, move(far, i=1)


def begin_keys(low, high):
    low_y = move(low, y=2)
    high_z = [move(high, z=k) for k in (1, -1, 2)]
    early = jnp.concatenate([low, high, low_y, *high_z])
    lows = jnp.concatenate([low, low_y])
    highs = jnp.concatenate([high, *high_z])
    late = [move(lows, z=k) for k in (1, -1, 2)] + [move(highs, y=2)]
    return early, late


def both_cores(x):
    return [x, move(x, i=1)]


def after(x, *others):
    return lax.optimization_barrier((x, *others))


def shards(latents, fresh, span_ids, noise_step, ada_table, w_qkv, w_out):
    pos = lax.axis_index("slot").astype(jnp.int32).reshape(1)
    sc = jnp.concatenate([span_ids, noise_step, pos])
    own = latents[0]

    def one_step(step, *parts):
        got = exchange(pack(step, sc, *parts))
        early, late = begin_keys(got[4:6, 3:], got[6:, 3:])
        state = attend(step, sc, got, both_cores(early), 768, 384)
        late, state = after(late, state)
        late = jnp.concatenate(late)
        attn = attend(step, sc, got, both_cores(late), 1280, 384, state)
        attn = exchange(attn).reshape(24, ROWS, HD)
        return out_projection(step, sc, attn, move(attn, i=1), ada_table, w_out)

    far = move(own, h=1)
    near = move(own, i=1)
    a = first_projection(sc, (own, near), 0, ada_table, w_qkv)
    far, a = after(far, a)
    far_near = move(far, i=1)
    b = first_projection(sc, (far, far_near), 2, ada_table, w_qkv)
    vel = one_step(0, a[0], b[0], move(a[1], i=1), move(b[1], i=1))
    xs = (own, near, far, far_near)
    mine, theirs, vel, fin = second_projection(sc, xs, gather_slots(vel), fresh, ada_table, w_qkv)
    out = one_step(1, mine, move(theirs, i=1))
    rs = [out[0], move(out[1], i=1), move(out[2], h=1), move(out[3], h=1, i=1)]
    return finish(sc, vel, rs)[:, None], fin


def solution(mesh):
    in_specs = (
        P("slot", "ctx", None),
        P("ctx", None),
        P(),
        P(),
        P(),
        P(None, "slot"),
        P(None, "slot"),
    )
    out_specs = (P(None, "slot", "ctx", None), P("ctx", "slot"))
    return jax.shard_map(shards, mesh=mesh, in_specs=in_specs, out_specs=out_specs, check_vma=False)
```

```python
import math

import jax
import jax.numpy as jnp
from jax import lax
from jax.experimental import pallas as pl
from jax.experimental.pallas import tpu as pltpu
from jax.sharding import PartitionSpec as P

HD = 128
EPS = 1e-06
BF = jnp.bfloat16
F32 = jnp.float32
AXES = ("slot", "ctx")
VM = pl.BlockSpec(memory_space=pltpu.VMEM)
SM = pl.BlockSpec(memory_space=pltpu.SMEM)
SLOTS = 4
PER = 2
TOK = 64
HALF = 32
ROWS = SLOTS * HALF
WIDTH = 3072
COLS = WIDTH // SLOTS
LOG2E = 1.4426950408889634


def where_is(flat):
    s, c = flat // 32, flat % 32
    return dict(h=s // 2, i=s % 2, z=c // 8, xl=(c // 4) % 2, y=c % 4)


def flat_of(d):
    return (d["h"] * 2 + d["i"]) * 32 + d["z"] * 8 + d["xl"] * 4 + d["y"]


def move(x, h=0, i=0, z=0, y=0):
    pairs = []
    for f in range(128):
        d = where_is(f)
        d["h"] = (d["h"] + h) % 2
        d["i"] = (d["i"] + i) % 2
        d["z"] = (d["z"] + z) % 4
        d["y"] = (d["y"] + y) % 4
        pairs.append((f, flat_of(d)))
    return lax.ppermute(x, AXES, pairs)


def group_lists():
    out = []
    for i in range(2):
        for z in range(4):
            for yh in range(2):
                out.append(
                    [
                        flat_of(dict(h=h, i=i, z=z, xl=xl, y=2 * yh + yl))
                        for h in range(2)
                        for xl in range(2)
                        for yl in range(2)
                    ]
                )
    return out


def exchange(x):
    return lax.all_to_all(x, AXES, 0, 0, tiled=True, axis_index_groups=group_lists())


def params(mib, **kw):
    return pltpu.CompilerParams(vmem_limit_bytes=mib * 1024 * 1024, **kw)


def first_slot(sc):
    best, at = sc[0], jnp.int32(0)
    for j in range(1, SLOTS):
        less = sc[j] < best
        best = jnp.where(less, sc[j], best)
        at = jnp.where(less, j, at)
    return at


def rank_of(sc, t, step):
    mine = sc[t]
    rank = jnp.int32(0)
    for j in range(SLOTS):
        rank = rank + (sc[j] < mine).astype(jnp.int32)
    if step == 0:
        return rank
    return jnp.where(rank == 0, SLOTS - 1, rank - 1)


def level_of(sc, t, step):
    rank = rank_of(sc, t, 0)
    level = PER * rank + sc[SLOTS + t] + 1
    if step == 0:
        return level
    return jnp.where(rank == 0, SLOTS * PER, level - 1)


def row_of(half, slot):
    return pl.ds(pl.multiple_of((half * SLOTS + slot) * HALF, HALF), HALF)


def col_of(slot, width=COLS):
    return pl.ds(pl.multiple_of(slot * width, 128), width)


def modulated(values, ada, level):
    center = jnp.mean(values, axis=-1, keepdims=True)
    off = values - center
    spread = jnp.mean(off * off, axis=-1, keepdims=True)
    normed = off * lax.rsqrt(spread + EPS)
    return (normed * (1.0 + ada[level, 1:2, :]) + ada[level, 0:1, :]).astype(BF)


def project(hidden, w, mine, theirs):
    out = jnp.dot(hidden[...], w[...], preferred_element_type=F32).astype(BF)
    cut = out.shape[0] // 2
    for k in range(mine.shape[0]):
        mine[k] = out[:cut, k * HD : (k + 1) * HD]
        theirs[k] = out[cut:, k * HD : (k + 1) * HD]


PAIR = 2 * HALF


def first_body(sc, x0, x1, ada, w, mine, theirs, hidden, *, far):
    s = sc[8]
    i = s % 2
    for r, x in enumerate((x0, x1)):
        t = s ^ (r + far)
        level = level_of(sc, t, 0)
        for a in range(2):
            values = x[a * HALF : (a + 1) * HALF, :].astype(F32)
            to = pl.ds(pl.multiple_of(((i ^ a) * 2 + t % 2) * HALF, HALF), HALF)
            hidden[to, :] = modulated(values, ada, level)
    project(hidden, w, mine, theirs)


def second_body(
    sc, x0, x1, x2, x3, here, away, fresh, ada, w, w_pair,
    mine, other, vel, fin, theirs, hidden, vall,
):
    s = sc[8]
    i = s % 2
    step_size = 1.0 / (SLOTS * PER)
    half = pl.ds(pl.multiple_of(i * HALF, HALF), HALF)
    for k in range(2):
        vall[:, col_of(s ^ k)] = here[k]
        vall[:, col_of(s ^ (2 + k))] = away[k]
    first = first_slot(sc)
    for r, x in enumerate((x0, x1, x2, x3)):
        t = s ^ r
        level = level_of(sc, t, 1)
        where = row_of(0, t)
        moved = x[half, :].astype(F32) - vall[where, :].astype(F32) * step_size
        taken = jnp.where(t == first, fresh[half, :], moved.astype(BF))
        hidden[where, :] = modulated(taken.astype(F32), ada, level)
    for r, x in enumerate((x0, x1, x2, x3)):

        @pl.when(s ^ r == first)
        def _():
            def done(slot):
                drift = vall[row_of(0, s ^ r), col_of(slot)].astype(F32)
                return (x[half, col_of(slot)].astype(F32) - drift * step_size).astype(BF)

            fin[...] = done(s)
            theirs[:, WIDTH:] = done(s ^ 1)

    vel[...] = vall[row_of(0, s), :]
    theirs[:, :WIDTH] = vall[row_of(0, s ^ 1), :]
    for out, weights in ((mine, w), (other, w_pair)):
        product = jnp.dot(hidden[...], weights[...], preferred_element_type=F32).astype(BF)
        for k in range(out.shape[0]):
            out[k] = product[:, k * HD : (k + 1) * HD]


def projected_shapes(heads, rows):
    return [jax.ShapeDtypeStruct((heads, rows, HD), BF)] * 2


def first_projection(sc, xs, far, ada, w):
    def body(*refs):
        first_body(*refs, far=far)

    return pl.pallas_call(
        body,
        in_specs=[SM] + [VM] * 4,
        out_specs=[VM] * 2,
        out_shape=projected_shapes(w.shape[1] // HD, PAIR),
        scratch_shapes=[pltpu.VMEM((2 * PAIR, WIDTH), BF)],
        compiler_params=params(12),
        cost_estimate=pl.CostEstimate(flops=4 * 10**9, bytes_accessed=10**7, transcendentals=0),
        name="modulate_project",
    )(sc, *xs, ada, w)


def second_projection(sc, xs, here, away, fresh, ada, w, w_pair):
    return pl.pallas_call(
        second_body,
        in_specs=[SM] + [VM] * 10,
        out_specs=[VM] * 5,
        out_shape=projected_shapes(w.shape[1] // HD, ROWS)
        + [jax.ShapeDtypeStruct((HALF, n), BF) for n in (WIDTH, COLS, WIDTH + COLS)],
        scratch_shapes=[pltpu.VMEM((ROWS, WIDTH), BF)] * 2,
        compiler_params=params(14),
        cost_estimate=pl.CostEstimate(flops=4 * 10**9, bytes_accessed=10**7, transcendentals=0),
        name="advance_modulate_project",
    )(sc, *xs, here, away, fresh, ada, w, w_pair)


def pack_body(step, sc, *refs):
    parts, (out, chip) = refs[:-2], refs[-2:]
    i, h = sc[8] % 2, sc[8] // 2
    for k in range(2):
        to = pl.ds(10 * jnp.where(k == 0, i, 1 - i), 10)
        if step == 1:
            chip[to] = parts[k][...]
            continue
        for n in range(2):
            at = pl.multiple_of((h ^ n) * PAIR, PAIR)
            chip[to, pl.ds(at, PAIR)] = parts[2 * k + n][...]
    for g in range(8):
        out[g, 3] = chip[4 + g]
        out[g, 4] = chip[12 + g]

    def queries(low, high, at):
        for n in range(24):
            if low <= n < high:
                out[n // 3, n % 3] = chip[n - at]
            else:
                out[n // 3, n % 3] = jnp.zeros((ROWS, HD), BF)

    @pl.when(h == 0)
    def _():
        queries(0, 20, 0)

    @pl.when(h != 0)
    def _():
        queries(20, 24, 20)


def pack(step, sc, *parts):
    def body(*refs):
        pack_body(step, *refs)

    return pl.pallas_call(
        body,
        in_specs=[SM] + [VM] * len(parts),
        out_specs=VM,
        out_shape=jax.ShapeDtypeStruct((8, 5, ROWS, HD), BF),
        scratch_shapes=[pltpu.VMEM((20, ROWS, HD), BF)],
        compiler_params=params(8),
        name="pack_heads",
    )(sc, *parts)


QROWS = 4 * 3 * HALF


def attend_body(step, parts, chunk, block, last, sc, q, *refs):
    blocks, refs = refs[:parts], refs[parts:]
    if last:
        top_in, acc_in, out, qs, ks, vs = refs
    else:
        top_out, acc_out, qs, ks, vs = refs
    keys = ks.shape[0] // SLOTS
    ranks = [rank_of(sc, t, step) for t in range(SLOTS)]
    at = 0
    for ref in blocks:
        for b in range(ref.shape[0]):
            for j in range(SLOTS):
                rows = slice(j * HALF, (j + 1) * HALF)
                to = pl.ds(pl.multiple_of(ranks[j] * keys + at * HALF, HALF), HALF)
                ks[to, :] = ref[b, 0, rows, :]
                vs[to, :HD] = ref[b, 1, rows, :]
            at += 1
    vs[:, HD:] = jnp.ones((SLOTS * keys, HD), BF)
    factor = LOG2E / math.sqrt(HD)
    for c in range(4):
        for m in range(3):
            both = ((q[c, m].astype(F32) + q[4 + c, m].astype(F32)) * factor).astype(BF)
            for j in range(SLOTS):
                to = pl.ds(pl.multiple_of(ranks[j] * QROWS + (c * 3 + m) * HALF, HALF), HALF)
                qs[to, :] = both[j * HALF : (j + 1) * HALF]

    def scores_of(rank, r, n, size):
        return lax.dot_general(
            qs[rank * QROWS + r : rank * QROWS + r + block], ks[n : n + size, :],
            (((1,), (1,)), ((), ())), preferred_element_type=F32,
        )

    todo = []
    for rank in reversed(range(SLOTS)):
        for r in range(0, QROWS, block):
            span = (rank + 1) * keys
            todo += [(rank, r, n, min(chunk, span - n)) for n in range(0, span, chunk)]
    ahead = scores_of(*todo[0])
    for x, (rank, r, n, size) in enumerate(todo):
        scores = ahead
        rows = slice(r, r + block)
        if n == 0 and last:
            old, total = top_in[rank, rows], acc_in[rank, rows]
        if x + 1 < len(todo):
            ahead = scores_of(*todo[x + 1])
        new = jnp.max(scores, axis=-1, keepdims=True)
        fresh = n == 0 and not last
        new = jnp.broadcast_to(new, (block, HD)) if fresh else jnp.maximum(old, new)
        weights = jnp.exp2(scores - new[:, :1]).astype(BF)
        part = jnp.dot(weights, vs[n : n + size, :], preferred_element_type=F32)
        if fresh:
            total = part
        else:
            shrink = jnp.exp2(old - new)
            total = total * jnp.concatenate([shrink, shrink], axis=1) + part
        old = new
        if n + size < (rank + 1) * keys:
            continue
        if not last:
            top_out[rank, rows] = new
            acc_out[rank, rows] = total
            continue
        res = (total[:, :HD] / total[:, HD:]).astype(BF)
        slot = jnp.int32(0)
        for j in range(1, SLOTS):
            slot = jnp.where(ranks[j] == rank, j, slot)
        to = pl.ds(pl.multiple_of(slot * HALF, HALF), HALF)
        for k in range(block // HALF):
            c, m = divmod(r // HALF + k, 3)
            out[c, m, to, :] = res[k * HALF : (k + 1) * HALF]
            out[4 + c, m, to, :] = res[k * HALF : (k + 1) * HALF]


def attend(step, sc, q, blocks, chunk, block, state=None):
    last = state is not None
    keys = sum(b.shape[0] for b in blocks) * HALF

    def body(*refs):
        attend_body(step, len(blocks), chunk, block, last, *refs)

    scratch = [
        pltpu.VMEM((SLOTS * QROWS, HD), BF),
        pltpu.VMEM((SLOTS * keys, HD), BF),
        pltpu.VMEM((SLOTS * keys, 2 * HD), BF),
    ]
    if last:
        out_shape = jax.ShapeDtypeStruct((8, 3, ROWS, HD), BF)
    else:
        out_shape = [
            jax.ShapeDtypeStruct((SLOTS, QROWS, HD), F32),
            jax.ShapeDtypeStruct((SLOTS, QROWS, 2 * HD), F32),
        ]
    pairs = 10 * QROWS * keys
    return pl.pallas_call(
        body,
        in_specs=[SM] + [VM] * (1 + len(blocks) + (2 if last else 0)),
        out_specs=VM if last else [VM, VM],
        out_shape=out_shape,
        scratch_shapes=scratch,
        compiler_params=params(20 if last else 12),
        cost_estimate=pl.CostEstimate(
            flops=pairs * HD * 8, bytes_accessed=8 * 10**6, transcendentals=pairs
        ),
        name="span_attention_end" if last else "span_attention_begin",
    )(sc, q, *blocks, *(state or ()))


def out_body(step, sc, mine, ada, w, w_pair, out, attn):
    s = sc[8]
    for m in range(24):
        attn[:, m * HD : (m + 1) * HD] = mine[m // 3, m % 3]
    for k, weights in enumerate((w, w_pair)):
        product = jnp.dot(attn[...], weights[...], preferred_element_type=F32)
        for t in range(SLOTS):
            gate = ada[level_of(sc, t, step), 2:3, col_of(s ^ k)]
            piece = (product[t * HALF : (t + 1) * HALF] * gate).astype(BF)
            if step == 0:
                out[k, t * HALF : (t + 1) * HALF, :] = piece
            else:
                out[s ^ t, k] = piece


def out_projection(step, sc, mine, ada, w, w_pair):
    shape = (2, ROWS, COLS) if step == 0 else (SLOTS, 2, HALF, COLS)

    def body(*refs):
        out_body(step, *refs)

    return pl.pallas_call(
        body,
        in_specs=[SM] + [VM] * 4,
        out_specs=VM,
        out_shape=jax.ShapeDtypeStruct(shape, BF),
        scratch_shapes=[pltpu.VMEM((ROWS, WIDTH), BF)],
        compiler_params=params(10),
        cost_estimate=pl.CostEstimate(flops=2 * 10**9, bytes_accessed=6 * 10**6, transcendentals=0),
        name="out_projection",
    )(sc, mine, ada, w, w_pair)


def finish_body(sc, vel, fin, theirs, r0, r1, r2, r3, out, done):
    s = sc[8]
    i = s % 2
    halves = [pl.ds(pl.multiple_of((i ^ a) * HALF, HALF), HALF) for a in range(2)]
    out[0, halves[0], :] = vel[...]
    out[0, halves[1], :] = theirs[:, :WIDTH]
    done[halves[0], :] = fin[...]
    done[halves[1], :] = theirs[:, WIDTH:]
    for k, r in enumerate((r0, r1, r2, r3)):
        for c in range(2):
            out[1, halves[k % 2], col_of(s ^ k ^ c)] = r[c]


def finish(sc, vel, fin, theirs, rs):
    return pl.pallas_call(
        finish_body,
        in_specs=[SM] + [VM] * 7,
        out_specs=[VM, VM],
        out_shape=[
            jax.ShapeDtypeStruct((2, TOK, WIDTH), BF),
            jax.ShapeDtypeStruct((TOK, COLS), BF),
        ],
        compiler_params=params(8),
        name="collect_velocity",
    )(sc, vel, fin, theirs, *rs)


def begin_keys(low, high):
    low_y = move(low, y=2)
    high_z = [move(high, z=k) for k in (1, -1, 2)]
    early = jnp.concatenate([low, high, low_y, *high_z])
    lows = jnp.concatenate([low, low_y])
    highs = jnp.concatenate([high, *high_z])
    late = [move(lows, z=k) for k in (1, -1, 2)] + [move(highs, y=2)]
    return early, late


def both_cores(x):
    return [x, move(x, i=1)]


def after(x, *others):
    return lax.optimization_barrier((x, *others))


def shards(latents, fresh, span_ids, noise_step, ada_table, w_qkv, w_out):
    pos = lax.axis_index("slot").astype(jnp.int32).reshape(1)
    sc = jnp.concatenate([span_ids, noise_step, pos])
    own = latents[0]

    def beside(x, other):
        x, other = after(x, other)
        other = move(other, i=1)
        return after(exchange(x), other)

    def attention(step, got):
        early, late = begin_keys(got[4:6, 3:], got[6:, 3:])
        state = attend(step, sc, got, both_cores(early), 768, 384)
        late, state = after(late, state)
        late = jnp.concatenate(late)
        attn = attend(step, sc, got, both_cores(late), 1280, 384, state)
        return attn

    far = move(own, h=1)
    near = move(own, i=1)
    a = first_projection(sc, (own, near), 0, ada_table, w_qkv)
    far, a = after(far, a)
    far_near = move(far, i=1)
    b = first_projection(sc, (far, far_near), 2, ada_table, w_qkv)
    xs = (own, near, far, far_near)

    packed = pack(0, sc, a[0], b[0], move(a[1], i=1), move(b[1], i=1))
    got, w_out_pair = beside(packed, w_out)
    attn, w_pair = beside(attention(0, got), w_qkv)
    vel = out_projection(0, sc, attn, ada_table, w_out, w_out_pair)
    mine, other, vel, fin, theirs = second_projection(
        sc, xs, vel, move(vel, h=1), fresh, ada_table, w_qkv, w_pair
    )
    attn = attention(1, exchange(pack(1, sc, mine, other)))
    attn, theirs = after(exchange(attn), theirs)
    theirs = move(theirs, i=1)
    out = out_projection(1, sc, attn, ada_table, w_out, w_out_pair)
    rs = [out[0], move(out[1], i=1), move(out[2], h=1), move(out[3], h=1, i=1)]
    vel, fin = finish(sc, vel, fin, theirs, rs)
    return vel[:, None], fin


def solution(mesh):
    in_specs = (
        P("slot", "ctx", None),
        P("ctx", None),
        P(),
        P(),
        P(),
        P(None, "slot"),
        P(None, "slot"),
    )
    out_specs = (P(None, "slot", "ctx", None), P("ctx", "slot"))
    return jax.shard_map(shards, mesh=mesh, in_specs=in_specs, out_specs=out_specs, check_vma=False)
```

```python
import math

import jax
import jax.numpy as jnp
from jax import lax
from jax.experimental import pallas as pl
from jax.experimental.pallas import tpu as pltpu
from jax.sharding import PartitionSpec as P

HD = 128
EPS = 1e-06
BF = jnp.bfloat16
F32 = jnp.float32
AXES = ("slot", "ctx")
VM = pl.BlockSpec(memory_space=pltpu.VMEM)
SM = pl.BlockSpec(memory_space=pltpu.SMEM)
SLOTS = 4
PER = 2
TOK = 64
HALF = 32
ROWS = SLOTS * HALF
WIDTH = 3072
COLS = WIDTH // SLOTS
LOG2E = 1.4426950408889634


def where_is(flat):
    s, c = flat // 32, flat % 32
    return dict(h=s // 2, i=s % 2, z=c // 8, xl=(c // 4) % 2, y=c % 4)


def flat_of(d):
    return (d["h"] * 2 + d["i"]) * 32 + d["z"] * 8 + d["xl"] * 4 + d["y"]


def move(x, h=0, i=0, z=0, y=0):
    pairs = []
    for f in range(128):
        d = where_is(f)
        d["h"] = (d["h"] + h) % 2
        d["i"] = (d["i"] + i) % 2
        d["z"] = (d["z"] + z) % 4
        d["y"] = (d["y"] + y) % 4
        pairs.append((f, flat_of(d)))
    return lax.ppermute(x, AXES, pairs)


def group_lists():
    out = []
    for i in range(2):
        for z in range(4):
            for yh in range(2):
                out.append(
                    [
                        flat_of(dict(h=h, i=i, z=z, xl=xl, y=2 * yh + yl))
                        for h in range(2)
                        for xl in range(2)
                        for yl in range(2)
                    ]
                )
    return out


def exchange(x):
    return lax.all_to_all(x, AXES, 0, 0, tiled=True, axis_index_groups=group_lists())


def params(mib, **kw):
    return pltpu.CompilerParams(vmem_limit_bytes=mib * 1024 * 1024, **kw)


def first_slot(sc):
    best, at = sc[0], jnp.int32(0)
    for j in range(1, SLOTS):
        less = sc[j] < best
        best = jnp.where(less, sc[j], best)
        at = jnp.where(less, j, at)
    return at


def rank_of(sc, t, step):
    mine = sc[t]
    rank = jnp.int32(0)
    for j in range(SLOTS):
        rank = rank + (sc[j] < mine).astype(jnp.int32)
    if step == 0:
        return rank
    return jnp.where(rank == 0, SLOTS - 1, rank - 1)


def level_of(sc, t, step):
    rank = rank_of(sc, t, 0)
    level = PER * rank + sc[SLOTS + t] + 1
    if step == 0:
        return level
    return jnp.where(rank == 0, SLOTS * PER, level - 1)


def row_of(half, slot):
    return pl.ds(pl.multiple_of((half * SLOTS + slot) * HALF, HALF), HALF)


def col_of(slot, width=COLS):
    return pl.ds(pl.multiple_of(slot * width, 128), width)


def modulated(values, ada, level):
    center = jnp.mean(values, axis=-1, keepdims=True)
    off = values - center
    spread = jnp.mean(off * off, axis=-1, keepdims=True)
    normed = off * lax.rsqrt(spread + EPS)
    return (normed * (1.0 + ada[level, 1:2, :]) + ada[level, 0:1, :]).astype(BF)


def project(hidden, w, mine, theirs):
    out = jnp.dot(hidden[...], w[...], preferred_element_type=F32).astype(BF)
    cut = out.shape[0] // 2
    for k in range(mine.shape[0]):
        mine[k] = out[:cut, k * HD : (k + 1) * HD]
        theirs[k] = out[cut:, k * HD : (k + 1) * HD]


PAIR = 2 * HALF


def first_body(sc, x0, x1, ada, w, mine, theirs, hidden, *, far):
    s = sc[8]
    i = s % 2
    for r, x in enumerate((x0, x1)):
        t = s ^ (r + far)
        level = level_of(sc, t, 0)
        for a in range(2):
            values = x[a * HALF : (a + 1) * HALF, :].astype(F32)
            to = pl.ds(pl.multiple_of(((i ^ a) * 2 + t % 2) * HALF, HALF), HALF)
            hidden[to, :] = modulated(values, ada, level)
    project(hidden, w, mine, theirs)


def second_body(
    sc, x0, x1, x2, x3, here, away, fresh, ada, w, w_pair,
    mine, other, vel, fin, theirs, hidden, vall,
):
    s = sc[8]
    i = s % 2
    step_size = 1.0 / (SLOTS * PER)
    half = pl.ds(pl.multiple_of(i * HALF, HALF), HALF)
    for k in range(2):
        vall[:, col_of(s ^ k)] = here[k]
        vall[:, col_of(s ^ (2 + k))] = away[k]
    first = first_slot(sc)
    for r, x in enumerate((x0, x1, x2, x3)):
        t = s ^ r
        level = level_of(sc, t, 1)
        where = row_of(0, t)
        moved = x[half, :].astype(F32) - vall[where, :].astype(F32) * step_size
        taken = jnp.where(t == first, fresh[half, :], moved.astype(BF))
        hidden[where, :] = modulated(taken.astype(F32), ada, level)
    for r, x in enumerate((x0, x1, x2, x3)):

        @pl.when(s ^ r == first)
        def _():
            def done(slot):
                drift = vall[row_of(0, s ^ r), col_of(slot)].astype(F32)
                return (x[half, col_of(slot)].astype(F32) - drift * step_size).astype(BF)

            fin[...] = done(s)
            theirs[:, WIDTH:] = done(s ^ 1)

    vel[...] = vall[row_of(0, s), :]
    theirs[:, :WIDTH] = vall[row_of(0, s ^ 1), :]
    for out, weights in ((mine, w), (other, w_pair)):
        product = jnp.dot(hidden[...], weights[...], preferred_element_type=F32).astype(BF)
        for k in range(out.shape[0]):
            out[k] = product[:, k * HD : (k + 1) * HD]


def projected_shapes(heads, rows):
    return [jax.ShapeDtypeStruct((heads, rows, HD), BF)] * 2


def first_projection(sc, xs, far, ada, w):
    def body(*refs):
        first_body(*refs, far=far)

    return pl.pallas_call(
        body,
        in_specs=[SM] + [VM] * 4,
        out_specs=[VM] * 2,
        out_shape=projected_shapes(w.shape[1] // HD, PAIR),
        scratch_shapes=[pltpu.VMEM((2 * PAIR, WIDTH), BF)],
        compiler_params=params(12),
        cost_estimate=pl.CostEstimate(flops=4 * 10**9, bytes_accessed=10**7, transcendentals=0),
        name="modulate_project",
    )(sc, *xs, ada, w)


def second_projection(sc, xs, here, away, fresh, ada, w, w_pair):
    return pl.pallas_call(
        second_body,
        in_specs=[SM] + [VM] * 10,
        out_specs=[VM] * 5,
        out_shape=projected_shapes(w.shape[1] // HD, ROWS)
        + [jax.ShapeDtypeStruct((HALF, n), BF) for n in (WIDTH, COLS, WIDTH + COLS)],
        scratch_shapes=[pltpu.VMEM((ROWS, WIDTH), BF)] * 2,
        compiler_params=params(14),
        cost_estimate=pl.CostEstimate(flops=4 * 10**9, bytes_accessed=10**7, transcendentals=0),
        name="advance_modulate_project",
    )(sc, *xs, here, away, fresh, ada, w, w_pair)


def pack_body(step, sc, *refs):
    parts, (out, chip) = refs[:-2], refs[-2:]
    i, h = sc[8] % 2, sc[8] // 2
    for k in range(2):
        to = pl.ds(10 * jnp.where(k == 0, i, 1 - i), 10)
        if step == 1:
            chip[to] = parts[k][...]
            continue
        for n in range(2):
            at = pl.multiple_of((h ^ n) * PAIR, PAIR)
            chip[to, pl.ds(at, PAIR)] = parts[2 * k + n][...]
    for g in range(8):
        out[g, 3] = chip[4 + g]
        out[g, 4] = chip[12 + g]

    def queries(low, high, at):
        for n in range(24):
            if low <= n < high:
                out[n // 3, n % 3] = chip[n - at]
            else:
                out[n // 3, n % 3] = jnp.zeros((ROWS, HD), BF)

    @pl.when(h == 0)
    def _():
        queries(0, 20, 0)

    @pl.when(h != 0)
    def _():
        queries(20, 24, 20)


def pack(step, sc, *parts):
    def body(*refs):
        pack_body(step, *refs)

    return pl.pallas_call(
        body,
        in_specs=[SM] + [VM] * len(parts),
        out_specs=VM,
        out_shape=jax.ShapeDtypeStruct((8, 5, ROWS, HD), BF),
        scratch_shapes=[pltpu.VMEM((20, ROWS, HD), BF)],
        compiler_params=params(8),
        name="pack_heads",
    )(sc, *parts)


QROWS = 4 * 3 * HALF


def attend_body(step, parts, chunk, block, last, sc, q, *refs):
    blocks, refs = refs[:parts], refs[parts:]
    if last:
        top_in, acc_in, out, qs, ks, vs = refs
    else:
        top_out, acc_out, qs, ks, vs = refs
    keys = ks.shape[0] // SLOTS
    ranks = [rank_of(sc, t, step) for t in range(SLOTS)]
    at = 0
    for ref in blocks:
        for b in range(ref.shape[0]):
            for j in range(SLOTS):
                rows = slice(j * HALF, (j + 1) * HALF)
                to = pl.ds(pl.multiple_of(ranks[j] * keys + at * HALF, HALF), HALF)
                ks[to, :] = ref[b, 0, rows, :]
                vs[to, :HD] = ref[b, 1, rows, :]
            at += 1
    vs[:, HD:] = jnp.ones((SLOTS * keys, HD), BF)
    factor = LOG2E / math.sqrt(HD)
    for c in range(4):
        for m in range(3):
            both = ((q[c, m].astype(F32) + q[4 + c, m].astype(F32)) * factor).astype(BF)
            for j in range(SLOTS):
                to = pl.ds(pl.multiple_of(ranks[j] * QROWS + (c * 3 + m) * HALF, HALF), HALF)
                qs[to, :] = both[j * HALF : (j + 1) * HALF]

    def some_rows(index, _):
        r = pl.multiple_of(index * block, block)
        rows = pl.ds(r, block)

        def scores_of(rank, n, size):
            return lax.dot_general(
                qs[pl.ds(rank * QROWS + r, block), :], ks[n : n + size, :],
                (((1,), (1,)), ((), ())), preferred_element_type=F32,
            )

        todo = []
        for rank in reversed(range(SLOTS)):
            span = (rank + 1) * keys
            todo += [(rank, n, min(chunk, span - n)) for n in range(0, span, chunk)]
        ahead = scores_of(*todo[0])
        for x, (rank, n, size) in enumerate(todo):
            scores = ahead
            if n == 0 and last:
                old, total = top_in[rank, rows], acc_in[rank, rows]
            if x + 1 < len(todo):
                ahead = scores_of(*todo[x + 1])
            new = jnp.max(scores, axis=-1, keepdims=True)
            fresh = n == 0 and not last
            new = jnp.broadcast_to(new, (block, HD)) if fresh else jnp.maximum(old, new)
            weights = jnp.exp2(scores - new[:, :1]).astype(BF)
            part = jnp.dot(weights, vs[n : n + size, :], preferred_element_type=F32)
            if fresh:
                total = part
            else:
                shrink = jnp.exp2(old - new)
                total = total * jnp.concatenate([shrink, shrink], axis=1) + part
            old = new
            if n + size < (rank + 1) * keys:
                continue
            if not last:
                top_out[rank, rows] = new
                acc_out[rank, rows] = total
                continue
            res = (total[:, :HD] / total[:, HD:]).astype(BF)
            slot = jnp.int32(0)
            for j in range(1, SLOTS):
                slot = jnp.where(ranks[j] == rank, j, slot)
            to = pl.ds(pl.multiple_of(slot * HALF, HALF), HALF)
            for k in range(block // HALF):
                head = index * (block // HALF) + k
                out[head, to, :] = res[k * HALF : (k + 1) * HALF]
                out[12 + head, to, :] = res[k * HALF : (k + 1) * HALF]
        return 0

    lax.fori_loop(0, QROWS // block, some_rows, 0)


def attend(step, sc, q, blocks, chunk, block, state=None):
    last = state is not None
    keys = sum(b.shape[0] for b in blocks) * HALF

    def body(*refs):
        attend_body(step, len(blocks), chunk, block, last, *refs)

    scratch = [
        pltpu.VMEM((SLOTS * QROWS, HD), BF),
        pltpu.VMEM((SLOTS * keys, HD), BF),
        pltpu.VMEM((SLOTS * keys, 2 * HD), BF),
    ]
    if last:
        out_shape = jax.ShapeDtypeStruct((24, ROWS, HD), BF)
    else:
        out_shape = [
            jax.ShapeDtypeStruct((SLOTS, QROWS, HD), F32),
            jax.ShapeDtypeStruct((SLOTS, QROWS, 2 * HD), F32),
        ]
    pairs = 10 * QROWS * keys
    return pl.pallas_call(
        body,
        in_specs=[SM] + [VM] * (1 + len(blocks) + (2 if last else 0)),
        out_specs=VM if last else [VM, VM],
        out_shape=out_shape,
        scratch_shapes=scratch,
        compiler_params=params(20 if last else 12),
        cost_estimate=pl.CostEstimate(
            flops=pairs * HD * 8, bytes_accessed=8 * 10**6, transcendentals=pairs
        ),
        name="span_attention_end" if last else "span_attention_begin",
    )(sc, q, *blocks, *(state or ()))


def out_body(step, sc, mine, ada, w, w_pair, out, attn):
    s = sc[8]
    for m in range(24):
        attn[:, m * HD : (m + 1) * HD] = mine[m // 3, m % 3]
    for k, weights in enumerate((w, w_pair)):
        product = jnp.dot(attn[...], weights[...], preferred_element_type=F32)
        for t in range(SLOTS):
            gate = ada[level_of(sc, t, step), 2:3, col_of(s ^ k)]
            piece = (product[t * HALF : (t + 1) * HALF] * gate).astype(BF)
            if step == 0:
                out[k, t * HALF : (t + 1) * HALF, :] = piece
            else:
                out[s ^ t, k] = piece


def out_projection(step, sc, mine, ada, w, w_pair):
    shape = (2, ROWS, COLS) if step == 0 else (SLOTS, 2, HALF, COLS)

    def body(*refs):
        out_body(step, *refs)

    return pl.pallas_call(
        body,
        in_specs=[SM] + [VM] * 4,
        out_specs=VM,
        out_shape=jax.ShapeDtypeStruct(shape, BF),
        scratch_shapes=[pltpu.VMEM((ROWS, WIDTH), BF)],
        compiler_params=params(10),
        cost_estimate=pl.CostEstimate(flops=2 * 10**9, bytes_accessed=6 * 10**6, transcendentals=0),
        name="out_projection",
    )(sc, mine, ada, w, w_pair)


def finish_body(sc, vel, fin, theirs, r0, r1, r2, r3, out, done):
    s = sc[8]
    i = s % 2
    halves = [pl.ds(pl.multiple_of((i ^ a) * HALF, HALF), HALF) for a in range(2)]
    out[0, halves[0], :] = vel[...]
    out[0, halves[1], :] = theirs[:, :WIDTH]
    done[halves[0], :] = fin[...]
    done[halves[1], :] = theirs[:, WIDTH:]
    for k, r in enumerate((r0, r1, r2, r3)):
        for c in range(2):
            out[1, halves[k % 2], col_of(s ^ k ^ c)] = r[c]


def finish(sc, vel, fin, theirs, rs):
    return pl.pallas_call(
        finish_body,
        in_specs=[SM] + [VM] * 7,
        out_specs=[VM, VM],
        out_shape=[
            jax.ShapeDtypeStruct((2, TOK, WIDTH), BF),
            jax.ShapeDtypeStruct((TOK, COLS), BF),
        ],
        compiler_params=params(8),
        name="collect_velocity",
    )(sc, vel, fin, theirs, *rs)


def begin_keys(low, high):
    low_y = move(low, y=2)
    high_z = [move(high, z=k) for k in (1, -1, 2)]
    early = jnp.concatenate([low, high, low_y, *high_z])
    lows = jnp.concatenate([low, low_y])
    highs = jnp.concatenate([high, *high_z])
    late = [move(lows, z=k) for k in (1, -1, 2)] + [move(highs, y=2)]
    return early, late


def both_cores(x):
    return [x, move(x, i=1)]


def after(x, *others):
    return lax.optimization_barrier((x, *others))


def shards(latents, fresh, span_ids, noise_step, ada_table, w_qkv, w_out):
    pos = lax.axis_index("slot").astype(jnp.int32).reshape(1)
    sc = jnp.concatenate([span_ids, noise_step, pos])
    own = latents[0]

    def beside(x, other):
        x, other = after(x, other)
        other = move(other, i=1)
        return after(exchange(x), other)

    def attention(step, got):
        early, late = begin_keys(got[4:6, 3:], got[6:, 3:])
        state = attend(step, sc, got, both_cores(early), 768, 192)
        late, state = after(late, state)
        late = jnp.concatenate(late)
        attn = attend(step, sc, got, both_cores(late), 1280, 192, state)
        return attn.reshape(8, 3, ROWS, HD)

    far = move(own, h=1)
    near = move(own, i=1)
    a = first_projection(sc, (own, near), 0, ada_table, w_qkv)
    far, a = after(far, a)
    far_near = move(far, i=1)
    b = first_projection(sc, (far, far_near), 2, ada_table, w_qkv)
    xs = (own, near, far, far_near)

    packed = pack(0, sc, a[0], b[0], move(a[1], i=1), move(b[1], i=1))
    got, w_out_pair = beside(packed, w_out)
    attn, w_pair = beside(attention(0, got), w_qkv)
    vel = out_projection(0, sc, attn, ada_table, w_out, w_out_pair)
    mine, other, vel, fin, theirs = second_projection(
        sc, xs, vel, move(vel, h=1), fresh, ada_table, w_qkv, w_pair
    )
    attn = attention(1, exchange(pack(1, sc, mine, other)))
    attn, theirs = after(exchange(attn), theirs)
    theirs = move(theirs, i=1)
    out = out_projection(1, sc, attn, ada_table, w_out, w_out_pair)
    rs = [out[0], move(out[1], i=1), move(out[2], h=1), move(out[3], h=1, i=1)]
    vel, fin = finish(sc, vel, fin, theirs, rs)
    return vel[:, None], fin


def solution(mesh):
    in_specs = (
        P("slot", "ctx", None),
        P("ctx", None),
        P(),
        P(),
        P(),
        P(None, "slot"),
        P(None, "slot"),
    )
    out_specs = (P(None, "slot", "ctx", None), P("ctx", "slot"))
    return jax.shard_map(shards, mesh=mesh, in_specs=in_specs, out_specs=out_specs, check_vma=False)
```

```python
import math

import jax
import jax.numpy as jnp
from jax import lax
from jax.experimental import pallas as pl
from jax.experimental.pallas import tpu as pltpu
from jax.sharding import PartitionSpec as P

HD = 128
EPS = 1e-06
BF = jnp.bfloat16
F32 = jnp.float32
AXES = ("slot", "ctx")
VM = pl.BlockSpec(memory_space=pltpu.VMEM)
SM = pl.BlockSpec(memory_space=pltpu.SMEM)
SLOTS = 4
PER = 2
TOK = 64
HALF = 32
ROWS = SLOTS * HALF
WIDTH = 3072
COLS = WIDTH // SLOTS
LOG2E = 1.4426950408889634


def where_is(flat):
    s, c = flat // 32, flat % 32
    return dict(h=s // 2, i=s % 2, z=c // 8, xl=(c // 4) % 2, y=c % 4)


def flat_of(d):
    return (d["h"] * 2 + d["i"]) * 32 + d["z"] * 8 + d["xl"] * 4 + d["y"]


def move(x, h=0, i=0, z=0, y=0):
    pairs = []
    for f in range(128):
        d = where_is(f)
        d["h"] = (d["h"] + h) % 2
        d["i"] = (d["i"] + i) % 2
        d["z"] = (d["z"] + z) % 4
        d["y"] = (d["y"] + y) % 4
        pairs.append((f, flat_of(d)))
    return lax.ppermute(x, AXES, pairs)


def group_lists():
    out = []
    for i in range(2):
        for z in range(4):
            for yh in range(2):
                out.append(
                    [
                        flat_of(dict(h=h, i=i, z=z, xl=xl, y=2 * yh + yl))
                        for h in range(2)
                        for xl in range(2)
                        for yl in range(2)
                    ]
                )
    return out


def exchange(x):
    return lax.all_to_all(x, AXES, 0, 0, tiled=True, axis_index_groups=group_lists())


def params(mib, **kw):
    return pltpu.CompilerParams(vmem_limit_bytes=mib * 1024 * 1024, **kw)


def first_slot(sc):
    best, at = sc[0], jnp.int32(0)
    for j in range(1, SLOTS):
        less = sc[j] < best
        best = jnp.where(less, sc[j], best)
        at = jnp.where(less, j, at)
    return at


def rank_of(sc, t, step):
    mine = sc[t]
    rank = jnp.int32(0)
    for j in range(SLOTS):
        rank = rank + (sc[j] < mine).astype(jnp.int32)
    if step == 0:
        return rank
    return jnp.where(rank == 0, SLOTS - 1, rank - 1)


def level_of(sc, t, step):
    rank = rank_of(sc, t, 0)
    level = PER * rank + sc[SLOTS + t] + 1
    if step == 0:
        return level
    return jnp.where(rank == 0, SLOTS * PER, level - 1)


def row_of(half, slot):
    return pl.ds(pl.multiple_of((half * SLOTS + slot) * HALF, HALF), HALF)


def col_of(slot, width=COLS):
    return pl.ds(pl.multiple_of(slot * width, 128), width)


def modulated(values, ada, level):
    center = jnp.mean(values, axis=-1, keepdims=True)
    off = values - center
    spread = jnp.mean(off * off, axis=-1, keepdims=True)
    normed = off * lax.rsqrt(spread + EPS)
    return (normed * (1.0 + ada[level, 1:2, :]) + ada[level, 0:1, :]).astype(BF)


def project(hidden, w, mine, theirs):
    out = jnp.dot(hidden[...], w[...], preferred_element_type=F32).astype(BF)
    cut = out.shape[0] // 2
    for k in range(mine.shape[0]):
        mine[k] = out[:cut, k * HD : (k + 1) * HD]
        theirs[k] = out[cut:, k * HD : (k + 1) * HD]


PAIR = 2 * HALF


def first_body(sc, x0, x1, ada, w, mine, theirs, hidden, *, far):
    s = sc[8]
    i = s % 2
    for r, x in enumerate((x0, x1)):
        t = s ^ (r + far)
        level = level_of(sc, t, 0)
        for a in range(2):
            values = x[a * HALF : (a + 1) * HALF, :].astype(F32)
            to = pl.ds(pl.multiple_of(((i ^ a) * 2 + t % 2) * HALF, HALF), HALF)
            hidden[to, :] = modulated(values, ada, level)
    project(hidden, w, mine, theirs)


def second_body(
    sc, x0, x1, x2, x3, here, away, fresh, ada, w, w_pair,
    mine, other, vel, fin, theirs, hidden, vall,
):
    s = sc[8]
    i = s % 2
    step_size = 1.0 / (SLOTS * PER)
    half = pl.ds(pl.multiple_of(i * HALF, HALF), HALF)
    for k in range(2):
        vall[:, col_of(s ^ k)] = here[k]
        vall[:, col_of(s ^ (2 + k))] = away[k]
    first = first_slot(sc)
    for r, x in enumerate((x0, x1, x2, x3)):
        t = s ^ r
        level = level_of(sc, t, 1)
        where = row_of(0, t)
        moved = x[half, :].astype(F32) - vall[where, :].astype(F32) * step_size
        taken = jnp.where(t == first, fresh[half, :], moved.astype(BF))
        hidden[where, :] = modulated(taken.astype(F32), ada, level)
    for r, x in enumerate((x0, x1, x2, x3)):

        @pl.when(s ^ r == first)
        def _():
            def done(slot):
                drift = vall[row_of(0, s ^ r), col_of(slot)].astype(F32)
                return (x[half, col_of(slot)].astype(F32) - drift * step_size).astype(BF)

            fin[...] = done(s)
            theirs[:, WIDTH:] = done(s ^ 1)

    vel[...] = vall[row_of(0, s), :]
    theirs[:, :WIDTH] = vall[row_of(0, s ^ 1), :]
    for out, weights in ((mine, w), (other, w_pair)):
        product = jnp.dot(hidden[...], weights[...], preferred_element_type=F32).astype(BF)
        for k in range(out.shape[0]):
            out[k] = product[:, k * HD : (k + 1) * HD]


def projected_shapes(heads, rows):
    return [jax.ShapeDtypeStruct((heads, rows, HD), BF)] * 2


def first_projection(sc, xs, far, ada, w):
    def body(*refs):
        first_body(*refs, far=far)

    return pl.pallas_call(
        body,
        in_specs=[SM] + [VM] * 4,
        out_specs=[VM] * 2,
        out_shape=projected_shapes(w.shape[1] // HD, PAIR),
        scratch_shapes=[pltpu.VMEM((2 * PAIR, WIDTH), BF)],
        compiler_params=params(12),
        cost_estimate=pl.CostEstimate(flops=4 * 10**9, bytes_accessed=10**7, transcendentals=0),
        name="modulate_project",
    )(sc, *xs, ada, w)


def second_projection(sc, xs, here, away, fresh, ada, w, w_pair):
    return pl.pallas_call(
        second_body,
        in_specs=[SM] + [VM] * 10,
        out_specs=[VM] * 5,
        out_shape=projected_shapes(w.shape[1] // HD, ROWS)
        + [jax.ShapeDtypeStruct((HALF, n), BF) for n in (WIDTH, COLS, WIDTH + COLS)],
        scratch_shapes=[pltpu.VMEM((ROWS, WIDTH), BF)] * 2,
        compiler_params=params(14),
        cost_estimate=pl.CostEstimate(flops=4 * 10**9, bytes_accessed=10**7, transcendentals=0),
        name="advance_modulate_project",
    )(sc, *xs, here, away, fresh, ada, w, w_pair)


def pack_body(step, sc, *refs):
    parts, (out, last, chip) = refs[:-3], refs[-3:]
    i, h = sc[8] % 2, sc[8] // 2
    for k in range(2):
        to = pl.ds(10 * jnp.where(k == 0, i, 1 - i), 10)
        if step == 1:
            chip[to] = parts[k][...]
            continue
        for n in range(2):
            at = pl.multiple_of((h ^ n) * PAIR, PAIR)
            chip[to, pl.ds(at, PAIR)] = parts[2 * k + n][...]
    nothing = jnp.zeros((ROWS, HD), BF)
    last[0] = chip[11]
    last[1] = chip[19]

    @pl.when(h == 0)
    def _():
        for n in range(24):
            out[n // 3, n % 3] = chip[n] if n < 20 else nothing

    @pl.when(h != 0)
    def _():
        for g in range(7):
            out[g, 0] = chip[4 + g]
            out[g, 1] = chip[12 + g]
            out[g, 2] = chip[0] if g == 6 else nothing
        for m in range(3):
            out[7, m] = chip[1 + m]


def pack(step, sc, *parts):
    def body(*refs):
        pack_body(step, *refs)

    return pl.pallas_call(
        body,
        in_specs=[SM] + [VM] * len(parts),
        out_specs=[VM, VM],
        out_shape=[
            jax.ShapeDtypeStruct((8, 3, ROWS, HD), BF),
            jax.ShapeDtypeStruct((2, ROWS, HD), BF),
        ],
        scratch_shapes=[pltpu.VMEM((20, ROWS, HD), BF)],
        compiler_params=params(8),
        name="pack_heads",
    )(sc, *parts)


QROWS = 4 * 3 * HALF


def attend_body(step, parts, chunk, block, last, sc, q, *refs):
    blocks, refs = refs[:parts], refs[parts:]
    if last:
        top_in, acc_in, out, qs, ks, vs = refs
    else:
        top_out, acc_out, qs, ks, vs = refs
    keys = ks.shape[0] // SLOTS
    ranks = [rank_of(sc, t, step) for t in range(SLOTS)]
    at = 0
    for ref in blocks:
        for b in range(ref.shape[0]):
            for j in range(SLOTS):
                rows = slice(j * HALF, (j + 1) * HALF)
                to = pl.ds(pl.multiple_of(ranks[j] * keys + at * HALF, HALF), HALF)
                ks[to, :] = ref[b, 0, rows, :]
                vs[to, :HD] = ref[b, 1, rows, :]
            at += 1
    vs[:, HD:] = jnp.ones((SLOTS * keys, HD), BF)
    factor = LOG2E / math.sqrt(HD)
    for c in range(4):
        for m in range(3):
            near = q[c, m].astype(F32)
            other = q[4 + c, m].astype(F32)
            if m == 2:
                near = near + other
            both = (jnp.where(sc[9] == 7, other, near) * factor).astype(BF)
            for j in range(SLOTS):
                to = pl.ds(pl.multiple_of(ranks[j] * QROWS + (c * 3 + m) * HALF, HALF), HALF)
                qs[to, :] = both[j * HALF : (j + 1) * HALF]

    def some_rows(index, _):
        r = pl.multiple_of(index * block, block)
        rows = pl.ds(r, block)

        def scores_of(rank, n, size):
            return lax.dot_general(
                qs[pl.ds(rank * QROWS + r, block), :], ks[n : n + size, :],
                (((1,), (1,)), ((), ())), preferred_element_type=F32,
            )

        todo = []
        for rank in reversed(range(SLOTS)):
            span = (rank + 1) * keys
            todo += [(rank, n, min(chunk, span - n)) for n in range(0, span, chunk)]
        ahead = scores_of(*todo[0])
        for x, (rank, n, size) in enumerate(todo):
            scores = ahead
            if n == 0 and last:
                old, total = top_in[rank, rows], acc_in[rank, rows]
            if x + 1 < len(todo):
                ahead = scores_of(*todo[x + 1])
            new = jnp.max(scores, axis=-1, keepdims=True)
            fresh = n == 0 and not last
            new = jnp.broadcast_to(new, (block, HD)) if fresh else jnp.maximum(old, new)
            weights = jnp.exp2(scores - new[:, :1]).astype(BF)
            part = jnp.dot(weights, vs[n : n + size, :], preferred_element_type=F32)
            if fresh:
                total = part
            else:
                shrink = jnp.exp2(old - new)
                total = total * jnp.concatenate([shrink, shrink], axis=1) + part
            old = new
            if n + size < (rank + 1) * keys:
                continue
            if not last:
                top_out[rank, rows] = new
                acc_out[rank, rows] = total
                continue
            res = (total[:, :HD] / total[:, HD:]).astype(BF)
            slot = jnp.int32(0)
            for j in range(1, SLOTS):
                slot = jnp.where(ranks[j] == rank, j, slot)
            to = pl.ds(pl.multiple_of(slot * HALF, HALF), HALF)
            for k in range(block // HALF):
                head = index * (block // HALF) + k
                out[head, to, :] = res[k * HALF : (k + 1) * HALF]
                out[12 + head, to, :] = res[k * HALF : (k + 1) * HALF]
        return 0

    lax.fori_loop(0, QROWS // block, some_rows, 0)


def attend(step, sc, q, blocks, chunk, block, state=None):
    last = state is not None
    keys = sum(b.shape[0] for b in blocks) * HALF

    def body(*refs):
        attend_body(step, len(blocks), chunk, block, last, *refs)

    scratch = [
        pltpu.VMEM((SLOTS * QROWS, HD), BF),
        pltpu.VMEM((SLOTS * keys, HD), BF),
        pltpu.VMEM((SLOTS * keys, 2 * HD), BF),
    ]
    if last:
        out_shape = jax.ShapeDtypeStruct((24, ROWS, HD), BF)
    else:
        out_shape = [
            jax.ShapeDtypeStruct((SLOTS, QROWS, HD), F32),
            jax.ShapeDtypeStruct((SLOTS, QROWS, 2 * HD), F32),
        ]
    pairs = 10 * QROWS * keys
    return pl.pallas_call(
        body,
        in_specs=[SM] + [VM] * (1 + len(blocks) + (2 if last else 0)),
        out_specs=VM if last else [VM, VM],
        out_shape=out_shape,
        scratch_shapes=scratch,
        compiler_params=params(20 if last else 12),
        cost_estimate=pl.CostEstimate(
            flops=pairs * HD * 8, bytes_accessed=8 * 10**6, transcendentals=pairs
        ),
        name="span_attention_end" if last else "span_attention_begin",
    )(sc, q, *blocks, *(state or ()))


def out_body(step, sc, mine, ada, w, w_pair, out, attn):
    s = sc[8]
    for m in range(24):
        attn[:, m * HD : (m + 1) * HD] = mine[m // 3, m % 3]
    for k, weights in enumerate((w, w_pair)):
        product = jnp.dot(attn[...], weights[...], preferred_element_type=F32)
        for t in range(SLOTS):
            gate = ada[level_of(sc, t, step), 2:3, col_of(s ^ k)]
            piece = (product[t * HALF : (t + 1) * HALF] * gate).astype(BF)
            if step == 0:
                out[k, t * HALF : (t + 1) * HALF, :] = piece
            else:
                out[s ^ t, k] = piece


def out_projection(step, sc, mine, ada, w, w_pair):
    shape = (2, ROWS, COLS) if step == 0 else (SLOTS, 2, HALF, COLS)

    def body(*refs):
        out_body(step, *refs)

    return pl.pallas_call(
        body,
        in_specs=[SM] + [VM] * 4,
        out_specs=VM,
        out_shape=jax.ShapeDtypeStruct(shape, BF),
        scratch_shapes=[pltpu.VMEM((ROWS, WIDTH), BF)],
        compiler_params=params(10),
        cost_estimate=pl.CostEstimate(flops=2 * 10**9, bytes_accessed=6 * 10**6, transcendentals=0),
        name="out_projection",
    )(sc, mine, ada, w, w_pair)


def hold(w):
    def body(x, y, sem):
        copy = pltpu.make_async_copy(x, y, sem)
        copy.start()
        copy.wait()

    return pl.pallas_call(
        body,
        in_specs=[pl.BlockSpec(memory_space=pl.ANY)],
        out_specs=VM,
        out_shape=jax.ShapeDtypeStruct(w.shape, w.dtype),
        scratch_shapes=[pltpu.SemaphoreType.DMA(())],
        compiler_params=params(6),
        name="hold_weights",
    )(w)


def finish_body(sc, vel, fin, theirs, r0, r1, r2, r3, out, done):
    s = sc[8]
    i = s % 2
    halves = [pl.ds(pl.multiple_of((i ^ a) * HALF, HALF), HALF) for a in range(2)]
    out[0, halves[0], :] = vel[...]
    out[0, halves[1], :] = theirs[:, :WIDTH]
    done[halves[0], :] = fin[...]
    done[halves[1], :] = theirs[:, WIDTH:]
    for k, r in enumerate((r0, r1, r2, r3)):
        for c in range(2):
            out[1, halves[k % 2], col_of(s ^ k ^ c)] = r[c]


def finish(sc, vel, fin, theirs, rs):
    return pl.pallas_call(
        finish_body,
        in_specs=[SM] + [VM] * 7,
        out_specs=[VM, VM],
        out_shape=[
            jax.ShapeDtypeStruct((2, TOK, WIDTH), BF),
            jax.ShapeDtypeStruct((TOK, COLS), BF),
        ],
        compiler_params=params(8),
        name="collect_velocity",
    )(sc, vel, fin, theirs, *rs)


def seventh(x):
    out = []
    for xl, yl in ((0, 0), (0, 1), (1, 0)):
        pairs = []
        for f in range(128):
            d = where_is(f)
            if (d["h"], d["xl"], d["y"] % 2) == (1, xl, yl):
                pairs.append((f, flat_of(dict(d, xl=1, y=d["y"] // 2 * 2 + 1))))
        out.append(lax.ppermute(x, AXES, pairs))
    return out


def begin_keys(low, high):
    low_y = move(low, y=2)
    high_z = [move(high, z=k) for k in (1, -1, 2)]
    early = jnp.concatenate([low, high, low_y, *high_z])
    lows = jnp.concatenate([low, low_y])
    highs = jnp.concatenate([high, *high_z])
    late = [move(lows, z=k) for k in (1, -1, 2)] + [move(highs, y=2)]
    return early, late


def both_cores(x):
    return [x, move(x, i=1)]


def after(x, *others):
    return lax.optimization_barrier((x, *others))


def shards(latents, fresh, span_ids, noise_step, ada_table, w_qkv, w_out):
    pos = lax.axis_index("slot").astype(jnp.int32).reshape(1)
    ctx = lax.axis_index("ctx").astype(jnp.int32).reshape(1)
    group = 4 * (pos // 2) + ctx // 4 % 2 * 2 + ctx % 2
    sc = jnp.concatenate([span_ids, noise_step, pos, group])
    own = latents[0]

    def beside(x, *others):
        return after(exchange(x), *others)

    def attention(step, got, last, weights):
        keys = jnp.where(group[0] == 7, jnp.stack(last), got[4:, :2])
        early, late = begin_keys(keys[:2], keys[2:])
        state = attend(step, sc, got, both_cores(early), 768, 192)
        state, weights = after(state, weights)
        weights = [hold(w) for w in weights]
        late, state, weights = after(late, state, weights)
        late = jnp.concatenate(late)
        attn = attend(step, sc, got, both_cores(late), 1280, 192, state)
        return attn.reshape(8, 3, ROWS, HD), weights

    far = move(own, h=1)
    near = move(own, i=1)
    a = first_projection(sc, (own, near), 0, ada_table, w_qkv)
    far, a = after(far, a)
    far_near = move(far, i=1)
    b = first_projection(sc, (far, far_near), 2, ada_table, w_qkv)
    xs = (own, near, far, far_near)

    packed, last = pack(0, sc, a[0], b[0], move(a[1], i=1), move(b[1], i=1))
    packed, last, w_out_pair = after(packed, last, w_out)
    got, w_out_pair, *others = beside(packed, move(w_out_pair, i=1), *seventh(last))
    attn, held = attention(0, got, [*others, last], [w_out, w_out_pair])
    attn, w_pair = after(attn, w_qkv)
    attn, w_pair = beside(attn, move(w_pair, i=1))
    vel = out_projection(0, sc, attn, ada_table, *held)
    mine, other, vel, fin, theirs = second_projection(
        sc, xs, vel, move(vel, h=1), fresh, ada_table, w_qkv, w_pair
    )
    packed, last = pack(1, sc, mine, other)
    got, *others = beside(packed, *seventh(last))
    attn, held = attention(1, got, [*others, last], [w_out, w_out_pair])
    attn, theirs = after(exchange(attn), theirs)
    theirs = move(theirs, i=1)
    out = out_projection(1, sc, attn, ada_table, *held)
    rs = [out[0], move(out[1], i=1), move(out[2], h=1), move(out[3], h=1, i=1)]
    vel, fin = finish(sc, vel, fin, theirs, rs)
    return vel[:, None], fin


def solution(mesh):
    in_specs = (
        P("slot", "ctx", None),
        P("ctx", None),
        P(),
        P(),
        P(),
        P(None, "slot"),
        P(None, "slot"),
    )
    out_specs = (P(None, "slot", "ctx", None), P("ctx", "slot"))
    return jax.shard_map(shards, mesh=mesh, in_specs=in_specs, out_specs=out_specs, check_vma=False)
```

```python
import math

import jax
import jax.numpy as jnp
from jax import lax
from jax.experimental import pallas as pl
from jax.experimental.pallas import tpu as pltpu
from jax.sharding import PartitionSpec as P

HD = 128
EPS = 1e-06
BF = jnp.bfloat16
F32 = jnp.float32
AXES = ("slot", "ctx")
VM = pl.BlockSpec(memory_space=pltpu.VMEM)
SM = pl.BlockSpec(memory_space=pltpu.SMEM)
SLOTS = 4
PER = 2
TOK = 64
HALF = 32
ROWS = SLOTS * HALF
WIDTH = 3072
COLS = WIDTH // SLOTS
LOG2E = 1.4426950408889634


def where_is(flat):
    s, c = flat // 32, flat % 32
    return dict(h=s // 2, i=s % 2, z=c // 8, xl=(c // 4) % 2, y=c % 4)


def flat_of(d):
    return (d["h"] * 2 + d["i"]) * 32 + d["z"] * 8 + d["xl"] * 4 + d["y"]


def move(x, h=0, i=0, z=0, y=0):
    pairs = []
    for f in range(128):
        d = where_is(f)
        d["h"] = (d["h"] + h) % 2
        d["i"] = (d["i"] + i) % 2
        d["z"] = (d["z"] + z) % 4
        d["y"] = (d["y"] + y) % 4
        pairs.append((f, flat_of(d)))
    return lax.ppermute(x, AXES, pairs)


def group_lists():
    out = []
    for i in range(2):
        for z in range(4):
            for yh in range(2):
                out.append(
                    [
                        flat_of(dict(h=h, i=i, z=z, xl=xl, y=2 * yh + yl))
                        for h in range(2)
                        for xl in range(2)
                        for yl in range(2)
                    ]
                )
    return out


def exchange(x):
    return lax.all_to_all(x, AXES, 0, 0, tiled=True, axis_index_groups=group_lists())


def params(mib, **kw):
    return pltpu.CompilerParams(vmem_limit_bytes=mib * 1024 * 1024, **kw)


def first_slot(sc):
    best, at = sc[0], jnp.int32(0)
    for j in range(1, SLOTS):
        less = sc[j] < best
        best = jnp.where(less, sc[j], best)
        at = jnp.where(less, j, at)
    return at


def rank_of(sc, t, step):
    mine = sc[t]
    rank = jnp.int32(0)
    for j in range(SLOTS):
        rank = rank + (sc[j] < mine).astype(jnp.int32)
    if step == 0:
        return rank
    return jnp.where(rank == 0, SLOTS - 1, rank - 1)


def level_of(sc, t, step):
    rank = rank_of(sc, t, 0)
    level = PER * rank + sc[SLOTS + t] + 1
    if step == 0:
        return level
    return jnp.where(rank == 0, SLOTS * PER, level - 1)


def row_of(half, slot):
    return pl.ds(pl.multiple_of((half * SLOTS + slot) * HALF, HALF), HALF)


def col_of(slot, width=COLS):
    return pl.ds(pl.multiple_of(slot * width, 128), width)


def modulated(values, ada, level):
    center = jnp.mean(values, axis=-1, keepdims=True)
    off = values - center
    spread = jnp.mean(off * off, axis=-1, keepdims=True)
    normed = off * lax.rsqrt(spread + EPS)
    return (normed * (1.0 + ada[level, 1:2, :]) + ada[level, 0:1, :]).astype(BF)


def project(hidden, w, mine, theirs):
    out = jnp.dot(hidden[...], w[...], preferred_element_type=F32).astype(BF)
    cut = out.shape[0] // 2
    for k in range(mine.shape[0]):
        mine[k] = out[:cut, k * HD : (k + 1) * HD]
        theirs[k] = out[cut:, k * HD : (k + 1) * HD]


PAIR = 2 * HALF


def first_body(sc, x0, x1, ada, w, mine, theirs, hidden, *, far):
    s = sc[8]
    i = s % 2
    for r, x in enumerate((x0, x1)):
        t = s ^ (r + far)
        level = level_of(sc, t, 0)
        for a in range(2):
            values = x[a * HALF : (a + 1) * HALF, :].astype(F32)
            to = pl.ds(pl.multiple_of(((i ^ a) * 2 + t % 2) * HALF, HALF), HALF)
            hidden[to, :] = modulated(values, ada, level)
    project(hidden, w, mine, theirs)


def place_heads(h, chip, out, last):
    nothing = jnp.zeros((ROWS, HD), BF)
    last[0] = chip[11]
    last[1] = chip[19]

    @pl.when(h == 0)
    def _():
        for n in range(24):
            out[n // 3, n % 3] = chip[n] if n < 20 else nothing

    @pl.when(h != 0)
    def _():
        for g in range(7):
            out[g, 0] = chip[4 + g]
            out[g, 1] = chip[12 + g]
            out[g, 2] = chip[0] if g == 6 else nothing
        for m in range(3):
            out[7, m] = chip[1 + m]


def second_body(
    sc, x0, x1, x2, x3, here, away, fresh, ada, w, w_pair,
    out, last, vel, fin, theirs, hidden, vall, chip,
):
    s = sc[8]
    i = s % 2
    step_size = 1.0 / (SLOTS * PER)
    half = pl.ds(pl.multiple_of(i * HALF, HALF), HALF)
    for k in range(2):
        vall[:, col_of(s ^ k)] = here[k]
        vall[:, col_of(s ^ (2 + k))] = away[k]
    first = first_slot(sc)
    for r, x in enumerate((x0, x1, x2, x3)):
        t = s ^ r
        level = level_of(sc, t, 1)
        where = row_of(0, t)
        moved = x[half, :].astype(F32) - vall[where, :].astype(F32) * step_size
        taken = jnp.where(t == first, fresh[half, :], moved.astype(BF))
        hidden[where, :] = modulated(taken.astype(F32), ada, level)
    for r, x in enumerate((x0, x1, x2, x3)):

        @pl.when(s ^ r == first)
        def _():
            def done(slot):
                drift = vall[row_of(0, s ^ r), col_of(slot)].astype(F32)
                return (x[half, col_of(slot)].astype(F32) - drift * step_size).astype(BF)

            fin[...] = done(s)
            theirs[:, WIDTH:] = done(s ^ 1)

    vel[...] = vall[row_of(0, s), :]
    theirs[:, :WIDTH] = vall[row_of(0, s ^ 1), :]
    for k, weights in enumerate((w, w_pair)):
        product = jnp.dot(hidden[...], weights[...], preferred_element_type=F32).astype(BF)
        for m in range(10):
            chip[10 * (i ^ k) + m] = product[:, m * HD : (m + 1) * HD]
    place_heads(s // 2, chip, out, last)


def projected_shapes(heads, rows):
    return [jax.ShapeDtypeStruct((heads, rows, HD), BF)] * 2


def packed_shapes():
    return [jax.ShapeDtypeStruct(n + (ROWS, HD), BF) for n in ((8, 3), (2,))]


def first_projection(sc, xs, far, ada, w):
    def body(*refs):
        first_body(*refs, far=far)

    return pl.pallas_call(
        body,
        in_specs=[SM] + [VM] * 4,
        out_specs=[VM] * 2,
        out_shape=projected_shapes(w.shape[1] // HD, PAIR),
        scratch_shapes=[pltpu.VMEM((2 * PAIR, WIDTH), BF)],
        compiler_params=params(12),
        cost_estimate=pl.CostEstimate(flops=4 * 10**9, bytes_accessed=10**7, transcendentals=0),
        name="modulate_project",
    )(sc, *xs, ada, w)


def second_projection(sc, xs, here, away, fresh, ada, w, w_pair):
    return pl.pallas_call(
        second_body,
        in_specs=[SM] + [VM] * 10,
        out_specs=[VM] * 5,
        out_shape=packed_shapes()
        + [jax.ShapeDtypeStruct((HALF, n), BF) for n in (WIDTH, COLS, WIDTH + COLS)],
        scratch_shapes=[pltpu.VMEM((ROWS, WIDTH), BF)] * 2 + [pltpu.VMEM((20, ROWS, HD), BF)],
        compiler_params=params(14),
        cost_estimate=pl.CostEstimate(flops=4 * 10**9, bytes_accessed=10**7, transcendentals=0),
        name="advance_modulate_project",
    )(sc, *xs, here, away, fresh, ada, w, w_pair)


def pack_body(sc, *refs):
    parts, (out, last, chip) = refs[:-3], refs[-3:]
    i, h = sc[8] % 2, sc[8] // 2
    for k in range(2):
        to = pl.ds(10 * jnp.where(k == 0, i, 1 - i), 10)
        for n in range(2):
            at = pl.multiple_of((h ^ n) * PAIR, PAIR)
            chip[to, pl.ds(at, PAIR)] = parts[2 * k + n][...]
    place_heads(h, chip, out, last)


def pack(sc, *parts):
    return pl.pallas_call(
        pack_body,
        in_specs=[SM] + [VM] * len(parts),
        out_specs=[VM, VM],
        out_shape=packed_shapes(),
        scratch_shapes=[pltpu.VMEM((20, ROWS, HD), BF)],
        compiler_params=params(8),
        name="pack_heads",
    )(sc, *parts)


QROWS = 4 * 3 * HALF


def attend_body(step, parts, chunk, block, last, sc, q, *refs):
    blocks, refs = refs[:parts], refs[parts:]
    if last:
        top_in, acc_in, out, qs, ks, vs = refs
    else:
        top_out, acc_out, qs, ks, vs = refs
    keys = ks.shape[0] // SLOTS
    ranks = [rank_of(sc, t, step) for t in range(SLOTS)]
    at = 0
    for ref in blocks:
        for b in range(ref.shape[0]):
            for j in range(SLOTS):
                rows = slice(j * HALF, (j + 1) * HALF)
                to = pl.ds(pl.multiple_of(ranks[j] * keys + at * HALF, HALF), HALF)
                ks[to, :] = ref[b, 0, rows, :]
                vs[to, :HD] = ref[b, 1, rows, :]
            at += 1
    vs[:, HD:] = jnp.ones((SLOTS * keys, HD), BF)
    factor = LOG2E / math.sqrt(HD)
    for c in range(4):
        for m in range(3):
            near = q[c, m].astype(F32)
            other = q[4 + c, m].astype(F32)
            if m == 2:
                near = near + other
            both = (jnp.where(sc[9] == 7, other, near) * factor).astype(BF)
            for j in range(SLOTS):
                to = pl.ds(pl.multiple_of(ranks[j] * QROWS + (c * 3 + m) * HALF, HALF), HALF)
                qs[to, :] = both[j * HALF : (j + 1) * HALF]

    def some_rows(index, _):
        r = pl.multiple_of(index * block, block)
        rows = pl.ds(r, block)

        def scores_of(rank, n, size):
            return lax.dot_general(
                qs[pl.ds(rank * QROWS + r, block), :], ks[n : n + size, :],
                (((1,), (1,)), ((), ())), preferred_element_type=F32,
            )

        todo = []
        for rank in reversed(range(SLOTS)):
            span = (rank + 1) * keys
            todo += [(rank, n, min(chunk, span - n)) for n in range(0, span, chunk)]
        ahead = scores_of(*todo[0])
        for x, (rank, n, size) in enumerate(todo):
            scores = ahead
            if n == 0 and last:
                old, total = top_in[rank, rows], acc_in[rank, rows]
            if x + 1 < len(todo):
                ahead = scores_of(*todo[x + 1])
            new = jnp.max(scores, axis=-1, keepdims=True)
            fresh = n == 0 and not last
            new = jnp.broadcast_to(new, (block, HD)) if fresh else jnp.maximum(old, new)
            weights = jnp.exp2(scores - new[:, :1]).astype(BF)
            part = jnp.dot(weights, vs[n : n + size, :], preferred_element_type=F32)
            if fresh:
                total = part
            else:
                shrink = jnp.exp2(old - new)
                total = total * jnp.concatenate([shrink, shrink], axis=1) + part
            old = new
            if n + size < (rank + 1) * keys:
                continue
            if not last:
                top_out[rank, rows] = new
                acc_out[rank, rows] = total
                continue
            res = (total[:, :HD] / total[:, HD:]).astype(BF)
            slot = jnp.int32(0)
            for j in range(1, SLOTS):
                slot = jnp.where(ranks[j] == rank, j, slot)
            to = pl.ds(pl.multiple_of(slot * HALF, HALF), HALF)
            for k in range(block // HALF):
                head = index * (block // HALF) + k
                out[head, to, :] = res[k * HALF : (k + 1) * HALF]
                out[12 + head, to, :] = res[k * HALF : (k + 1) * HALF]
        return 0

    lax.fori_loop(0, QROWS // block, some_rows, 0)


def attend(step, sc, q, blocks, chunk, block, state=None):
    last = state is not None
    keys = sum(b.shape[0] for b in blocks) * HALF

    def body(*refs):
        attend_body(step, len(blocks), chunk, block, last, *refs)

    scratch = [
        pltpu.VMEM((SLOTS * QROWS, HD), BF),
        pltpu.VMEM((SLOTS * keys, HD), BF),
        pltpu.VMEM((SLOTS * keys, 2 * HD), BF),
    ]
    if last:
        out_shape = jax.ShapeDtypeStruct((24, ROWS, HD), BF)
    else:
        out_shape = [
            jax.ShapeDtypeStruct((SLOTS, QROWS, HD), F32),
            jax.ShapeDtypeStruct((SLOTS, QROWS, 2 * HD), F32),
        ]
    pairs = 10 * QROWS * keys
    return pl.pallas_call(
        body,
        in_specs=[SM] + [VM] * (1 + len(blocks) + (2 if last else 0)),
        out_specs=VM if last else [VM, VM],
        out_shape=out_shape,
        scratch_shapes=scratch,
        compiler_params=params(20 if last else 12),
        cost_estimate=pl.CostEstimate(
            flops=pairs * HD * 8, bytes_accessed=8 * 10**6, transcendentals=pairs
        ),
        name="span_attention_end" if last else "span_attention_begin",
    )(sc, q, *blocks, *(state or ()))


def out_body(step, sc, mine, ada, w, w_pair, out, attn):
    s = sc[8]
    for m in range(24):
        attn[:, m * HD : (m + 1) * HD] = mine[m // 3, m % 3]
    for k, weights in enumerate((w, w_pair)):
        product = jnp.dot(attn[...], weights[...], preferred_element_type=F32)
        for t in range(SLOTS):
            gate = ada[level_of(sc, t, step), 2:3, col_of(s ^ k)]
            piece = (product[t * HALF : (t + 1) * HALF] * gate).astype(BF)
            if step == 0:
                out[k, t * HALF : (t + 1) * HALF, :] = piece
            else:
                out[s ^ t, k] = piece


def out_projection(step, sc, mine, ada, w, w_pair):
    shape = (2, ROWS, COLS) if step == 0 else (SLOTS, 2, HALF, COLS)

    def body(*refs):
        out_body(step, *refs)

    return pl.pallas_call(
        body,
        in_specs=[SM] + [VM] * 4,
        out_specs=VM,
        out_shape=jax.ShapeDtypeStruct(shape, BF),
        scratch_shapes=[pltpu.VMEM((ROWS, WIDTH), BF)],
        compiler_params=params(10),
        cost_estimate=pl.CostEstimate(flops=2 * 10**9, bytes_accessed=6 * 10**6, transcendentals=0),
        name="out_projection",
    )(sc, mine, ada, w, w_pair)


def hold(w):
    def body(x, y, sem):
        copy = pltpu.make_async_copy(x, y, sem)
        copy.start()
        copy.wait()

    return pl.pallas_call(
        body,
        in_specs=[pl.BlockSpec(memory_space=pl.ANY)],
        out_specs=VM,
        out_shape=jax.ShapeDtypeStruct(w.shape, w.dtype),
        scratch_shapes=[pltpu.SemaphoreType.DMA(())],
        compiler_params=params(6),
        name="hold_weights",
    )(w)


def finish_body(sc, vel, fin, theirs, r0, r1, r2, r3, out, done):
    s = sc[8]
    i = s % 2
    halves = [pl.ds(pl.multiple_of((i ^ a) * HALF, HALF), HALF) for a in range(2)]
    out[0, halves[0], :] = vel[...]
    out[0, halves[1], :] = theirs[:, :WIDTH]
    done[halves[0], :] = fin[...]
    done[halves[1], :] = theirs[:, WIDTH:]
    for k, r in enumerate((r0, r1, r2, r3)):
        for c in range(2):
            out[1, halves[k % 2], col_of(s ^ k ^ c)] = r[c]


def finish(sc, vel, fin, theirs, rs):
    return pl.pallas_call(
        finish_body,
        in_specs=[SM] + [VM] * 7,
        out_specs=[VM, VM],
        out_shape=[
            jax.ShapeDtypeStruct((2, TOK, WIDTH), BF),
            jax.ShapeDtypeStruct((TOK, COLS), BF),
        ],
        compiler_params=params(8),
        name="collect_velocity",
    )(sc, vel, fin, theirs, *rs)


def seventh(x):
    out = []
    for xl, yl in ((0, 0), (0, 1), (1, 0)):
        pairs = []
        for f in range(128):
            d = where_is(f)
            if (d["h"], d["xl"], d["y"] % 2) == (1, xl, yl):
                pairs.append((f, flat_of(dict(d, xl=1, y=d["y"] // 2 * 2 + 1))))
        out.append(lax.ppermute(x, AXES, pairs))
    return out


def begin_keys(x, weights):
    y = move(x[:3], y=2)
    zs = [move(x[1:], z=k) for k in (1, -1, 2)]
    _, weights = after(x, weights)
    y, zs, weights = after(y, zs, [hold(w) for w in weights])
    early = jnp.concatenate([x, y, *zs])
    along_z = jnp.concatenate([x[:1], y[:2]])
    along_y = jnp.concatenate([x[3:], *[z[1:] for z in zs]])
    late = [move(along_z, z=k) for k in (1, -1, 2)] + [move(along_y, y=2)]
    return early, late, weights


def both_cores(x):
    return [x, move(x, i=1)]


def after(x, *others):
    return lax.optimization_barrier((x, *others))


def shards(latents, fresh, span_ids, noise_step, ada_table, w_qkv, w_out):
    pos = lax.axis_index("slot").astype(jnp.int32).reshape(1)
    ctx = lax.axis_index("ctx").astype(jnp.int32).reshape(1)
    group = 4 * (pos // 2) + ctx // 4 % 2 * 2 + ctx % 2
    sc = jnp.concatenate([span_ids, noise_step, pos, group])
    own = latents[0]

    def beside(x, *others):
        return after(exchange(x), *others)

    def attention(step, got, last, weights):
        keys = jnp.where(group[0] == 7, jnp.stack(last), got[4:, :2])
        early, late, weights = begin_keys(keys, weights)
        state = attend(step, sc, got, both_cores(early), 1024, 192)
        late, state = after(late, state)
        late = jnp.concatenate(late)
        attn = attend(step, sc, got, both_cores(late), 1024, 192, state)
        return attn.reshape(8, 3, ROWS, HD), weights

    far = move(own, h=1)
    near = move(own, i=1)
    a = first_projection(sc, (own, near), 0, ada_table, w_qkv)
    far, a = after(far, a)
    far_near = move(far, i=1)
    b = first_projection(sc, (far, far_near), 2, ada_table, w_qkv)
    xs = (own, near, far, far_near)

    packed, last = pack(sc, a[0], b[0], move(a[1], i=1), move(b[1], i=1))
    packed, last, w_out_pair = after(packed, last, w_out)
    got, w_out_pair, *others = beside(packed, move(w_out_pair, i=1), *seventh(last))
    attn, held = attention(0, got, [*others, last], [w_out, w_out_pair])
    attn, w_pair = after(attn, w_qkv)
    attn, w_pair = beside(attn, move(w_pair, i=1))
    vel = out_projection(0, sc, attn, ada_table, *held)
    packed, last, vel, fin, theirs = second_projection(
        sc, xs, vel, move(vel, h=1), fresh, ada_table, w_qkv, w_pair
    )
    got, *others = beside(packed, *seventh(last))
    attn, held = attention(1, got, [*others, last], [w_out, w_out_pair])
    attn, theirs = after(exchange(attn), theirs)
    theirs = move(theirs, i=1)
    out = out_projection(1, sc, attn, ada_table, *held)
    rs = [out[0], move(out[1], i=1), move(out[2], h=1), move(out[3], h=1, i=1)]
    vel, fin = finish(sc, vel, fin, theirs, rs)
    return vel[:, None], fin


def solution(mesh):
    in_specs = (
        P("slot", "ctx", None),
        P("ctx", None),
        P(),
        P(),
        P(),
        P(None, "slot"),
        P(None, "slot"),
    )
    out_specs = (P(None, "slot", "ctx", None), P("ctx", "slot"))
    return jax.shard_map(shards, mesh=mesh, in_specs=in_specs, out_specs=out_specs, check_vma=False)
```

```python
import math

import jax
import jax.numpy as jnp
from jax import lax
from jax.experimental import pallas as pl
from jax.experimental.pallas import tpu as pltpu
from jax.sharding import PartitionSpec as P

HD = 128
EPS = 1e-06
BF = jnp.bfloat16
F32 = jnp.float32
AXES = ("slot", "ctx")
VM = pl.BlockSpec(memory_space=pltpu.VMEM)
SM = pl.BlockSpec(memory_space=pltpu.SMEM)
SLOTS = 4
PER = 2
TOK = 64
HALF = 32
ROWS = SLOTS * HALF
WIDTH = 3072
COLS = WIDTH // SLOTS
LOG2E = 1.4426950408889634


def where_is(flat):
    s, c = flat // 32, flat % 32
    return dict(h=s // 2, i=s % 2, z=c // 8, xl=(c // 4) % 2, y=c % 4)


def flat_of(d):
    return (d["h"] * 2 + d["i"]) * 32 + d["z"] * 8 + d["xl"] * 4 + d["y"]


def move(x, h=0, i=0, z=0, y=0):
    pairs = []
    for f in range(128):
        d = where_is(f)
        d["h"] = (d["h"] + h) % 2
        d["i"] = (d["i"] + i) % 2
        d["z"] = (d["z"] + z) % 4
        d["y"] = (d["y"] + y) % 4
        pairs.append((f, flat_of(d)))
    return lax.ppermute(x, AXES, pairs)


def group_lists():
    out = []
    for i in range(2):
        for z in range(4):
            for yh in range(2):
                out.append(
                    [
                        flat_of(dict(h=h, i=i, z=z, xl=xl, y=2 * yh + yl))
                        for h in range(2)
                        for xl in range(2)
                        for yl in range(2)
                    ]
                )
    return out


def exchange(x):
    return lax.all_to_all(x, AXES, 0, 0, tiled=True, axis_index_groups=group_lists())


def params(mib, **kw):
    return pltpu.CompilerParams(vmem_limit_bytes=mib * 1024 * 1024, **kw)


def first_slot(sc):
    best, at = sc[0], jnp.int32(0)
    for j in range(1, SLOTS):
        less = sc[j] < best
        best = jnp.where(less, sc[j], best)
        at = jnp.where(less, j, at)
    return at


def rank_of(sc, t, step):
    mine = sc[t]
    rank = jnp.int32(0)
    for j in range(SLOTS):
        rank = rank + (sc[j] < mine).astype(jnp.int32)
    if step == 0:
        return rank
    return jnp.where(rank == 0, SLOTS - 1, rank - 1)


def level_of(sc, t, step):
    rank = rank_of(sc, t, 0)
    level = PER * rank + sc[SLOTS + t] + 1
    if step == 0:
        return level
    return jnp.where(rank == 0, SLOTS * PER, level - 1)


def row_of(half, slot):
    return pl.ds(pl.multiple_of((half * SLOTS + slot) * HALF, HALF), HALF)


def col_of(slot, width=COLS):
    return pl.ds(pl.multiple_of(slot * width, 128), width)


def modulated(values, ada, level):
    center = jnp.mean(values, axis=-1, keepdims=True)
    off = values - center
    spread = jnp.mean(off * off, axis=-1, keepdims=True)
    normed = off * lax.rsqrt(spread + EPS)
    return (normed * (1.0 + ada[level, 1:2, :]) + ada[level, 0:1, :]).astype(BF)


def project(hidden, w, mine, theirs):
    out = jnp.dot(hidden[...], w[...], preferred_element_type=F32).astype(BF)
    cut = out.shape[0] // 2
    for k in range(mine.shape[0]):
        mine[k] = out[:cut, k * HD : (k + 1) * HD]
        theirs[k] = out[cut:, k * HD : (k + 1) * HD]


PAIR = 2 * HALF


def first_body(sc, x0, x1, ada, w, mine, theirs, hidden, *, far):
    s = sc[8]
    i = s % 2
    for r, x in enumerate((x0, x1)):
        t = s ^ (r + far)
        level = level_of(sc, t, 0)
        for a in range(2):
            values = x[a * HALF : (a + 1) * HALF, :].astype(F32)
            to = pl.ds(pl.multiple_of(((i ^ a) * 2 + t % 2) * HALF, HALF), HALF)
            hidden[to, :] = modulated(values, ada, level)
    project(hidden, w, mine, theirs)


def place_heads(h, chip, out, last):
    nothing = jnp.zeros((ROWS, HD), BF)
    last[0] = chip[11]
    last[1] = chip[19]

    @pl.when(h == 0)
    def _():
        for n in range(24):
            out[n // 3, n % 3] = chip[n] if n < 20 else nothing

    @pl.when(h != 0)
    def _():
        for g in range(7):
            out[g, 0] = chip[4 + g]
            out[g, 1] = chip[12 + g]
            out[g, 2] = chip[0] if g == 6 else nothing
        for m in range(3):
            out[7, m] = chip[1 + m]


def second_body(
    sc, x0, x1, x2, x3, here, away, fresh, ada, w, w_pair,
    out, last, vel, fin, theirs, hidden, vall, chip,
):
    s = sc[8]
    i = s % 2
    step_size = 1.0 / (SLOTS * PER)
    half = pl.ds(pl.multiple_of(i * HALF, HALF), HALF)
    for k in range(2):
        vall[:, col_of(s ^ k)] = here[k]
        vall[:, col_of(s ^ (2 + k))] = away[k]
    first = first_slot(sc)
    for r, x in enumerate((x0, x1, x2, x3)):
        t = s ^ r
        level = level_of(sc, t, 1)
        where = row_of(0, t)
        moved = x[half, :].astype(F32) - vall[where, :].astype(F32) * step_size
        taken = jnp.where(t == first, fresh[half, :], moved.astype(BF))
        hidden[where, :] = modulated(taken.astype(F32), ada, level)
    for r, x in enumerate((x0, x1, x2, x3)):

        @pl.when(s ^ r == first)
        def _():
            def done(slot):
                drift = vall[row_of(0, s ^ r), col_of(slot)].astype(F32)
                return (x[half, col_of(slot)].astype(F32) - drift * step_size).astype(BF)

            fin[...] = done(s)
            theirs[:, WIDTH:] = done(s ^ 1)

    vel[...] = vall[row_of(0, s), :]
    theirs[:, :WIDTH] = vall[row_of(0, s ^ 1), :]
    for k, weights in enumerate((w, w_pair)):
        product = jnp.dot(hidden[...], weights[...], preferred_element_type=F32).astype(BF)
        for m in range(10):
            chip[10 * (i ^ k) + m] = product[:, m * HD : (m + 1) * HD]
    place_heads(s // 2, chip, out, last)


def projected_shapes(heads, rows):
    return [jax.ShapeDtypeStruct((heads, rows, HD), BF)] * 2


def packed_shapes():
    return [jax.ShapeDtypeStruct(n + (ROWS, HD), BF) for n in ((8, 3), (2,))]


def first_projection(sc, xs, far, ada, w):
    def body(*refs):
        first_body(*refs, far=far)

    return pl.pallas_call(
        body,
        in_specs=[SM] + [VM] * 4,
        out_specs=[VM] * 2,
        out_shape=projected_shapes(w.shape[1] // HD, PAIR),
        scratch_shapes=[pltpu.VMEM((2 * PAIR, WIDTH), BF)],
        compiler_params=params(12),
        cost_estimate=pl.CostEstimate(flops=4 * 10**9, bytes_accessed=10**7, transcendentals=0),
        name="modulate_project",
    )(sc, *xs, ada, w)


def second_projection(sc, xs, here, away, fresh, ada, w, w_pair):
    return pl.pallas_call(
        second_body,
        in_specs=[SM] + [VM] * 10,
        out_specs=[VM] * 5,
        out_shape=packed_shapes()
        + [jax.ShapeDtypeStruct((HALF, n), BF) for n in (WIDTH, COLS, WIDTH + COLS)],
        scratch_shapes=[pltpu.VMEM((ROWS, WIDTH), BF)] * 2 + [pltpu.VMEM((20, ROWS, HD), BF)],
        compiler_params=params(14),
        cost_estimate=pl.CostEstimate(flops=4 * 10**9, bytes_accessed=10**7, transcendentals=0),
        name="advance_modulate_project",
    )(sc, *xs, here, away, fresh, ada, w, w_pair)


def pack_body(sc, *refs):
    parts, (out, last, chip) = refs[:-3], refs[-3:]
    i, h = sc[8] % 2, sc[8] // 2
    for k in range(2):
        to = pl.ds(10 * jnp.where(k == 0, i, 1 - i), 10)
        for n in range(2):
            at = pl.multiple_of((h ^ n) * PAIR, PAIR)
            chip[to, pl.ds(at, PAIR)] = parts[2 * k + n][...]
    place_heads(h, chip, out, last)


def pack(sc, *parts):
    return pl.pallas_call(
        pack_body,
        in_specs=[SM] + [VM] * len(parts),
        out_specs=[VM, VM],
        out_shape=packed_shapes(),
        scratch_shapes=[pltpu.VMEM((20, ROWS, HD), BF)],
        compiler_params=params(8),
        name="pack_heads",
    )(sc, *parts)


QROWS = 4 * 3 * HALF


def attend_body(step, parts, chunk, block, last, sc, q, *refs):
    blocks, refs = refs[:parts], refs[parts:]
    if last:
        top_in, acc_in, out, qs, ks, vs = refs
    else:
        top_out, acc_out, qs, ks, vs = refs
    keys = ks.shape[0] // SLOTS
    ranks = [rank_of(sc, t, step) for t in range(SLOTS)]
    at = 0
    for ref in blocks:
        for b in range(ref.shape[0]):
            for j in range(SLOTS):
                rows = slice(j * HALF, (j + 1) * HALF)
                to = pl.ds(pl.multiple_of(ranks[j] * keys + at * HALF, HALF), HALF)
                ks[to, :] = ref[b, 0, rows, :]
                vs[to, :HD] = ref[b, 1, rows, :]
            at += 1
    vs[:, HD:] = jnp.ones((SLOTS * keys, HD), BF)
    factor = LOG2E / math.sqrt(HD)
    for c in range(4):
        for m in range(3):
            near = q[c, m].astype(F32)
            other = q[4 + c, m].astype(F32)
            if m == 2:
                near = near + other
            both = (jnp.where(sc[9] == 7, other, near) * factor).astype(BF)
            for j in range(SLOTS):
                to = pl.ds(pl.multiple_of(ranks[j] * QROWS + (c * 3 + m) * HALF, HALF), HALF)
                qs[to, :] = both[j * HALF : (j + 1) * HALF]

    def some_rows(index, _):
        r = pl.multiple_of(index * block, block)
        rows = pl.ds(r, block)

        def scores_of(rank, n, size):
            return lax.dot_general(
                qs[pl.ds(rank * QROWS + r, block), :], ks[n : n + size, :],
                (((1,), (1,)), ((), ())), preferred_element_type=F32,
            )

        todo = []
        for rank in reversed(range(SLOTS)):
            span = (rank + 1) * keys
            todo += [(rank, n, min(chunk, span - n)) for n in range(0, span, chunk)]
        ahead = scores_of(*todo[0])
        for x, (rank, n, size) in enumerate(todo):
            scores = ahead
            if n == 0 and last:
                old, total = top_in[rank, rows], acc_in[rank, rows]
            if x + 1 < len(todo):
                ahead = scores_of(*todo[x + 1])
            new = jnp.max(scores, axis=-1, keepdims=True)
            fresh = n == 0 and not last
            new = jnp.broadcast_to(new, (block, HD)) if fresh else jnp.maximum(old, new)
            weights = jnp.exp2(scores - new[:, :1]).astype(BF)
            part = jnp.dot(weights, vs[n : n + size, :], preferred_element_type=F32)
            if fresh:
                total = part
            else:
                shrink = jnp.exp2(old - new)
                total = total * jnp.concatenate([shrink, shrink], axis=1) + part
            old = new
            if n + size < (rank + 1) * keys:
                continue
            if not last:
                top_out[rank, rows] = new
                acc_out[rank, rows] = total
                continue
            res = (total[:, :HD] / total[:, HD:]).astype(BF)
            slot = jnp.int32(0)
            for j in range(1, SLOTS):
                slot = jnp.where(ranks[j] == rank, j, slot)
            to = pl.ds(pl.multiple_of(slot * HALF, HALF), HALF)
            for k in range(block // HALF):
                head = index * (block // HALF) + k
                out[head, to, :] = res[k * HALF : (k + 1) * HALF]
                out[12 + head, to, :] = res[k * HALF : (k + 1) * HALF]
        return 0

    lax.fori_loop(0, QROWS // block, some_rows, 0)


def attend(step, sc, q, blocks, chunk, block, state=None):
    last = state is not None
    keys = sum(b.shape[0] for b in blocks) * HALF

    def body(*refs):
        attend_body(step, len(blocks), chunk, block, last, *refs)

    scratch = [
        pltpu.VMEM((SLOTS * QROWS, HD), BF),
        pltpu.VMEM((SLOTS * keys, HD), BF),
        pltpu.VMEM((SLOTS * keys, 2 * HD), BF),
    ]
    if last:
        out_shape = jax.ShapeDtypeStruct((24, ROWS, HD), BF)
    else:
        out_shape = [
            jax.ShapeDtypeStruct((SLOTS, QROWS, HD), F32),
            jax.ShapeDtypeStruct((SLOTS, QROWS, 2 * HD), F32),
        ]
    pairs = 10 * QROWS * keys
    return pl.pallas_call(
        body,
        in_specs=[SM] + [VM] * (1 + len(blocks) + (2 if last else 0)),
        out_specs=VM if last else [VM, VM],
        out_shape=out_shape,
        scratch_shapes=scratch,
        compiler_params=params(20 if last else 18),
        cost_estimate=pl.CostEstimate(
            flops=pairs * HD * 8, bytes_accessed=8 * 10**6, transcendentals=pairs
        ),
        name="span_attention_end" if last else "span_attention_begin",
    )(sc, q, *blocks, *(state or ()))


def out_body(step, sc, mine, ada, w, w_pair, out, attn):
    s = sc[8]
    for m in range(24):
        attn[:, m * HD : (m + 1) * HD] = mine[m // 3, m % 3]
    for k, weights in enumerate((w, w_pair)):
        product = jnp.dot(attn[...], weights[...], preferred_element_type=F32)
        for t in range(SLOTS):
            gate = ada[level_of(sc, t, step), 2:3, col_of(s ^ k)]
            piece = (product[t * HALF : (t + 1) * HALF] * gate).astype(BF)
            if step == 0:
                out[k, t * HALF : (t + 1) * HALF, :] = piece
            else:
                out[s ^ t, k] = piece


def out_projection(step, sc, mine, ada, w, w_pair):
    shape = (2, ROWS, COLS) if step == 0 else (SLOTS, 2, HALF, COLS)

    def body(*refs):
        out_body(step, *refs)

    return pl.pallas_call(
        body,
        in_specs=[SM] + [VM] * 4,
        out_specs=VM,
        out_shape=jax.ShapeDtypeStruct(shape, BF),
        scratch_shapes=[pltpu.VMEM((ROWS, WIDTH), BF)],
        compiler_params=params(10),
        cost_estimate=pl.CostEstimate(flops=2 * 10**9, bytes_accessed=6 * 10**6, transcendentals=0),
        name="out_projection",
    )(sc, mine, ada, w, w_pair)


def hold(w):
    def body(x, y, sem):
        copy = pltpu.make_async_copy(x, y, sem)
        copy.start()
        copy.wait()

    return pl.pallas_call(
        body,
        in_specs=[pl.BlockSpec(memory_space=pl.ANY)],
        out_specs=VM,
        out_shape=jax.ShapeDtypeStruct(w.shape, w.dtype),
        scratch_shapes=[pltpu.SemaphoreType.DMA(())],
        compiler_params=params(6),
        name="hold_weights",
    )(w)


def finish_body(sc, vel, fin, theirs, r0, r1, r2, r3, out, done):
    s = sc[8]
    i = s % 2
    halves = [pl.ds(pl.multiple_of((i ^ a) * HALF, HALF), HALF) for a in range(2)]
    out[0, halves[0], :] = vel[...]
    out[0, halves[1], :] = theirs[:, :WIDTH]
    done[halves[0], :] = fin[...]
    done[halves[1], :] = theirs[:, WIDTH:]
    for k, r in enumerate((r0, r1, r2, r3)):
        for c in range(2):
            out[1, halves[k % 2], col_of(s ^ k ^ c)] = r[c]


def finish(sc, vel, fin, theirs, rs):
    return pl.pallas_call(
        finish_body,
        in_specs=[SM] + [VM] * 7,
        out_specs=[VM, VM],
        out_shape=[
            jax.ShapeDtypeStruct((2, TOK, WIDTH), BF),
            jax.ShapeDtypeStruct((TOK, COLS), BF),
        ],
        compiler_params=params(8),
        name="collect_velocity",
    )(sc, vel, fin, theirs, *rs)


def seventh(x):
    out = []
    for xl, yl in ((0, 0), (0, 1), (1, 0)):
        pairs = []
        for f in range(128):
            d = where_is(f)
            if (d["h"], d["xl"], d["y"] % 2) == (1, xl, yl):
                pairs.append((f, flat_of(dict(d, xl=1, y=d["y"] // 2 * 2 + 1))))
        out.append(lax.ppermute(x, AXES, pairs))
    return out


def begin_keys(x, weights):
    y = move(x[:3], y=2)
    zs = [move(x[1:], z=k) for k in (1, -1, 2)]
    _, weights = after(x, weights)
    y, zs, weights = after(y, zs, [hold(w) for w in weights])
    early = jnp.concatenate([x, y, *zs])
    along_z = jnp.concatenate([x[:1], y[:2]])
    along_y = jnp.concatenate([x[3:], *[z[1:] for z in zs]])
    late = [move(along_z, z=k) for k in (1, -1, 2)] + [move(along_y, y=2)]
    return early, late, weights


def both_cores(x):
    return [x, move(x, i=1)]


def after(x, *others):
    return lax.optimization_barrier((x, *others))


def shards(latents, fresh, span_ids, noise_step, ada_table, w_qkv, w_out):
    pos = lax.axis_index("slot").astype(jnp.int32).reshape(1)
    ctx = lax.axis_index("ctx").astype(jnp.int32).reshape(1)
    group = 4 * (pos // 2) + ctx // 4 % 2 * 2 + ctx % 2
    sc = jnp.concatenate([span_ids, noise_step, pos, group])
    own = latents[0]

    def beside(x, *others):
        return after(exchange(x), *others)

    def attention(step, got, last, weights):
        keys = jnp.where(group[0] == 7, jnp.stack(last), got[4:, :2])
        early, late, weights = begin_keys(keys, weights)
        state = attend(step, sc, got, both_cores(early), 4096, 192)
        late, state = after(late, state)
        late = jnp.concatenate(late)
        attn = attend(step, sc, got, both_cores(late), 4096, 192, state)
        return attn.reshape(8, 3, ROWS, HD), weights

    far = move(own, h=1)
    near = move(own, i=1)
    a = first_projection(sc, (own, near), 0, ada_table, w_qkv)
    far, a = after(far, a)
    far_near = move(far, i=1)
    b = first_projection(sc, (far, far_near), 2, ada_table, w_qkv)
    xs = (own, near, far, far_near)

    packed, last = pack(sc, a[0], b[0], move(a[1], i=1), move(b[1], i=1))
    packed, last, w_out_pair = after(packed, last, w_out)
    got, w_out_pair, *others = beside(packed, move(w_out_pair, i=1), *seventh(last))
    attn, held = attention(0, got, [*others, last], [w_out, w_out_pair])
    attn, w_pair = after(attn, w_qkv)
    attn, w_pair = beside(attn, move(w_pair, i=1))
    vel = out_projection(0, sc, attn, ada_table, *held)
    packed, last, vel, fin, theirs = second_projection(
        sc, xs, vel, move(vel, h=1), fresh, ada_table, w_qkv, w_pair
    )
    got, *others = beside(packed, *seventh(last))
    attn, held = attention(1, got, [*others, last], [w_out, w_out_pair])
    attn, theirs = after(exchange(attn), theirs)
    theirs = move(theirs, i=1)
    out = out_projection(1, sc, attn, ada_table, *held)
    rs = [out[0], move(out[1], i=1), move(out[2], h=1), move(out[3], h=1, i=1)]
    vel, fin = finish(sc, vel, fin, theirs, rs)
    return vel[:, None], fin


def solution(mesh):
    in_specs = (
        P("slot", "ctx", None),
        P("ctx", None),
        P(),
        P(),
        P(),
        P(None, "slot"),
        P(None, "slot"),
    )
    out_specs = (P(None, "slot", "ctx", None), P("ctx", "slot"))
    return jax.shard_map(shards, mesh=mesh, in_specs=in_specs, out_specs=out_specs, check_vma=False)
```

```python
import math

import jax
import jax.numpy as jnp
from jax import lax
from jax.experimental import pallas as pl
from jax.experimental.pallas import tpu as pltpu
from jax.sharding import PartitionSpec as P

HD = 128
EPS = 1e-06
BF = jnp.bfloat16
F32 = jnp.float32
AXES = ("slot", "ctx")
VM = pl.BlockSpec(memory_space=pltpu.VMEM)
SM = pl.BlockSpec(memory_space=pltpu.SMEM)
SLOTS = 4
PER = 2
TOK = 64
HALF = 32
ROWS = SLOTS * HALF
WIDTH = 3072
COLS = WIDTH // SLOTS
LOG2E = 1.4426950408889634


def where_is(flat):
    s, c = flat // 32, flat % 32
    return dict(h=s // 2, i=s % 2, z=c // 8, xl=(c // 4) % 2, y=c % 4)


def flat_of(d):
    return (d["h"] * 2 + d["i"]) * 32 + d["z"] * 8 + d["xl"] * 4 + d["y"]


def move(x, h=0, i=0, z=0, y=0):
    pairs = []
    for f in range(128):
        d = where_is(f)
        d["h"] = (d["h"] + h) % 2
        d["i"] = (d["i"] + i) % 2
        d["z"] = (d["z"] + z) % 4
        d["y"] = (d["y"] + y) % 4
        pairs.append((f, flat_of(d)))
    return lax.ppermute(x, AXES, pairs)


def group_lists():
    out = []
    for i in range(2):
        for z in range(4):
            for yh in range(2):
                out.append(
                    [
                        flat_of(dict(h=h, i=i, z=z, xl=xl, y=2 * yh + yl))
                        for h in range(2)
                        for xl in range(2)
                        for yl in range(2)
                    ]
                )
    return out


def exchange(x):
    return lax.all_to_all(x, AXES, 0, 0, tiled=True, axis_index_groups=group_lists())


def params(mib, **kw):
    return pltpu.CompilerParams(vmem_limit_bytes=mib * 1024 * 1024, **kw)


def first_slot(sc):
    best, at = sc[0], jnp.int32(0)
    for j in range(1, SLOTS):
        less = sc[j] < best
        best = jnp.where(less, sc[j], best)
        at = jnp.where(less, j, at)
    return at


def rank_of(sc, t, step):
    mine = sc[t]
    rank = jnp.int32(0)
    for j in range(SLOTS):
        rank = rank + (sc[j] < mine).astype(jnp.int32)
    if step == 0:
        return rank
    return jnp.where(rank == 0, SLOTS - 1, rank - 1)


def level_of(sc, t, step):
    rank = rank_of(sc, t, 0)
    level = PER * rank + sc[SLOTS + t] + 1
    if step == 0:
        return level
    return jnp.where(rank == 0, SLOTS * PER, level - 1)


def row_of(half, slot):
    return pl.ds(pl.multiple_of((half * SLOTS + slot) * HALF, HALF), HALF)


def col_of(slot, width=COLS):
    return pl.ds(pl.multiple_of(slot * width, 128), width)


def modulated(values, ada, level):
    center = jnp.mean(values, axis=-1, keepdims=True)
    off = values - center
    spread = jnp.mean(off * off, axis=-1, keepdims=True)
    normed = off * lax.rsqrt(spread + EPS)
    return (normed * (1.0 + ada[level, 1:2, :]) + ada[level, 0:1, :]).astype(BF)


def project(hidden, w, mine, theirs):
    out = jnp.dot(hidden[...], w[...], preferred_element_type=F32).astype(BF)
    cut = out.shape[0] // 2
    for k in range(mine.shape[0]):
        mine[k] = out[:cut, k * HD : (k + 1) * HD]
        theirs[k] = out[cut:, k * HD : (k + 1) * HD]


PAIR = 2 * HALF


def first_body(sc, x0, x1, ada, w, mine, theirs, hidden, *, far):
    s = sc[8]
    i = s % 2
    for r, x in enumerate((x0, x1)):
        t = s ^ (r + far)
        level = level_of(sc, t, 0)
        for a in range(2):
            values = x[a * HALF : (a + 1) * HALF, :].astype(F32)
            to = pl.ds(pl.multiple_of(((i ^ a) * 2 + t % 2) * HALF, HALF), HALF)
            hidden[to, :] = modulated(values, ada, level)
    project(hidden, w, mine, theirs)


def place_heads(h, chip, out, last):
    nothing = jnp.zeros((ROWS, HD), BF)
    last[0] = chip[11]
    last[1] = chip[19]

    @pl.when(h == 0)
    def _():
        for n in range(24):
            out[n // 3, n % 3] = chip[n] if n < 20 else nothing

    @pl.when(h != 0)
    def _():
        for g in range(7):
            out[g, 0] = chip[4 + g]
            out[g, 1] = chip[12 + g]
            out[g, 2] = chip[0] if g == 6 else nothing
        for m in range(3):
            out[7, m] = chip[1 + m]


def second_body(
    sc, x0, x1, x2, x3, here, away, fresh, ada, w, w_pair,
    out, last, vel, fin, theirs, hidden, vall, chip,
):
    s = sc[8]
    i = s % 2
    step_size = 1.0 / (SLOTS * PER)
    half = pl.ds(pl.multiple_of(i * HALF, HALF), HALF)
    for k in range(2):
        vall[:, col_of(s ^ k)] = here[k]
        vall[:, col_of(s ^ (2 + k))] = away[k]
    first = first_slot(sc)
    for r, x in enumerate((x0, x1, x2, x3)):
        t = s ^ r
        level = level_of(sc, t, 1)
        where = row_of(0, t)
        moved = x[half, :].astype(F32) - vall[where, :].astype(F32) * step_size
        taken = jnp.where(t == first, fresh[half, :], moved.astype(BF))
        hidden[where, :] = modulated(taken.astype(F32), ada, level)
    for r, x in enumerate((x0, x1, x2, x3)):

        @pl.when(s ^ r == first)
        def _():
            def done(slot):
                drift = vall[row_of(0, s ^ r), col_of(slot)].astype(F32)
                return (x[half, col_of(slot)].astype(F32) - drift * step_size).astype(BF)

            fin[...] = done(s)
            theirs[:, WIDTH:] = done(s ^ 1)

    vel[...] = vall[row_of(0, s), :]
    theirs[:, :WIDTH] = vall[row_of(0, s ^ 1), :]
    for k, weights in enumerate((w, w_pair)):
        product = jnp.dot(hidden[...], weights[...], preferred_element_type=F32).astype(BF)
        for m in range(10):
            chip[10 * (i ^ k) + m] = product[:, m * HD : (m + 1) * HD]
    place_heads(s // 2, chip, out, last)


def projected_shapes(heads, rows):
    return [jax.ShapeDtypeStruct((heads, rows, HD), BF)] * 2


def packed_shapes():
    return [jax.ShapeDtypeStruct(n + (ROWS, HD), BF) for n in ((8, 3), (2,))]


def first_projection(sc, xs, far, ada, w):
    def body(*refs):
        first_body(*refs, far=far)

    return pl.pallas_call(
        body,
        in_specs=[SM] + [VM] * 4,
        out_specs=[VM] * 2,
        out_shape=projected_shapes(w.shape[1] // HD, PAIR),
        scratch_shapes=[pltpu.VMEM((2 * PAIR, WIDTH), BF)],
        compiler_params=params(12),
        cost_estimate=pl.CostEstimate(flops=4 * 10**9, bytes_accessed=10**7, transcendentals=0),
        name="modulate_project",
    )(sc, *xs, ada, w)


def second_projection(sc, xs, here, away, fresh, ada, w, w_pair):
    return pl.pallas_call(
        second_body,
        in_specs=[SM] + [VM] * 10,
        out_specs=[VM] * 5,
        out_shape=packed_shapes()
        + [jax.ShapeDtypeStruct((HALF, n), BF) for n in (WIDTH, COLS, WIDTH + COLS)],
        scratch_shapes=[pltpu.VMEM((ROWS, WIDTH), BF)] * 2 + [pltpu.VMEM((20, ROWS, HD), BF)],
        compiler_params=params(14),
        cost_estimate=pl.CostEstimate(flops=4 * 10**9, bytes_accessed=10**7, transcendentals=0),
        name="advance_modulate_project",
    )(sc, *xs, here, away, fresh, ada, w, w_pair)


def pack_body(sc, *refs):
    parts, (out, last, chip) = refs[:-3], refs[-3:]
    i, h = sc[8] % 2, sc[8] // 2
    for k in range(2):
        to = pl.ds(10 * jnp.where(k == 0, i, 1 - i), 10)
        for n in range(2):
            at = pl.multiple_of((h ^ n) * PAIR, PAIR)
            chip[to, pl.ds(at, PAIR)] = parts[2 * k + n][...]
    place_heads(h, chip, out, last)


def pack(sc, *parts):
    return pl.pallas_call(
        pack_body,
        in_specs=[SM] + [VM] * len(parts),
        out_specs=[VM, VM],
        out_shape=packed_shapes(),
        scratch_shapes=[pltpu.VMEM((20, ROWS, HD), BF)],
        compiler_params=params(8),
        name="pack_heads",
    )(sc, *parts)


QROWS = 4 * 3 * HALF


def attend_body(step, parts, chunk, block, last, sc, *refs):
    if not last:
        q, refs = refs[0], refs[1:]
    blocks, refs = refs[:parts], refs[parts:]
    if last:
        top_in, acc_in, qs, out, ks, vs = refs
    else:
        top_out, acc_out, qs, ks, vs = refs
    keys = ks.shape[0] // SLOTS
    ranks = [rank_of(sc, t, step) for t in range(SLOTS)]
    at = 0
    for ref in blocks:
        for b in range(ref.shape[0]):
            for j in range(SLOTS):
                rows = slice(j * HALF, (j + 1) * HALF)
                to = pl.ds(pl.multiple_of(ranks[j] * keys + at * HALF, HALF), HALF)
                ks[to, :] = ref[b, 0, rows, :]
                vs[to, :HD] = ref[b, 1, rows, :]
            at += 1
    vs[:, HD:] = jnp.ones((SLOTS * keys, HD), BF)
    if not last:
        factor = LOG2E / math.sqrt(HD)
        for c in range(4):
            for m in range(3):
                near = q[c, m].astype(F32)
                other = q[4 + c, m].astype(F32)
                if m == 2:
                    near = near + other
                both = (jnp.where(sc[9] == 7, other, near) * factor).astype(BF)
                for j in range(SLOTS):
                    to = pl.ds(pl.multiple_of(ranks[j] * QROWS + (c * 3 + m) * HALF, HALF), HALF)
                    qs[to, :] = both[j * HALF : (j + 1) * HALF]

    def some_rows(index, _):
        r = pl.multiple_of(index * block, block)
        rows = pl.ds(r, block)

        def scores_of(rank, n, size):
            return lax.dot_general(
                qs[pl.ds(rank * QROWS + r, block), :], ks[n : n + size, :],
                (((1,), (1,)), ((), ())), preferred_element_type=F32,
            )

        todo = []
        for rank in reversed(range(SLOTS)):
            span = (rank + 1) * keys
            todo += [(rank, n, min(chunk, span - n)) for n in range(0, span, chunk)]
        ahead = scores_of(*todo[0])
        for x, (rank, n, size) in enumerate(todo):
            scores = ahead
            if n == 0 and last:
                old, total = top_in[rank, rows], acc_in[rank, rows]
            if x + 1 < len(todo):
                ahead = scores_of(*todo[x + 1])
            new = jnp.max(scores, axis=-1, keepdims=True)
            fresh = n == 0 and not last
            new = jnp.broadcast_to(new, (block, HD)) if fresh else jnp.maximum(old, new)
            weights = jnp.exp2(scores - new[:, :1]).astype(BF)
            part = jnp.dot(weights, vs[n : n + size, :], preferred_element_type=F32)
            if fresh:
                total = part
            else:
                shrink = jnp.exp2(old - new)
                total = total * jnp.concatenate([shrink, shrink], axis=1) + part
            old = new
            if n + size < (rank + 1) * keys:
                continue
            if not last:
                top_out[rank, rows] = new
                acc_out[rank, rows] = total
                continue
            res = (total[:, :HD] / total[:, HD:]).astype(BF)
            slot = jnp.int32(0)
            for j in range(1, SLOTS):
                slot = jnp.where(ranks[j] == rank, j, slot)
            to = pl.ds(pl.multiple_of(slot * HALF, HALF), HALF)
            for k in range(block // HALF):
                head = index * (block // HALF) + k
                out[head, to, :] = res[k * HALF : (k + 1) * HALF]
                out[12 + head, to, :] = res[k * HALF : (k + 1) * HALF]
        return 0

    lax.fori_loop(0, QROWS // block, some_rows, 0)


def attend(step, sc, q, blocks, chunk, block, state=None):
    last = state is not None
    keys = sum(b.shape[0] for b in blocks) * HALF

    def body(*refs):
        attend_body(step, len(blocks), chunk, block, last, *refs)

    scratch = [
        pltpu.VMEM((SLOTS * keys, HD), BF),
        pltpu.VMEM((SLOTS * keys, 2 * HD), BF),
    ]
    if last:
        out_shape = jax.ShapeDtypeStruct((24, ROWS, HD), BF)
    else:
        out_shape = [
            jax.ShapeDtypeStruct((SLOTS, QROWS, HD), F32),
            jax.ShapeDtypeStruct((SLOTS, QROWS, 2 * HD), F32),
            jax.ShapeDtypeStruct((SLOTS * QROWS, HD), BF),
        ]
    pairs = 10 * QROWS * keys
    return pl.pallas_call(
        body,
        in_specs=[SM] + [VM] * (len(blocks) + (3 if last else 1)),
        out_specs=VM if last else [VM] * 3,
        out_shape=out_shape,
        scratch_shapes=scratch,
        compiler_params=params(20 if last else 18),
        cost_estimate=pl.CostEstimate(
            flops=pairs * HD * 8, bytes_accessed=8 * 10**6, transcendentals=pairs
        ),
        name="span_attention_end" if last else "span_attention_begin",
    )(sc, *(() if last else (q,)), *blocks, *(state or ()))


def out_body(step, sc, mine, ada, w, w_pair, out, attn):
    s = sc[8]
    for m in range(24):
        attn[:, m * HD : (m + 1) * HD] = mine[m // 3, m % 3]
    for k, weights in enumerate((w, w_pair)):
        product = jnp.dot(attn[...], weights[...], preferred_element_type=F32)
        for t in range(SLOTS):
            gate = ada[level_of(sc, t, step), 2:3, col_of(s ^ k)]
            piece = (product[t * HALF : (t + 1) * HALF] * gate).astype(BF)
            if step == 0:
                out[k, t * HALF : (t + 1) * HALF, :] = piece
            else:
                out[s ^ t, k] = piece


def out_projection(step, sc, mine, ada, w, w_pair):
    shape = (2, ROWS, COLS) if step == 0 else (SLOTS, 2, HALF, COLS)

    def body(*refs):
        out_body(step, *refs)

    return pl.pallas_call(
        body,
        in_specs=[SM] + [VM] * 4,
        out_specs=VM,
        out_shape=jax.ShapeDtypeStruct(shape, BF),
        scratch_shapes=[pltpu.VMEM((ROWS, WIDTH), BF)],
        compiler_params=params(10),
        cost_estimate=pl.CostEstimate(flops=2 * 10**9, bytes_accessed=6 * 10**6, transcendentals=0),
        name="out_projection",
    )(sc, mine, ada, w, w_pair)


def hold(w):
    def body(x, y, sem):
        copy = pltpu.make_async_copy(x, y, sem)
        copy.start()
        copy.wait()

    return pl.pallas_call(
        body,
        in_specs=[pl.BlockSpec(memory_space=pl.ANY)],
        out_specs=VM,
        out_shape=jax.ShapeDtypeStruct(w.shape, w.dtype),
        scratch_shapes=[pltpu.SemaphoreType.DMA(())],
        compiler_params=params(6),
        name="hold_weights",
    )(w)


def finish_body(sc, vel, fin, theirs, r0, r1, r2, r3, out, done):
    s = sc[8]
    i = s % 2
    halves = [pl.ds(pl.multiple_of((i ^ a) * HALF, HALF), HALF) for a in range(2)]
    out[0, halves[0], :] = vel[...]
    out[0, halves[1], :] = theirs[:, :WIDTH]
    done[halves[0], :] = fin[...]
    done[halves[1], :] = theirs[:, WIDTH:]
    for k, r in enumerate((r0, r1, r2, r3)):
        for c in range(2):
            out[1, halves[k % 2], col_of(s ^ k ^ c)] = r[c]


def finish(sc, vel, fin, theirs, rs):
    return pl.pallas_call(
        finish_body,
        in_specs=[SM] + [VM] * 7,
        out_specs=[VM, VM],
        out_shape=[
            jax.ShapeDtypeStruct((2, TOK, WIDTH), BF),
            jax.ShapeDtypeStruct((TOK, COLS), BF),
        ],
        compiler_params=params(8),
        name="collect_velocity",
    )(sc, vel, fin, theirs, *rs)


def seventh(x):
    out = []
    for xl, yl in ((0, 0), (0, 1), (1, 0)):
        pairs = []
        for f in range(128):
            d = where_is(f)
            if (d["h"], d["xl"], d["y"] % 2) == (1, xl, yl):
                pairs.append((f, flat_of(dict(d, xl=1, y=d["y"] // 2 * 2 + 1))))
        out.append(lax.ppermute(x, AXES, pairs))
    return out


def begin_keys(x, weights):
    y = move(x[:3], y=2)
    zs = [move(x[1:], z=k) for k in (1, -1, 2)]
    _, weights = after(x, weights)
    y, zs, weights = after(y, zs, [hold(w) for w in weights])
    early = jnp.concatenate([x, y, *zs])
    along_z = jnp.concatenate([x[:1], y[:2]])
    along_y = jnp.concatenate([x[3:], *[z[1:] for z in zs]])
    late = [move(along_z, z=k) for k in (1, -1, 2)] + [move(along_y, y=2)]
    return early, late, weights


def both_cores(x):
    return [x, move(x, i=1)]


def after(x, *others):
    return lax.optimization_barrier((x, *others))


def shards(latents, fresh, span_ids, noise_step, ada_table, w_qkv, w_out):
    pos = lax.axis_index("slot").astype(jnp.int32).reshape(1)
    ctx = lax.axis_index("ctx").astype(jnp.int32).reshape(1)
    group = 4 * (pos // 2) + ctx // 4 % 2 * 2 + ctx % 2
    sc = jnp.concatenate([span_ids, noise_step, pos, group])
    own = latents[0]

    def beside(x, *others):
        return after(exchange(x), *others)

    def attention(step, got, last, weights):
        keys = jnp.where(group[0] == 7, jnp.stack(last), got[4:, :2])
        early, late, weights = begin_keys(keys, weights)
        state = attend(step, sc, got, both_cores(early), 4096, 192)
        late, state = after(late, state)
        late = jnp.concatenate(late)
        attn = attend(step, sc, got, both_cores(late), 4096, 192, state)
        return attn.reshape(8, 3, ROWS, HD), weights

    far = move(own, h=1)
    near = move(own, i=1)
    a = first_projection(sc, (own, near), 0, ada_table, w_qkv)
    far, a = after(far, a)
    far_near = move(far, i=1)
    b = first_projection(sc, (far, far_near), 2, ada_table, w_qkv)
    xs = (own, near, far, far_near)

    packed, last = pack(sc, a[0], b[0], move(a[1], i=1), move(b[1], i=1))
    packed, last, w_out_pair = after(packed, last, w_out)
    got, w_out_pair, *others = beside(packed, move(w_out_pair, i=1), *seventh(last))
    attn, held = attention(0, got, [*others, last], [w_out, w_out_pair])
    attn, w_pair = after(attn, w_qkv)
    attn, w_pair = beside(attn, move(w_pair, i=1))
    vel = out_projection(0, sc, attn, ada_table, *held)
    packed, last, vel, fin, theirs = second_projection(
        sc, xs, vel, move(vel, h=1), fresh, ada_table, w_qkv, w_pair
    )
    got, *others = beside(packed, *seventh(last))
    attn, held = attention(1, got, [*others, last], [w_out, w_out_pair])
    attn, theirs = after(exchange(attn), theirs)
    theirs = move(theirs, i=1)
    out = out_projection(1, sc, attn, ada_table, *held)
    rs = [out[0], move(out[1], i=1), move(out[2], h=1), move(out[3], h=1, i=1)]
    vel, fin = finish(sc, vel, fin, theirs, rs)
    return vel[:, None], fin


def solution(mesh):
    in_specs = (
        P("slot", "ctx", None),
        P("ctx", None),
        P(),
        P(),
        P(),
        P(None, "slot"),
        P(None, "slot"),
    )
    out_specs = (P(None, "slot", "ctx", None), P("ctx", "slot"))
    return jax.shard_map(shards, mesh=mesh, in_specs=in_specs, out_specs=out_specs, check_vma=False)
```
